32 devices in a mesh: dp: 8 (over z, x), tensor: 4 (over y, core).
Axes of the slice: x: 2, y: 2, z: 4, core: 2. Of those that a mesh axis runs over, the one named last changes fastest.
Arguments:
- hidden_in: bfloat16 [4096, 1024], P('dp'), may hold values from -6 to 6
- logits_in: bfloat16 [8, 16, 512, 512], P('dp', 'tensor'), may hold values from -5 to 5
- cotangent: bfloat16 [4096, 1024], P(('dp', 'tensor')), may hold values from -6 to 6
- bucket_ids: int32 [8], P('dp'), may hold values from 0 to 2, as said below
- seq_counts: int32 [8], P('dp'), may hold values from 1 to 4, as said below
- key_mask: int32 [4096], P('dp'), may hold values from 0 to 1, as said below
- w_qkv: float32 [2, 3, 1024, 1024], P(None, None, 'dp', 'tensor'), may hold values from -0.1875 to 0.1875
- w_out: float32 [2, 1024, 1024], P(None, 'tensor', 'dp'), may hold values from -1 to 1
- w_in: float32 [2, 1024, 4096], P(None, 'dp', 'tensor'), may hold values from -0.1875 to 0.1875
- w_back: float32 [2, 4096, 1024], P(None, 'tensor', 'dp'), may hold values from -0.09375 to 0.09375
- vectors: float32 [2, 8, 1024], P(None, None, ('dp', 'tensor')), may hold values from -0.4 to 1.4, as said below
- bias_in: float32 [2, 4096], P(None, ('dp', 'tensor')), may hold values from -1 to 1
- m_qkv: float32 [2, 3, 1024, 1024], P(None, None, 'dp', 'tensor'), may hold values from -6 to 6
- m_out: float32 [2, 1024, 1024], P(None, 'tensor', 'dp'), may hold values from -6 to 6
- m_in: float32 [2, 1024, 4096], P(None, 'dp', 'tensor'), may hold values from -6 to 6
- m_back: float32 [2, 4096, 1024], P(None, 'tensor', 'dp'), may hold values from -6 to 6
- m_vectors: float32 [2, 8, 1024], P(None, None, ('dp', 'tensor')), may hold values from -6 to 6
- m_bias: float32 [2, 4096], P(None, ('dp', 'tensor')), may hold values from -6 to 6
- v_qkv: float32 [2, 3, 1024, 1024], P(None, None, 'dp', 'tensor'), may hold values from 0.5 to 50
- v_out: float32 [2, 1024, 1024], P(None, 'tensor', 'dp'), may hold values from 0.5 to 50
- v_in: float32 [2, 1024, 4096], P(None, 'dp', 'tensor'), may hold values from 0.5 to 50
- v_back: float32 [2, 4096, 1024], P(None, 'tensor', 'dp'), may hold values from 0.5 to 50
- v_vectors: float32 [2, 8, 1024], P(None, None, ('dp', 'tensor')), may hold values from 0.5 to 50
- v_bias: float32 [2, 4096], P(None, ('dp', 'tensor')), may hold values from 0.5 to 50
Outputs:
- hidden_out: bfloat16 [4096, 1024], P(('dp', 'tensor'))
- logits_out: bfloat16 [8, 16, 512, 512], P('dp', 'tensor')
- grad_hidden: float32 [4096, 1024], P(('dp', 'tensor'))
- grad_logits: float32 [8, 16, 512, 512], P('dp', 'tensor')
- grad_qkv: float32 [2, 3, 1024, 1024], P(None, None, 'dp', 'tensor')
- grad_wout: float32 [2, 1024, 1024], P(None, 'tensor', 'dp')
- grad_win: float32 [2, 1024, 4096], P(None, 'dp', 'tensor')
- grad_wback: float32 [2, 4096, 1024], P(None, 'tensor', 'dp')
- grad_vectors: float32 [2, 8, 1024], P(None, None, ('dp', 'tensor'))
- grad_bias: float32 [2, 4096], P(None, ('dp', 'tensor'))
- new_qkv: float32 [2, 3, 1024, 1024], P(None, None, 'dp', 'tensor')
- new_wout: float32 [2, 1024, 1024], P(None, 'tensor', 'dp')
- new_win: float32 [2, 1024, 4096], P(None, 'dp', 'tensor')
- new_wback: float32 [2, 4096, 1024], P(None, 'tensor', 'dp')
- new_vectors: float32 [2, 8, 1024], P(None, None, ('dp', 'tensor'))
- new_bias: float32 [2, 4096], P(None, ('dp', 'tensor'))
- first_qkv: float32 [2, 3, 1024, 1024], P(None, None, 'dp', 'tensor')
- first_wout: float32 [2, 1024, 1024], P(None, 'tensor', 'dp')
- first_win: float32 [2, 1024, 4096], P(None, 'dp', 'tensor')
- first_wback: float32 [2, 4096, 1024], P(None, 'tensor', 'dp')
- first_vectors: float32 [2, 8, 1024], P(None, None, ('dp', 'tensor'))
- first_bias: float32 [2, 4096], P(None, ('dp', 'tensor'))
- trust_ratios: float32 [2, 6], replicated
The draws below stay inside these ranges and needn't reach their ends.
Inputs may be any that keep to these rules, and one draw needn't show every extreme that they name: The tokens of dp index d form sequences of 512 / 4 * 2**bucket_ids[d] tokens each, one after another. `seq_counts`: at least half of the sequences of a dp index are in use; the others are empty. `key_mask`: within each sequence the ones form a prefix of more than half of its tokens. `vectors`: rows 0 and 1 of each layer are gains, rows 2 to 7 biases.
All inputs are finite; a program needn't handle non-finite values.
Results may differ from the reference program's by a relative error of at most 0.038.
Values may be sent and summed in bfloat16 or wider, within the bound.
A program may use at most 192 MiB of HBM per device.

```python
import math
import jax
import jax.numpy as jnp
from jax import lax

D = 1024
H = 16
HD = 64
FF = 4096
LAYERS = 2
BLOCK = 512
TOK_DEV = 512
TOKENS = 4096
NB = 8


def bucket_plan(key):
    devices = TOKENS // TOK_DEV
    draw_one, draw_two, draw_three = jax.random.split(key, 3)
    buckets = jax.random.randint(draw_one, (devices,), 0, 3)
    widest = jax.random.randint(draw_two, (), 0, devices)
    narrow = (widest + 1 + jax.random.randint(draw_three, (), 0, devices - 1)) % devices
    places = jnp.arange(devices)
    buckets = jnp.where(places == widest, 0, jnp.where(places == narrow, 2, buckets))
    return (buckets.astype(jnp.int32), widest, narrow)


def draw_bucket_ids(key, part):
    return bucket_plan(key)[0]


def draw_seq_counts(key, part):
    buckets, widest, narrow = bucket_plan(key)
    key = jax.random.fold_in(key, 11)
    devices = TOKENS // TOK_DEV
    slots = 4 * TOK_DEV // BLOCK // jnp.left_shift(1, buckets)
    removed = jax.random.randint(key, (devices,), 0, slots // 2 + 1)
    places = jnp.arange(devices)
    counts = jnp.where(places == widest, slots, jnp.where(places == narrow, slots - slots // 2, slots - removed))
    return counts.astype(jnp.int32)


def draw_key_mask(key, part):
    buckets = bucket_plan(key)[0]
    key = jax.random.fold_in(key, 23)
    devices = TOKENS // TOK_DEV
    most_slots = 4 * TOK_DEV // BLOCK
    span_all = BLOCK // 4 * jnp.left_shift(1, buckets)
    extension = jax.random.randint(key, (devices, most_slots), 0, (span_all - span_all // 2)[:, None])
    lengths = span_all[:, None] // 2 + 1 + extension
    position = jnp.arange(TOKENS)
    device = position // TOK_DEV
    within = position % TOK_DEV
    span_here = span_all[device]
    slot_at = within // span_here
    ones_at = within % span_here < lengths[device, slot_at]
    return ones_at.astype(jnp.int32)


def draw_vectors(key, part):
    key = jax.random.fold_in(key, 37)
    gain_key, shift_key = jax.random.split(key)
    gains = 1.0 + 0.15 * jnp.clip(jax.random.normal(gain_key, (LAYERS, 2, D)), -2.5, 2.5)
    shifts = 0.25 * jnp.clip(jax.random.normal(shift_key, (LAYERS, 6, D)), -1.6, 1.6)
    return jnp.concatenate([gains, shifts], axis=1).astype(jnp.float32)


def draw_cotangent(key, part):
    key = jax.random.fold_in(key, 41)
    base_key, common_key = jax.random.split(key)
    base = jnp.clip(jax.random.normal(base_key, (TOKENS, D)), -3.5, 3.5)
    common = 0.8 * jnp.clip(jax.random.normal(common_key, (TOKENS, 1)), -2.0, 2.0)
    return (base + common).astype(jnp.float32).astype(jnp.bfloat16)


def block_levels(stream_key, extent, cuts, least, largest):
    def one(axis_at, shards_of):
        draws = jax.random.uniform(jax.random.fold_in(jax.random.fold_in(stream_key, 6), axis_at), (shards_of,), jnp.float32, least / len(cuts), largest / len(cuts))
        return jnp.repeat(jnp.exp(draws), extent[axis_at] // shards_of).reshape((-1,) + (1,) * (len(extent) - axis_at - 1))

    level = one(*cuts[0])
    for cut in cuts[1:]:
        level = level * one(*cut)
    return level


def normal_values(own_key, shape, scale, bound, pieces=(), held_as=jnp.bfloat16):
    entries = jax.random.normal(own_key, shape, jnp.float32) * scale
    if len(pieces) > 0:
        entries = block_levels(own_key, shape, pieces, -0.22, 0.18) * entries
    return jnp.clip(entries, min=-bound, max=bound).astype(held_as)


def setup_inputs(seed: int = 0) -> dict:
    streams_of = jax.random.split(jax.random.key(seed), 25)
    return {
        "hidden_in": normal_values(streams_of[0], (TOKENS, D), 1.0, 6.0, ((0, 8),)),
        "logits_in": normal_values(streams_of[1], (NB, H, BLOCK, BLOCK), 1.0, 5.0, ((0, 8), (1, 4))),
        "cotangent": draw_cotangent(jax.random.fold_in(streams_of[24], 71), 0),
        "bucket_ids": draw_bucket_ids(jax.random.fold_in(streams_of[24], 71), 0),
        "seq_counts": draw_seq_counts(jax.random.fold_in(streams_of[24], 71), 0),
        "key_mask": draw_key_mask(jax.random.fold_in(streams_of[24], 71), 0),
        "w_qkv": normal_values(streams_of[6], (LAYERS, 3, D, D), D ** -0.5, 0.1875, ((2, 8), (3, 4)), jnp.float32),
        "w_out": normal_values(streams_of[7], (LAYERS, D, D), (D // 32) ** -0.5, 1.0, ((1, 4), (2, 8)), jnp.float32),
        "w_in": normal_values(streams_of[8], (LAYERS, D, FF), D ** -0.5, 0.1875, ((1, 8), (2, 4)), jnp.float32),
        "w_back": normal_values(streams_of[9], (LAYERS, FF, D), FF ** -0.5, 0.09375, ((1, 4), (2, 8)), jnp.float32),
        "vectors": draw_vectors(jax.random.fold_in(streams_of[24], 71), 0),
        "bias_in": normal_values(streams_of[11], (LAYERS, FF), 0.25, 1.0, ((1, 32),), jnp.float32),
        "m_qkv": normal_values(streams_of[12], (LAYERS, 3, D, D), 1.0, 6.0, ((2, 8), (3, 4)), jnp.float32),
        "m_out": normal_values(streams_of[13], (LAYERS, D, D), 1.0, 6.0, ((1, 4), (2, 8)), jnp.float32),
        "m_in": normal_values(streams_of[14], (LAYERS, D, FF), 1.0, 6.0, ((1, 8), (2, 4)), jnp.float32),
        "m_back": normal_values(streams_of[15], (LAYERS, FF, D), 1.0, 6.0, ((1, 4), (2, 8)), jnp.float32),
        "m_vectors": normal_values(streams_of[16], (LAYERS, 8, D), 1.0, 6.0, ((2, 32),), jnp.float32),
        "m_bias": normal_values(streams_of[17], (LAYERS, FF), 1.0, 6.0, ((1, 32),), jnp.float32),
        "v_qkv": jnp.clip(jnp.exp(math.log(50.0) - 4.6051702 * jax.random.uniform(streams_of[18], (LAYERS, 3, D, D), jnp.float32) ** block_levels(streams_of[18], (LAYERS, 3, D, D), ((2, 8), (3, 4)), -0.2, 0.2)), 0.5, 50.0),
        "v_out": jnp.clip(jnp.exp(math.log(50.0) - 4.6051702 * jax.random.uniform(streams_of[19], (LAYERS, D, D), jnp.float32) ** block_levels(streams_of[19], (LAYERS, D, D), ((1, 4), (2, 8)), -0.2, 0.2)), 0.5, 50.0),
        "v_in": jnp.clip(jnp.exp(math.log(50.0) - 4.6051702 * jax.random.uniform(streams_of[20], (LAYERS, D, FF), jnp.float32) ** block_levels(streams_of[20], (LAYERS, D, FF), ((1, 8), (2, 4)), -0.2, 0.2)), 0.5, 50.0),
        "v_back": jnp.clip(jnp.exp(math.log(50.0) - 4.6051702 * jax.random.uniform(streams_of[21], (LAYERS, FF, D), jnp.float32) ** block_levels(streams_of[21], (LAYERS, FF, D), ((1, 4), (2, 8)), -0.2, 0.2)), 0.5, 50.0),
        "v_vectors": jnp.clip(jnp.exp(math.log(50.0) - 4.6051702 * jax.random.uniform(streams_of[22], (LAYERS, 8, D), jnp.float32) ** block_levels(streams_of[22], (LAYERS, 8, D), ((2, 32),), -0.2, 0.2)), 0.5, 50.0),
        "v_bias": jnp.clip(jnp.exp(math.log(50.0) - 4.6051702 * jax.random.uniform(streams_of[23], (LAYERS, FF), jnp.float32) ** block_levels(streams_of[23], (LAYERS, FF), ((1, 32),), -0.2, 0.2)), 0.5, 50.0),
    }


@jax.custom_vjp
def low(v):
    return lax.optimization_barrier(v.astype(jnp.bfloat16)).astype(jnp.float32)

@jax.custom_vjp
def low_back(v):
    return v

def low_keep(v):
    return (low(v), None)

def low_pass(kept, grad):
    return (grad,)

def back_keep(v):
    return (v, None)

def back_low(kept, grad):
    return (low(grad),)
low.defvjp(low_keep, low_pass)
low_back.defvjp(back_keep, back_low)
PRECISE = lax.Precision.HIGHEST
NORM_EPS = 1e-05
ADAM_EPS = 1e-06
BETA_ONE = 0.9
BETA_TWO = 0.999
CORRECT_ONE = 1.0
CORRECT_TWO = 0.632304575228943
LEARN_RATE = 0.3
DECAY_RATE = 0.01
NEG_FILL = -1e+30

def rounded(values):
    return low(low_back(values))

def product(left, right):
    return jnp.dot(left, right, precision=PRECISE, preferred_element_type=jnp.float32)

def layer_norm(values, gain, shift):
    center = values - lax.optimization_barrier(jnp.mean(values, axis=-1, keepdims=True))
    spread = lax.optimization_barrier(jnp.mean(center * center, axis=-1, keepdims=True))
    return center * lax.rsqrt(spread + NORM_EPS) * gain + shift

def gelu_exact(values):
    return jax.nn.gelu(values, approximate=False)

def masked_softmax(scores, allowed):
    row_top = lax.optimization_barrier(jnp.max(jnp.where(allowed, scores, NEG_FILL), axis=-1, keepdims=True))
    unscaled = jnp.exp(jnp.where(allowed, scores - row_top, NEG_FILL))
    row_total = lax.optimization_barrier(jnp.sum(unscaled, axis=-1, keepdims=True))
    row_total = jnp.where(row_total > 0.5, row_total, 1.0)
    return unscaled / row_total

def block_allowed(block_at, bucket_ids, seq_counts, key_mask):
    per_device = TOK_DEV // BLOCK
    device = block_at // per_device
    bucket = bucket_ids[device]
    seq_span = jnp.where(bucket == 0, BLOCK // 4, jnp.where(bucket == 1, BLOCK // 2, BLOCK)).astype(jnp.int32)
    position = (block_at % per_device * BLOCK + jnp.arange(BLOCK, dtype=jnp.int32)).astype(jnp.int32)
    seq_of = position // seq_span
    keys_on = lax.dynamic_slice_in_dim(key_mask, (block_at * BLOCK).astype(jnp.int32), BLOCK)
    live_keys = (keys_on == 1) & (seq_of < seq_counts[device])
    return (seq_of[:, None] == seq_of[None, :]) & live_keys[None, :]

def forward(params, hidden, logits, allowed):
    w_qkv, w_out, w_in, w_back, vectors, bias_in = params
    rows_here = hidden.shape[0]
    for layer_at in range(LAYERS):
        vector = low(vectors[layer_at])
        w_query = low(w_qkv[layer_at, 0])
        w_keys = low(w_qkv[layer_at, 1])
        w_values = low(w_qkv[layer_at, 2])
        query = rounded(product(hidden, w_query) + vector[2]).reshape(rows_here, H, HD)
        keys = rounded(product(hidden, w_keys)).reshape(rows_here, H, HD)
        values = rounded(product(hidden, w_values) + vector[3]).reshape(rows_here, H, HD)
        raw = jnp.einsum('ihe,jhe->hij', query, keys, precision=PRECISE) * HD ** (-0.5)
        scores = low_back(raw + logits)
        stored = low(scores)
        probs = low(masked_softmax(scores, allowed[None]))
        mixed = rounded(jnp.einsum('hij,jhe->ihe', probs, values, precision=PRECISE).reshape(rows_here, D))
        branch = low_back(product(mixed, low(w_out[layer_at])))
        middle = low(layer_norm(branch + vector[4] + hidden, vector[0], vector[5]))
        before = low_back(product(middle, low(w_in[layer_at])) + low(bias_in[layer_at]))
        active = low(gelu_exact(before))
        feed = low_back(product(active, low(w_back[layer_at])))
        hidden = low(layer_norm(feed + vector[6] + middle, vector[1], vector[7]))
        logits = stored
    return (hidden, logits)

def reference(hidden_in, logits_in, cotangent, bucket_ids, seq_counts, key_mask, w_qkv, w_out, w_in, w_back, vectors, bias_in, m_qkv, m_out, m_in, m_back, m_vectors, m_bias, v_qkv, v_out, v_in, v_back, v_vectors, v_bias):
    masters = (w_qkv.astype(jnp.float32), w_out.astype(jnp.float32), w_in.astype(jnp.float32), w_back.astype(jnp.float32), vectors.astype(jnp.float32), bias_in.astype(jnp.float32))

    def one_block(totals, block_at):
        first_row = (block_at * BLOCK).astype(jnp.int32)
        hidden = lax.dynamic_slice_in_dim(hidden_in, first_row, BLOCK, 0).astype(jnp.float32)
        upstream = lax.dynamic_slice_in_dim(cotangent, first_row, BLOCK, 0).astype(jnp.float32)
        logits = lax.dynamic_index_in_dim(logits_in, block_at, 0, keepdims=False).astype(jnp.float32)
        allowed = block_allowed(block_at, bucket_ids, seq_counts, key_mask)

        def run_block(params_here, hidden_here, logits_here):
            return forward(params_here, hidden_here, logits_here, allowed)
        result_pair, pullback = jax.vjp(run_block, masters, hidden, logits)
        grads_here, grad_rows, grad_scores = pullback((upstream, jnp.zeros_like(result_pair[1])))
        totals = jax.tree.map(jnp.add, totals, grads_here)
        return (totals, (result_pair[0].astype(jnp.bfloat16), result_pair[1].astype(jnp.bfloat16), grad_rows, grad_scores))
    zeros_all = jax.tree.map(jnp.zeros_like, masters)
    gradients, stacked = lax.scan(one_block, zeros_all, jnp.arange(NB, dtype=jnp.int32))
    hidden_out = stacked[0].reshape(TOKENS, D)
    logits_out = stacked[1]
    grad_hidden = stacked[2].reshape(TOKENS, D)
    grad_logits = stacked[3]
    firsts = (m_qkv, m_out, m_in, m_back, m_vectors, m_bias)
    seconds = (v_qkv, v_out, v_in, v_back, v_vectors, v_bias)
    decays = (DECAY_RATE, DECAY_RATE, DECAY_RATE, DECAY_RATE, 0.0, 0.0)
    new_params = []
    new_firsts = []
    trust_rows = []
    for master, gradient, first_prev, second_prev, decay_rate in zip(masters, gradients, firsts, seconds, decays):
        moment_one = BETA_ONE * first_prev + (1.0 - BETA_ONE) * gradient
        moment_two = BETA_TWO * second_prev + (1.0 - BETA_TWO) * gradient * gradient
        update = moment_one / CORRECT_ONE / (jnp.sqrt(moment_two / CORRECT_TWO) + ADAM_EPS) + decay_rate * master
        weight_norm = jnp.sqrt(lax.optimization_barrier(jnp.sum((master * master).reshape(LAYERS, -1), axis=1)))
        update_norm = jnp.sqrt(lax.optimization_barrier(jnp.sum((update * update).reshape(LAYERS, -1), axis=1)))
        trust_one = weight_norm / update_norm
        shaped_trust = trust_one.reshape((LAYERS,) + (1,) * (master.ndim - 1))
        new_params.append(master - LEARN_RATE * shaped_trust * update)
        new_firsts.append(moment_one)
        trust_rows.append(trust_one)
    trust_ratios = jnp.stack(trust_rows).T
    return (hidden_out, logits_out, grad_hidden, grad_logits, gradients[0], gradients[1], gradients[2], gradients[3], gradients[4], gradients[5], new_params[0], new_params[1], new_params[2], new_params[3], new_params[4], new_params[5], new_firsts[0], new_firsts[1], new_firsts[2], new_firsts[3], new_firsts[4], new_firsts[5], trust_ratios)
```

```python
import functools

import jax
import jax.numpy as jnp
from jax import lax
from jax.experimental import pallas as pl
from jax.experimental.pallas import tpu as pltpu
from jax.sharding import PartitionSpec as P

LAYERS = 2


NORM_EPS = 1e-05
ADAM_EPS = 1e-06
BETA_ONE = 0.9
BETA_TWO = 0.999
CORRECT_ONE = 1.0
CORRECT_TWO = 0.632304575228943
LEARN_RATE = 0.3
DECAY_RATE = 0.01
NEG_FILL = -1e30


def layer_norm(values, gain, shift):
    center = values - jnp.mean(values, axis=-1, keepdims=True)
    spread = jnp.mean(center * center, axis=-1, keepdims=True)
    return center * lax.rsqrt(spread + NORM_EPS) * gain + shift


def gelu_exact(values):
    return jax.nn.gelu(values, approximate=False)


def plain_shards(
    hidden_in,
    logits_in,
    cotangent,
    bucket_ids,
    seq_counts,
    key_mask,
    w_qkv,
    w_out,
    w_in,
    w_back,
    vectors,
    bias_in,
    m_qkv,
    m_out,
    m_in,
    m_back,
    m_vectors,
    m_bias,
    v_qkv,
    v_out,
    v_in,
    v_back,
    v_vectors,
    v_bias,
):
    tensor_parts = lax.axis_size("tensor")
    tensor_index = lax.axis_index("tensor")
    data_parts = lax.axis_size("dp")
    tokens_here = hidden_in.shape[0]
    share_rows = tokens_here // tensor_parts
    first_row = tensor_index * share_rows
    block_count = logits_in.shape[0]
    heads_here = logits_in.shape[1]
    block_len = logits_in.shape[2]
    model_width = hidden_in.shape[1]
    head_cols = w_qkv.shape[3]
    head_size = head_cols // heads_here
    hidden_cols = w_in.shape[2]
    score_scale = head_size ** (-0.5)
    bucket = bucket_ids[0]
    seq_span = jnp.where(
        bucket == 0, block_len // 4, jnp.where(bucket == 1, block_len // 2, block_len)
    )
    position = jnp.arange(tokens_here, dtype=jnp.int32)
    seq_flat = position // seq_span
    seq_of = seq_flat.reshape(block_count, block_len)
    live_keys = ((key_mask == 1) & (seq_flat < seq_counts[0])).reshape(block_count, block_len)
    allowed = (seq_of[:, :, None] == seq_of[:, None, :]) & live_keys[:, None, :]
    vec_all, bin_all = (
        lax.all_gather(vectors.astype(jnp.bfloat16), ("dp", "tensor"), axis=2, tiled=True),
        lax.all_gather(bias_in.astype(jnp.bfloat16), ("dp", "tensor"), axis=1, tiled=True),
    )
    vec_all = vec_all.astype(jnp.float32)
    bin_all = bin_all.astype(jnp.float32)

    def sum_forward(term_fn):
        return lax.psum_scatter(
            term_fn(jnp.int32(0), share_rows * lax.axis_size("tensor")).astype(jnp.bfloat16),
            "tensor",
            scatter_dimension=0,
            tiled=True,
        ).astype(jnp.float32)

    def sum_backward(term_fn):
        return lax.psum_scatter(
            term_fn(jnp.int32(0), share_rows * lax.axis_size("tensor")).astype(jnp.bfloat16),
            "tensor",
            scatter_dimension=0,
            tiled=True,
        ).astype(jnp.float32)

    def gather_rows(own_rows):
        return lax.all_gather(own_rows, "tensor", axis=0, tiled=True)

    def gather_grads(own_rows):
        return lax.all_gather(own_rows, "tensor", axis=0, tiled=True)

    def own_cols(vector):
        return lax.dynamic_slice_in_dim(vector, tensor_index * head_cols, head_cols)

    def place_cols(part_sum, total_len, offset):
        return lax.dynamic_update_slice(jnp.zeros((total_len,), jnp.float32), part_sum, (offset,))

    def blocked(matrix):
        return matrix.reshape(block_count, block_len, head_cols)

    def headed(matrix):
        return matrix.reshape(block_len, heads_here, head_size)

    def block_scores(query_b, keys_b, earlier_b):
        raw = jnp.einsum(
            "ihe,jhe->hij", headed(query_b), headed(keys_b), preferred_element_type=jnp.float32
        )
        return raw * score_scale + earlier_b.astype(jnp.float32)

    def attend_block(inputs):
        query_b, keys_b, values_b, earlier_b, allowed_b = inputs
        scores = block_scores(query_b, keys_b, earlier_b)
        row_top = jnp.max(jnp.where(allowed_b[None], scores, NEG_FILL), axis=-1, keepdims=True)
        unscaled = jnp.exp(jnp.where(allowed_b[None], scores - row_top, NEG_FILL))
        row_total = jnp.sum(unscaled, axis=-1, keepdims=True)
        row_total = jnp.where(row_total > 0.5, row_total, 1.0)
        probs_low = (unscaled / row_total).astype(jnp.bfloat16)
        mixed = jnp.einsum(
            "hij,jhe->ihe", probs_low, headed(values_b), preferred_element_type=jnp.float32
        )
        return (
            mixed.reshape(block_len, head_cols).astype(jnp.bfloat16),
            scores.astype(jnp.bfloat16),
            row_top,
            row_total,
        )

    def attend_back(inputs):
        query_b, keys_b, values_b, earlier_b, allowed_b, row_top, row_total, dmixed_b, dlater_b = (
            inputs
        )
        scores = block_scores(query_b, keys_b, earlier_b)
        unscaled = jnp.exp(jnp.where(allowed_b[None], scores - row_top, NEG_FILL))
        probs = unscaled / row_total
        probs_low = probs.astype(jnp.bfloat16)
        dmixed_heads = headed(dmixed_b)
        dvalues = jnp.einsum(
            "hij,ihe->jhe", probs_low, dmixed_heads, preferred_element_type=jnp.float32
        )
        dprobs = jnp.einsum(
            "ihe,jhe->hij", dmixed_heads, headed(values_b), preferred_element_type=jnp.float32
        )
        dlocal = probs * (dprobs - jnp.sum(probs * dprobs, axis=-1, keepdims=True))
        dscores = (dlocal + dlater_b.astype(jnp.float32)).astype(jnp.bfloat16)
        dquery = (
            jnp.einsum("hij,jhe->ihe", dscores, headed(keys_b), preferred_element_type=jnp.float32)
            * score_scale
        )
        dkeys = (
            jnp.einsum("hij,ihe->jhe", dscores, headed(query_b), preferred_element_type=jnp.float32)
            * score_scale
        )
        return (
            dquery.reshape(block_len, head_cols),
            dkeys.reshape(block_len, head_cols),
            dvalues.reshape(block_len, head_cols),
            dscores,
        )

    full_in = hidden_in
    own_in = lax.dynamic_slice_in_dim(hidden_in, first_row, share_rows, 0)
    earlier = logits_in
    records = []
    for layer_at in range(LAYERS):
        fetched = (
            lax.all_gather(w_qkv[layer_at].astype(jnp.bfloat16), "dp", axis=1, tiled=True),
            lax.all_gather(w_out[layer_at].astype(jnp.bfloat16), "dp", axis=1, tiled=True),
            lax.all_gather(w_in[layer_at].astype(jnp.bfloat16), "dp", axis=0, tiled=True),
            lax.all_gather(w_back[layer_at].astype(jnp.bfloat16), "dp", axis=1, tiled=True),
        )
        forward_wqkv, forward_wout, forward_win, forward_wback = fetched
        forward_vector = vec_all[layer_at]
        forward_query = (
            jnp.dot(full_in, forward_wqkv[0], preferred_element_type=jnp.float32)
            + own_cols(forward_vector[2])
        ).astype(jnp.bfloat16)
        forward_keys = jnp.dot(full_in, forward_wqkv[1], preferred_element_type=jnp.float32).astype(
            jnp.bfloat16
        )
        forward_values = (
            jnp.dot(full_in, forward_wqkv[2], preferred_element_type=jnp.float32)
            + own_cols(forward_vector[3])
        ).astype(jnp.bfloat16)
        forward_attn_out, stored, forward_row_top, forward_row_total = lax.map(
            attend_block,
            (
                blocked(forward_query),
                blocked(forward_keys),
                blocked(forward_values),
                earlier,
                allowed,
            ),
        )
        forward_attn_out = forward_attn_out.reshape(tokens_here, head_cols)

        def attn_term(begin_row, row_count):
            return jnp.dot(forward_attn_out, forward_wout, preferred_element_type=jnp.float32)

        forward_mid_pre = sum_forward(attn_term) + forward_vector[4] + own_in.astype(jnp.float32)
        mid_own = layer_norm(forward_mid_pre, forward_vector[0], forward_vector[5]).astype(
            jnp.bfloat16
        )
        forward_mid_full = gather_rows(mid_own)
        bias_here = lax.dynamic_slice_in_dim(
            bin_all[layer_at], tensor_index * hidden_cols, hidden_cols
        )
        forward_pre_act = (
            jnp.dot(forward_mid_full, forward_win, preferred_element_type=jnp.float32) + bias_here
        )
        forward_active = gelu_exact(forward_pre_act).astype(jnp.bfloat16)

        def ffn_term(begin_row, row_count):
            return jnp.dot(forward_active, forward_wback, preferred_element_type=jnp.float32)

        forward_out_pre = sum_forward(ffn_term) + forward_vector[6] + mid_own.astype(jnp.float32)
        out_own = layer_norm(forward_out_pre, forward_vector[1], forward_vector[7]).astype(
            jnp.bfloat16
        )
        forward_state = (
            forward_query,
            forward_keys,
            forward_values,
            forward_attn_out,
            forward_row_top,
            forward_row_total,
            forward_mid_pre,
            forward_mid_full,
            forward_pre_act,
            forward_out_pre,
        )
        out_own, stored, state = (out_own, stored, forward_state)
        records.append((full_in, earlier, fetched, state))
        earlier = stored
        own_in = out_own
        if layer_at + 1 < LAYERS:
            full_in = gather_rows(out_own)
    logits_out = earlier
    d_own = cotangent.astype(jnp.float32)
    d_later = jnp.zeros_like(logits_in)
    mat_grads = [None] * LAYERS
    vec_grads = [None] * LAYERS
    bin_grads = [None] * LAYERS
    for layer_at in reversed(range(LAYERS)):
        full_in, earlier, fetched, state = records[layer_at]
        wqkv = lax.all_gather(w_qkv[layer_at].astype(jnp.bfloat16), "dp", axis=1, tiled=True)
        wout = lax.all_gather(w_out[layer_at].astype(jnp.bfloat16), "dp", axis=1, tiled=True)
        win = lax.all_gather(w_in[layer_at].astype(jnp.bfloat16), "dp", axis=0, tiled=True)
        wback = lax.all_gather(w_back[layer_at].astype(jnp.bfloat16), "dp", axis=1, tiled=True)
        (
            query,
            keys,
            values,
            attn_out,
            backward_row_top,
            backward_row_total,
            mid_pre,
            mid_full,
            pre_act,
            out_pre,
        ) = state
        backward_vector = vec_all[layer_at]
        out_grad, gain_two, shift_two = jax.vjp(
            layer_norm, out_pre, backward_vector[1], backward_vector[7]
        )[1](d_own)
        d_ffn = gather_grads(out_grad.astype(jnp.bfloat16))
        active = gelu_exact(pre_act).astype(jnp.bfloat16)
        grad_back = jnp.einsum("tf,td->fd", active, d_ffn, preferred_element_type=jnp.float32)
        d_active = jnp.einsum("td,fd->tf", d_ffn, wback, preferred_element_type=jnp.float32)
        d_pre = jax.vjp(gelu_exact, pre_act)[1](d_active)[0].astype(jnp.bfloat16)
        grad_in = jnp.einsum("td,tf->df", mid_full, d_pre, preferred_element_type=jnp.float32)

        def mid_term(begin_row, row_count):
            return jnp.einsum("tf,df->td", d_pre, win, preferred_element_type=jnp.float32)

        mid_grad = sum_backward(mid_term) + out_grad
        attn_grad, gain_one, shift_one = jax.vjp(
            layer_norm, mid_pre, backward_vector[0], backward_vector[5]
        )[1](mid_grad)
        d_attn = gather_grads(attn_grad.astype(jnp.bfloat16))
        grad_out_proj = jnp.einsum(
            "tc,td->cd", attn_out, d_attn, preferred_element_type=jnp.float32
        )
        d_mixed = jnp.einsum("td,cd->tc", d_attn, wout, preferred_element_type=jnp.float32).astype(
            jnp.bfloat16
        )
        backward_dquery, backward_dkeys, backward_dvalues, backward_dscores = lax.map(
            attend_back,
            (
                blocked(query),
                blocked(keys),
                blocked(values),
                earlier,
                allowed,
                backward_row_top,
                backward_row_total,
                blocked(d_mixed),
                d_later,
            ),
        )
        backward_dquery = backward_dquery.reshape(tokens_here, head_cols).astype(jnp.bfloat16)
        backward_dkeys = backward_dkeys.reshape(tokens_here, head_cols).astype(jnp.bfloat16)
        backward_dvalues = backward_dvalues.reshape(tokens_here, head_cols).astype(jnp.bfloat16)
        grad_qkv = jnp.stack(
            [
                jnp.einsum(
                    "td,tc->dc", full_in, backward_dquery, preferred_element_type=jnp.float32
                ),
                jnp.einsum(
                    "td,tc->dc", full_in, backward_dkeys, preferred_element_type=jnp.float32
                ),
                jnp.einsum(
                    "td,tc->dc", full_in, backward_dvalues, preferred_element_type=jnp.float32
                ),
            ]
        )

        def input_term(begin_row, row_count):
            total_term = jnp.einsum(
                "tc,dc->td", backward_dquery, wqkv[0], preferred_element_type=jnp.float32
            )
            total_term = total_term + jnp.einsum(
                "tc,dc->td", backward_dkeys, wqkv[1], preferred_element_type=jnp.float32
            )
            return total_term + jnp.einsum(
                "tc,dc->td", backward_dvalues, wqkv[2], preferred_element_type=jnp.float32
            )

        in_grad = sum_backward(input_term) + attn_grad
        col_offset = tensor_index * head_cols
        vec_grad = jnp.stack(
            [
                gain_one,
                gain_two,
                place_cols(
                    jnp.sum(backward_dquery.astype(jnp.float32), axis=0), model_width, col_offset
                ),
                place_cols(
                    jnp.sum(backward_dvalues.astype(jnp.float32), axis=0), model_width, col_offset
                ),
                jnp.sum(attn_grad, axis=0),
                shift_one,
                jnp.sum(out_grad, axis=0),
                shift_two,
            ]
        )
        bin_grad = place_cols(
            jnp.sum(d_pre.astype(jnp.float32), axis=0),
            hidden_cols * tensor_parts,
            tensor_index * hidden_cols,
        )
        d_own, d_later, mats, vec_grad, bin_grad = (
            in_grad,
            backward_dscores,
            (grad_qkv, grad_out_proj, grad_in, grad_back),
            vec_grad,
            bin_grad,
        )
        totals = (
            lax.psum(mats[0].astype(jnp.bfloat16), "dp").astype(jnp.float32),
            lax.psum(mats[1].astype(jnp.bfloat16), "dp").astype(jnp.float32),
            lax.psum(mats[2].astype(jnp.bfloat16), "dp").astype(jnp.float32),
            lax.psum(mats[3].astype(jnp.bfloat16), "dp").astype(jnp.float32),
        )
        data_index = lax.axis_index("dp")
        mat_grads[layer_at] = tuple(
            (
                lax.dynamic_slice_in_dim(
                    whole,
                    data_index * (whole.shape[axis_at] // data_parts),
                    whole.shape[axis_at] // data_parts,
                    axis_at,
                )
                for whole, axis_at in zip(totals, (1, 1, 0, 1))
            )
        )
        vec_grads[layer_at] = vec_grad
        bin_grads[layer_at] = bin_grad
    grad_logits = d_later.astype(jnp.float32)
    vec_sum, bin_sum = (
        lax.psum_scatter(jnp.stack(vec_grads), ("dp", "tensor"), scatter_dimension=2, tiled=True),
        lax.psum_scatter(jnp.stack(bin_grads), ("dp", "tensor"), scatter_dimension=1, tiled=True),
    )
    grads_all = (
        jnp.stack([mat_grads[level_at][0] for level_at in range(LAYERS)]),
        jnp.stack([mat_grads[level_at][1] for level_at in range(LAYERS)]),
        jnp.stack([mat_grads[level_at][2] for level_at in range(LAYERS)]),
        jnp.stack([mat_grads[level_at][3] for level_at in range(LAYERS)]),
        vec_sum,
        bin_sum,
    )
    masters = (w_qkv, w_out, w_in, w_back, vectors, bias_in)
    firsts = (m_qkv, m_out, m_in, m_back, m_vectors, m_bias)
    seconds = (v_qkv, v_out, v_in, v_back, v_vectors, v_bias)
    decays = (DECAY_RATE, DECAY_RATE, DECAY_RATE, DECAY_RATE, 0.0, 0.0)
    moved = []
    for master, gradient, first_prev, second_prev, decay_rate in zip(
        masters, grads_all, firsts, seconds, decays
    ):
        moment_one = BETA_ONE * first_prev + (1.0 - BETA_ONE) * gradient
        moment_two = BETA_TWO * second_prev + (1.0 - BETA_TWO) * gradient * gradient
        update = (
            moment_one / CORRECT_ONE / (jnp.sqrt(moment_two / CORRECT_TWO) + ADAM_EPS)
            + decay_rate * master
        )
        moved.append((moment_one, update))
    weight_sq = jnp.stack(
        [jnp.sum((master * master).reshape(LAYERS, -1), axis=1) for master in masters]
    )
    update_sq = jnp.stack(
        [jnp.sum((moved_one[1] * moved_one[1]).reshape(LAYERS, -1), axis=1) for moved_one in moved]
    )
    weight_tot, update_tot = lax.psum((weight_sq, update_sq), ("dp", "tensor"))
    trust_all = jnp.sqrt(weight_tot) / jnp.sqrt(update_tot)
    new_params = tuple(
        (
            master
            - LEARN_RATE
            * trust_all[group_at].reshape((LAYERS,) + (1,) * (master.ndim - 1))
            * moved_one[1]
            for group_at, (master, moved_one) in enumerate(zip(masters, moved))
        )
    )
    return (
        own_in,
        logits_out,
        d_own,
        grad_logits,
        grads_all[0],
        grads_all[1],
        grads_all[2],
        grads_all[3],
        grads_all[4],
        grads_all[5],
        new_params[0],
        new_params[1],
        new_params[2],
        new_params[3],
        new_params[4],
        new_params[5],
        moved[0][0],
        moved[1][0],
        moved[2][0],
        moved[3][0],
        moved[4][0],
        moved[5][0],
        trust_all.T,
    )


MESH = pl.DeviceIdType.MESH
TILE = 256
LANES = 128
ROWS_MAT = 4


def dot_nn(left, right):
    return lax.dot_general(
        left, right, (((1,), (0,)), ((), ())), preferred_element_type=jnp.float32
    )


def dot_nt(left, right):
    return lax.dot_general(
        left, right, (((1,), (1,)), ((), ())), preferred_element_type=jnp.float32
    )


def norm_parts(values):
    center = values - jnp.mean(values, axis=-1, keepdims=True)
    spread = jnp.mean(center * center, axis=-1, keepdims=True)
    return center, lax.rsqrt(spread + NORM_EPS)


def step_kernel(
    data_parts,
    hidden_in,
    logits_in,
    cotangent,
    row_ids,
    key_ids,
    small_in,
    own_qkv,
    own_out,
    own_in,
    own_back,
    hidden_out,
    logits_out,
    grad_hidden,
    grad_scores,
    sum_qkv,
    sum_out,
    sum_in,
    sum_back,
    small_out,
    w_q,
    w_o,
    w_i,
    w_b,
    scores,
    probs,
    h_full,
    m_full,
    active,
    attn,
    h_turn,
    m_turn,
    g_turn,
    o_turn,
    slope,
    qkv,
    x_own,
    y_own,
    d_qkv,
    d_attn,
    d_own,
    d_keep,
    turn_v,
    turn_k,
    part,
    got_core,
    sum_chip,
    got_y,
    vec_got,
    vec_all,
    bin_all,
    small_acc,
    small_got,
    small_send,
    small_sum,
    pk_q,
    pk_o,
    pk_i,
    pk_b,
    rx_q,
    rx_o,
    rx_i,
    rx_b,
    rz_q,
    rz_o,
    rz_i,
    rz_b,
    fin_q,
    fin_o,
    fin_i,
    fin_b,
    load_sem,
    own_sem,
    zs_sem,
    zr_sem,
    xs_sem,
    xr_sem,
    core_s,
    core_r,
    ys_sem,
    yr_sem,
    gat_s,
    gat_r,
    vec_s,
    vec_r,
    sml_s,
    sml_r,
    gxs_sem,
    gxr_sem,
    gzs_sem,
    gzr_sem,
    fin_sem,
    out_sem,
):
    dp = lax.axis_index("dp")
    ten = lax.axis_index("tensor")
    cols_n = data_parts // 2
    side = lax.rem(dp, 2)
    place = dp // 2
    row_y = ten // 2
    core = lax.rem(ten, 2)
    across = dp + 1 - 2 * side
    core_mate = ten + 1 - 2 * core
    y_mate = lax.rem(ten + 2, 4)
    width = hidden_in.shape[1]
    tokens = hidden_in.shape[0]
    share = tokens // 4
    half = share // 2
    head_cols = qkv.shape[3]
    hidden_cols = slope.shape[2]
    cut = width // data_parts
    tiles = width // TILE
    f32 = jnp.float32
    b16 = jnp.bfloat16

    def along(step):
        return lax.rem(place + step, cols_n) * 2 + side

    def mult(value, by):
        return pl.multiple_of(value, by)

    def rdma(src, dst, send, recv, to_dp, to_ten):
        return pltpu.make_async_remote_copy(
            src_ref=src,
            dst_ref=dst,
            send_sem=send,
            recv_sem=recv,
            device_id=(to_dp, to_ten),
            device_id_type=MESH,
        )

    def region(kind, layer, dev):
        at = pl.ds(mult(dev * cut, cut), cut)
        if kind == 0:
            return w_q.at[layer, :, at, :]
        if kind == 1:
            return w_o.at[layer, :, at]
        if kind == 2:
            return w_i.at[layer, at, :]
        return w_b.at[layer, :, at]

    owns = (own_qkv, own_out, own_in, own_back)

    load_h = pltpu.make_async_copy(hidden_in, h_full, load_sem.at[0])
    load_s = pltpu.make_async_copy(logits_in.at[0], scores, load_sem.at[1])
    load_h.start()
    load_s.start()
    own_loads = []
    for layer in range(LAYERS):
        for kind in range(ROWS_MAT):
            copy = pltpu.make_async_copy(
                owns[kind].at[layer], region(kind, layer, dp), own_sem.at[layer, kind]
            )
            copy.start()
            own_loads.append(copy)

    barrier = pltpu.get_barrier_semaphore()

    def greet(step, carry):
        pl.semaphore_signal(
            barrier, inc=1, device_id=(lax.rem(dp + step, data_parts), ten), device_id_type=MESH
        )
        return carry

    lax.fori_loop(1, data_parts, greet, 0)
    for other in range(1, 4):
        pl.semaphore_signal(
            barrier, inc=1, device_id=(dp, lax.rem(ten + other, 4)), device_id_type=MESH
        )
    pl.semaphore_wait(barrier, data_parts + 2)

    vec_got[ten, dp] = small_in[...]

    def vec_one(step):
        return rdma(
            small_in,
            vec_got.at[ten, dp],
            vec_s.at[step - 1],
            vec_r.at[step - 1],
            lax.rem(dp + step, data_parts),
            ten,
        )

    def vec_go(step, carry):
        vec_one(step).start()
        return carry

    lax.fori_loop(1, data_parts, vec_go, 0)

    def w_z(kind, layer, step):
        return rdma(
            owns[kind].at[layer],
            region(kind, layer, dp),
            zs_sem.at[layer, kind, step - 1],
            zr_sem.at[layer, kind, step - 1],
            along(step),
            ten,
        )

    def w_x_own(kind, layer):
        return rdma(
            owns[kind].at[layer],
            region(kind, layer, dp),
            xs_sem.at[layer, kind, 0],
            xr_sem.at[layer, kind, 0],
            across,
            ten,
        )

    def w_x_pass(kind, layer, step):
        came = region(kind, layer, along(cols_n - step))
        return rdma(
            came,
            came,
            xs_sem.at[layer, kind, step],
            xr_sem.at[layer, kind, step],
            across,
            ten,
        )

    order = [(kind, layer) for layer in range(LAYERS) for kind in range(ROWS_MAT)]
    for kind, layer in order:
        for step in range(1, cols_n):
            w_z(kind, layer, step).start()
        if (kind, layer) in order[:2]:
            w_x_own(kind, layer).start()

    def pass_on(index):
        if index >= len(order):
            return
        kind, layer = order[index]
        for step in range(1, cols_n):
            w_z(kind, layer, step).wait_recv()
            w_x_pass(kind, layer, step).start()
        if index + 2 < len(order):
            w_x_own(*order[index + 2]).start()

    def have(index):
        kind, layer = order[index]
        w_x_own(kind, layer).wait_recv()
        for step in range(1, cols_n):
            w_x_pass(kind, layer, step).wait_recv()

    def vec_wait(step, carry):
        vec_one(step).wait_send()
        vec_one(step).wait_recv()
        return carry

    lax.fori_loop(1, data_parts, vec_wait, 0)

    def vec_two(step):
        return rdma(
            vec_got.at[ten],
            vec_got.at[ten],
            vec_s.at[data_parts - 2 + step],
            vec_r.at[data_parts - 2 + step],
            dp,
            lax.rem(ten + step, 4),
        )

    for step in range(1, 4):
        vec_two(step).start()
    for step in range(1, 4):
        vec_two(step).wait_send()
        vec_two(step).wait_recv()
    for dev in range(data_parts):
        total = vec_got[0, dev].astype(f32)
        for other in range(1, 4):
            total = total + vec_got[other, dev].astype(f32)
        vec_all[:, dev * LANES : (dev + 1) * LANES] = total[0 : LAYERS * 8]
    for piece in range(hidden_cols // LANES):
        got = vec_got[piece % 4, ten * 2 + piece // 4].astype(f32)
        bin_all[:, piece * LANES : (piece + 1) * LANES] = got[LAYERS * 8 : LAYERS * 8 + 8]

    def vec_row(layer, row):
        return vec_all[layer * 8 + row : layer * 8 + row + 1, :]

    def block_rows(which_y, which_core):
        return pl.ds(mult((which_y * 2 + which_core) * share, share), share)

    far_block = block_rows(1 - row_y, 1 - core)
    mate_block = block_rows(row_y, 1 - core)
    over_block = block_rows(1 - row_y, core)
    own_block = block_rows(row_y, core)

    def tile_cols(tile):
        return pl.ds(mult(tile * TILE, TILE), TILE)

    def send_core(tile, which):
        rows = far_block if which == 0 else mate_block
        return rdma(
            part.at[rows, tile_cols(tile)],
            got_core.at[which, :, tile_cols(tile)],
            core_s.at[tile, which],
            core_r.at[tile, which],
            dp,
            core_mate,
        )

    def send_y(tile):
        return rdma(
            sum_chip.at[:, tile_cols(tile)],
            got_y.at[:, tile_cols(tile)],
            ys_sem.at[tile],
            yr_sem.at[tile],
            dp,
            y_mate,
        )

    def add_core(tile):
        send_core(tile, 0).wait_recv()
        at = tile_cols(tile)
        sum_chip[:, at] = (
            part[over_block, at].astype(f32) + got_core[0, :, at].astype(f32)
        ).astype(b16)
        send_y(tile).start()

    def sum_start(tile_fn):
        def one(tile, carry):
            part[:, tile_cols(tile)] = tile_fn(tile).astype(b16)
            send_core(tile, 0).start()
            send_core(tile, 1).start()

            @pl.when(tile > 0)
            def _():
                add_core(tile - 1)

            return carry

        lax.fori_loop(0, tiles, one, 0)
        add_core(tiles - 1)

    def sum_end():
        for tile in range(tiles):
            send_core(tile, 1).wait_recv()
            send_y(tile).wait_recv()
        for tile in range(tiles):
            send_core(tile, 0).wait_send()
            send_core(tile, 1).wait_send()
            send_y(tile).wait_send()

    def sum_rows(which):
        at = pl.ds(which * half, half)
        mine = pl.ds(mult(ten * share + which * half, half), half)
        return (
            part[mine, :].astype(f32) + got_core[1, at, :].astype(f32) + got_y[at, :].astype(f32)
        )

    def gat_copy(buf, which, kind):
        if kind == 2:
            rows = pl.ds(mult(y_mate * share + which * half, half), half)
        else:
            rows = pl.ds(mult(ten * share + which * half, half), half)
        return rdma(
            buf.at[rows],
            buf.at[rows],
            gat_s.at[which, kind],
            gat_r.at[which, kind],
            dp,
            y_mate if kind == 1 else core_mate,
        )

    def gat_start(buf, which):
        gat_copy(buf, which, 1).start()
        gat_copy(buf, which, 0).start()

    def gat_end(buf):
        for which in range(2):
            gat_copy(buf, which, 1).wait_recv()
            gat_copy(buf, which, 2).start()
        for which in range(2):
            gat_copy(buf, which, 0).wait_recv()
            gat_copy(buf, which, 2).wait_recv()
        for which in range(2):
            for kind in range(3):
                gat_copy(buf, which, kind).wait_send()

    def own_rows(which):
        return pl.ds(mult(ten * share + which * half, half), half)

    def turn(src, dst, layer):
        def one(at, carry):
            dst[layer, tile_cols(at), :] = src[:, tile_cols(at)].T
            return carry

        lax.fori_loop(0, src.shape[1] // TILE, one, 0)

    lane = lax.broadcasted_iota(jnp.int32, (1, LANES), 1)
    low_lanes = jnp.where(lane < 64, 1.0, 0.0).astype(b16)
    high_lanes = jnp.where(lane < 64, 0.0, 1.0).astype(b16)
    lane_masks = (low_lanes, high_lanes)
    scale = 0.125
    score_rows = 256
    pairs = head_cols // LANES

    def pair_cols(pair):
        return pl.ds(mult(pair * LANES, LANES), LANES)

    def attend(layer):
        def one(step, carry):
            pair = step // (tokens // score_rows)
            rows = pl.ds(
                mult(lax.rem(step, tokens // score_rows) * score_rows, score_rows), score_rows
            )
            at = pair_cols(pair)
            queries = qkv[layer, 0, rows, at]
            keys = qkv[layer, 1, :, at]
            values = qkv[layer, 2, :, at]
            allowed = row_ids[rows, 0:1] == key_ids[0:1, :]
            mixed = jnp.zeros((score_rows, LANES), f32)
            for head in range(2):
                raw = dot_nt(queries, keys * lane_masks[head])
                full = raw * scale + scores[pair * 2 + head, rows, :].astype(f32)
                scores[pair * 2 + head, rows, :] = full.astype(b16)
                top = jnp.max(jnp.where(allowed, full, NEG_FILL), axis=-1, keepdims=True)
                weight = jnp.exp(jnp.where(allowed, full - top, NEG_FILL))
                total = jnp.sum(weight, axis=-1, keepdims=True)
                total = jnp.where(total > 0.5, total, 1.0)
                low = (weight * (1.0 / total)).astype(b16)
                probs[layer, pair * 2 + head, rows, :] = low
                mixed = mixed + dot_nn(low, values * lane_masks[head])
            attn[rows, at] = mixed.astype(b16)
            return carry

        lax.fori_loop(0, pairs * (tokens // score_rows), one, 0)

    def attend_back(layer, first):
        def pair_one(pair, carry):
            at = pair_cols(pair)
            turn_v[...] = jnp.zeros_like(turn_v)
            turn_k[...] = jnp.zeros_like(turn_k)

            def one(step, inner):
                rows = pl.ds(mult(step * score_rows, score_rows), score_rows)
                queries = qkv[layer, 0, rows, at]
                keys = qkv[layer, 1, :, at]
                values = qkv[layer, 2, :, at]
                grads = d_attn[rows, at]
                turned_q = queries.T
                turned_g = grads.T
                d_query = jnp.zeros((score_rows, LANES), f32)
                for head in range(2):
                    low = probs[layer, pair * 2 + head, rows, :]
                    prob = low.astype(f32)
                    d_prob = dot_nt(grads, values * lane_masks[head])
                    inner_sum = jnp.sum(prob * d_prob, axis=-1, keepdims=True)
                    d_score = prob * (d_prob - inner_sum)
                    if not first:
                        d_score = d_score + scores[pair * 2 + head, rows, :].astype(f32)
                    d_low = d_score.astype(b16)
                    scores[pair * 2 + head, rows, :] = d_low
                    d_query = d_query + dot_nn(d_low, keys * lane_masks[head])
                    part_rows = slice(head * 64, head * 64 + 64)
                    turn_v[part_rows, :] += dot_nn(turned_g[part_rows, :], low)
                    turn_k[part_rows, :] += dot_nn(turned_q[part_rows, :], d_low)
                d_qkv[0, rows, at] = (d_query * scale).astype(b16)
                return inner

            lax.fori_loop(0, tokens // score_rows, one, 0)
            d_qkv[1, :, at] = (turn_k[...] * scale).T.astype(b16)
            d_qkv[2, :, at] = turn_v[...].T.astype(b16)
            return carry

        lax.fori_loop(0, pairs, pair_one, 0)

    own_cols = pl.ds(mult(ten * head_cols, head_cols), head_cols)
    small_acc[...] = jnp.zeros_like(small_acc)
    load_h.wait()
    for copy in own_loads:
        copy.wait()
    load_s.wait()
    for layer in range(LAYERS):
        base = layer * ROWS_MAT
        if layer == 0:
            pass_on(0)
        have(base)
        for which in range(3):
            product = dot_nn(h_full[...], w_q[layer, which])
            if which == 0:
                product = product + vec_all[layer * 8 + 2 : layer * 8 + 3, own_cols]
            if which == 2:
                product = product + vec_all[layer * 8 + 3 : layer * 8 + 4, own_cols]
            qkv[layer, which] = product.astype(b16)
        pass_on(base + 1)
        attend(layer)
        have(base + 1)

        sum_start(lambda tile: dot_nn(attn[...], w_o[layer, :, tile_cols(tile)]))
        pass_on(base + 2)
        sum_end()
        for which in range(2):
            at = pl.ds(which * half, half)
            mid = sum_rows(which) + vec_row(layer, 4) + h_full[own_rows(which), :].astype(f32)
            x_own[layer, at, :] = mid
            center, rate = norm_parts(mid)
            m_full[own_rows(which), :] = (
                center * rate * vec_row(layer, 0) + vec_row(layer, 5)
            ).astype(b16)
            gat_start(m_full, which)
        turn(attn, o_turn, layer)
        turn(h_full, h_turn, layer)
        gat_end(m_full)
        have(base + 2)

        def ffn_tile(tile, carry):
            at = tile_cols(tile)
            pre = dot_nn(m_full[...], w_i[layer, :, at]) + bin_all[layer : layer + 1, at]
            cumul = 0.5 * (1.0 + lax.erf(pre * 0.7071067811865476))
            dens = jnp.exp(-0.5 * pre * pre) * 0.3989422804014327
            active[:, at] = (pre * cumul).astype(b16)
            slope[layer, :, at] = (cumul + pre * dens).astype(b16)
            return carry

        lax.fori_loop(0, hidden_cols // TILE, ffn_tile, 0)
        pass_on(base + 3)
        turn(m_full, m_turn, layer)
        have(base + 3)
        sum_start(lambda tile: dot_nn(active[...], w_b[layer, :, tile_cols(tile)]))
        turn(active, g_turn, layer)
        pass_on(base + 4)
        sum_end()
        for which in range(2):
            at = pl.ds(which * half, half)
            late = sum_rows(which) + vec_row(layer, 6) + m_full[own_rows(which), :].astype(f32)
            y_own[layer, at, :] = late
            center, rate = norm_parts(late)
            result = (center * rate * vec_row(layer, 1) + vec_row(layer, 7)).astype(b16)
            if layer + 1 < LAYERS:
                h_full[own_rows(which), :] = result
                gat_start(h_full, which)
            else:
                hidden_out[at, :] = result
        if layer + 1 < LAYERS:
            gat_end(h_full)

    out_logits = pltpu.make_async_copy(scores, logits_out, out_sem.at[0])
    out_logits.start()
    for kind, layer in order:
        for step in range(1, cols_n):
            w_z(kind, layer, step).wait_send()
            w_x_pass(kind, layer, step).wait_send()
        w_x_own(kind, layer).wait_send()

    packs = (pk_q, pk_o, pk_i, pk_b)
    got_x = (rx_q, rx_o, rx_i, rx_b)
    got_z = (rz_q, rz_o, rz_i, rz_b)
    fins = (fin_q, fin_o, fin_i, fin_b)
    sums = (sum_qkv, sum_out, sum_in, sum_back)

    def g_x(kind, layer, at):
        return rdma(
            packs[kind].at[at, 1 - side],
            got_x[kind].at[layer, at],
            gxs_sem.at[kind, at],
            gxr_sem.at[layer, kind, at],
            across,
            ten,
        )

    def g_z(kind, layer, step):
        to = lax.rem(place + step, cols_n)
        return rdma(
            packs[kind].at[to, side],
            got_z[kind].at[layer, step - 1],
            gzs_sem.at[kind, step - 1],
            gzr_sem.at[layer, kind, step - 1],
            to * 2 + side,
            ten,
        )

    def g_free(kind, layer):
        for at in range(cols_n):
            g_x(kind, layer, at).wait_send()
        for step in range(1, cols_n):
            g_z(kind, layer, step).wait_send()

    def chunks_of(kind):
        if kind == 0:
            return [(which,) for which in range(3)]
        if kind == 3:
            return [(pl.ds(piece * 256, 256),) for piece in range(hidden_cols // 256)]
        return [()]

    def g_mid(kind, layer):
        for step in range(1, cols_n + 1):
            to = lax.rem(place + step, cols_n)
            g_x(kind, layer, to).wait_recv()
            for piece in chunks_of(kind):
                ours = (to, side) + piece
                theirs = (layer, to) + piece
                packs[kind][ours] = (
                    packs[kind][ours].astype(f32) + got_x[kind][theirs].astype(f32)
                ).astype(b16)
            if step < cols_n:
                g_z(kind, layer, step).start()

    def g_end(kind, layer):
        for step in range(1, cols_n):
            g_z(kind, layer, step).wait_recv()
        if layer + 1 < LAYERS:
            fin_copy(kind, layer + 1).wait()
        for piece in chunks_of(kind):
            total = packs[kind][(place, side) + piece].astype(f32)
            for step in range(1, cols_n):
                total = total + got_z[kind][(layer, step - 1) + piece].astype(f32)
            fins[kind][piece if piece else (slice(None),)] = total
        fin_copy(kind, layer).start()

    def fin_copy(kind, layer):
        return pltpu.make_async_copy(fins[kind], sums[kind].at[layer], fin_sem.at[kind])

    def pair_rows(at):
        return pl.ds(mult(at * 2 * cut, 2 * cut), 2 * cut)

    def grad_back(layer):
        def one(at, carry):
            for piece in range(hidden_cols // 512):
                rows = slice(piece * 512, (piece + 1) * 512)
                value = dot_nn(g_turn[layer, rows, :], m_full[:, pair_rows(at)]).astype(b16)
                pk_b[at, 0, rows, :] = value[:, :cut]
                pk_b[at, 1, rows, :] = value[:, cut:]
            g_x(3, layer, at).start()
            return carry

        lax.fori_loop(0, cols_n, one, 0)

    def grad_in(layer):
        def one(at, carry):
            for piece in range(hidden_cols // 512):
                cols = slice(piece * 512, (piece + 1) * 512)
                value = dot_nn(m_turn[layer, pair_rows(at), :], active[:, cols]).astype(b16)
                pk_i[at, 0, :, cols] = value[:cut]
                pk_i[at, 1, :, cols] = value[cut:]
            g_x(2, layer, at).start()
            return carry

        lax.fori_loop(0, cols_n, one, 0)

    def grad_out(layer):
        def one(at, carry):
            value = dot_nn(o_turn[layer], h_full[:, pair_rows(at)]).astype(b16)
            pk_o[at, 0] = value[:, :cut]
            pk_o[at, 1] = value[:, cut:]
            g_x(1, layer, at).start()
            return carry

        lax.fori_loop(0, cols_n, one, 0)

    def grad_qkv(layer):
        def one(at, carry):
            for which in range(3):
                value = dot_nn(h_turn[layer, pair_rows(at), :], d_qkv[which]).astype(b16)
                pk_q[at, 0, which] = value[:cut]
                pk_q[at, 1, which] = value[cut:]
            g_x(0, layer, at).start()
            return carry

        lax.fori_loop(0, cols_n, one, 0)

    def norm_back(kept, upstream, gain):
        center, rate = norm_parts(kept)
        unit = center * rate
        scaled = upstream * gain
        down = rate * (
            scaled
            - jnp.mean(scaled, axis=-1, keepdims=True)
            - unit * jnp.mean(scaled * unit, axis=-1, keepdims=True)
        )
        return down, unit

    def note(row, values):
        small_acc[row : row + 1, :] += jnp.sum(values, axis=0, keepdims=True)

    for layer in reversed(range(LAYERS)):
        last = layer + 1 == LAYERS
        base = layer * 8
        for which in range(2):
            at = pl.ds(which * half, half)
            upstream = cotangent[at, :].astype(f32) if last else d_own[at, :]
            down, unit = norm_back(y_own[layer, at, :], upstream, vec_row(layer, 1))
            note(base + 1, upstream * unit)
            note(base + 7, upstream)
            note(base + 6, down)
            d_keep[at, :] = down
            m_full[own_rows(which), :] = down.astype(b16)
            gat_start(m_full, which)
        if not last:
            g_mid(0, layer + 1)
        gat_end(m_full)
        if not last:
            g_free(3, layer + 1)
            g_end(3, layer + 1)
        grad_back(layer)

        def slope_tile(tile, carry):
            at = tile_cols(tile)
            d_active = dot_nt(m_full[...], w_b[layer, at, :])
            d_pre = (d_active * slope[layer, :, at].astype(f32)).astype(b16)
            active[:, at] = d_pre
            small_acc[LAYERS * 8 + layer : LAYERS * 8 + layer + 1, at] = jnp.sum(
                d_pre.astype(f32), axis=0, keepdims=True
            )
            return carry

        lax.fori_loop(0, hidden_cols // TILE, slope_tile, 0)
        sum_start(lambda tile: dot_nt(active[...], w_i[layer, tile_cols(tile), :]))
        if not last:
            g_free(2, layer + 1)
            g_end(2, layer + 1)
        grad_in(layer)
        g_mid(3, layer)
        sum_end()
        for which in range(2):
            at = pl.ds(which * half, half)
            upstream = sum_rows(which) + d_keep[at, :]
            down, unit = norm_back(x_own[layer, at, :], upstream, vec_row(layer, 0))
            note(base + 0, upstream * unit)
            note(base + 5, upstream)
            note(base + 4, down)
            d_keep[at, :] = down
            h_full[own_rows(which), :] = down.astype(b16)
            gat_start(h_full, which)
        if not last:
            g_free(1, layer + 1)
            g_end(1, layer + 1)
        gat_end(h_full)
        d_attn[...] = dot_nt(h_full[...], w_o[layer]).astype(b16)
        grad_out(layer)
        if last:
            out_logits.wait()
        g_mid(2, layer)
        attend_back(layer, last)
        small_acc[base + 2 : base + 3, own_cols] = jnp.sum(
            d_qkv[0].astype(f32), axis=0, keepdims=True
        )
        small_acc[base + 3 : base + 4, own_cols] = jnp.sum(
            d_qkv[2].astype(f32), axis=0, keepdims=True
        )
        if not last:
            g_free(0, layer + 1)
            g_end(0, layer + 1)

        def input_tile(tile):
            rows = tile_cols(tile)
            total = dot_nt(d_qkv[0], w_q[layer, 0, rows, :])
            total = total + dot_nt(d_qkv[1], w_q[layer, 1, rows, :])
            return total + dot_nt(d_qkv[2], w_q[layer, 2, rows, :])

        sum_start(input_tile)
        grad_qkv(layer)
        g_mid(1, layer)
        sum_end()
        for which in range(2):
            at = pl.ds(which * half, half)
            result = sum_rows(which) + d_keep[at, :]
            if layer:
                d_own[at, :] = result
            else:
                grad_hidden[at, :] = result

    out_scores = pltpu.make_async_copy(scores, grad_scores, out_sem.at[1])
    out_scores.start()

    small_got[ten] = small_acc[...]

    def small_one(step):
        return rdma(
            small_acc,
            small_got.at[ten],
            sml_s.at[step - 1],
            sml_r.at[step - 1],
            dp,
            lax.rem(ten + step, 4),
        )

    for step in range(1, 4):
        small_one(step).start()
    g_mid(0, 0)
    for step in range(1, 4):
        small_one(step).wait_recv()
    mat_rows = LAYERS * 8
    for dev in range(data_parts):
        cols = slice(dev * LANES, (dev + 1) * LANES)
        total = small_got[0, 0:mat_rows, cols]
        for other in range(1, 4):
            total = total + small_got[other, 0:mat_rows, cols]
        small_send[dev, 0:mat_rows, :] = total
        from_cols = pl.ds(mult(((dev % 2) * 4 + ten) * LANES, LANES), LANES)
        small_send[dev, mat_rows : mat_rows + 8, :] = small_got[
            dev // 2, mat_rows : mat_rows + 8, from_cols
        ]

    def small_two(step):
        to = lax.rem(dp + step, data_parts)
        return rdma(
            small_send.at[to],
            small_sum.at[step - 1],
            sml_s.at[2 + step],
            sml_r.at[2 + step],
            to,
            ten,
        )

    def small_go(step, carry):
        small_two(step).start()
        return carry

    lax.fori_loop(1, data_parts, small_go, 0)
    g_end(3, 0)
    g_end(2, 0)
    g_end(1, 0)
    small_out[...] = small_send[dp]

    def small_wait(step, carry):
        small_two(step).wait_recv()
        small_two(step).wait_send()
        small_out[...] += small_sum[step - 1]
        return carry

    lax.fori_loop(1, data_parts, small_wait, 0)
    for step in range(1, 4):
        small_one(step).wait_send()
    g_end(0, 0)
    for kind in range(ROWS_MAT):
        g_free(kind, 0)
        fin_copy(kind, 0).wait()
    out_scores.wait()


def fits(parts, head_cols, hidden_cols, heads_here, tokens, width, blocks):
    data_parts, tensor_parts = parts
    return (
        tensor_parts == 4
        and data_parts % 2 == 0
        and data_parts > 2
        and width // data_parts == LANES
        and head_cols // heads_here == 64
        and head_cols % TILE == 0
        and hidden_cols == data_parts * LANES
        and hidden_cols % 512 == 0
        and blocks == 1
        and tokens % 512 == 0
    )


def shards(*arrays, parts):
    (
        hidden_in,
        logits_in,
        cotangent,
        bucket_ids,
        seq_counts,
        key_mask,
        w_qkv,
        w_out,
        w_in,
        w_back,
        vectors,
        bias_in,
    ) = arrays[:12]
    data_parts = parts[0]
    tokens, width = hidden_in.shape
    head_cols = w_qkv.shape[3]
    hidden_cols = w_in.shape[2]
    heads = logits_in.shape[1]
    if not fits(parts, head_cols, hidden_cols, heads, tokens, width, logits_in.shape[0]):
        return plain_shards(*arrays)
    f32 = jnp.float32
    b16 = jnp.bfloat16
    ten = lax.axis_index("tensor")
    share = tokens // 4
    cut = width // data_parts
    cols_n = data_parts // 2
    bucket = bucket_ids[0]
    seq_span = jnp.where(bucket == 0, tokens // 4, jnp.where(bucket == 1, tokens // 2, tokens))
    seq_of = jnp.arange(tokens, dtype=jnp.int32) // seq_span
    live = (key_mask == 1) & (seq_of < seq_counts[0])
    row_ids = jnp.broadcast_to(seq_of.astype(f32)[:, None], (tokens, LANES))
    key_ids = jnp.broadcast_to(jnp.where(live, seq_of, -1).astype(f32)[None, :], (8, tokens))
    owned = vectors.shape[2]
    spread = jnp.tile(vectors.reshape(LAYERS * 8, owned), (1, LANES // owned))
    mine = (jnp.arange(LANES, dtype=jnp.int32) // owned) == ten
    spread = jnp.where(mine[None, :], spread, 0.0)
    small_in = jnp.concatenate(
        [spread, bias_in, jnp.zeros((32 - LAYERS * 9, LANES), f32)], axis=0
    ).astype(b16)

    hbm = pl.BlockSpec(memory_space=pl.ANY)
    vmem = pl.BlockSpec(memory_space=pltpu.VMEM)
    dma = pltpu.SemaphoreType.DMA
    shape = jax.ShapeDtypeStruct
    n = LAYERS
    grad_shapes = (
        (3, cut, head_cols),
        (head_cols, cut),
        (cut, hidden_cols),
        (hidden_cols, cut),
    )
    results = pl.pallas_call(
        functools.partial(step_kernel, data_parts),
        out_shape=(
            shape((share, width), b16),
            shape((heads, tokens, tokens), b16),
            shape((share, width), f32),
            shape((heads, tokens, tokens), b16),
        )
        + tuple(shape((n,) + size, f32) for size in grad_shapes)
        + (shape((24, LANES), f32),),
        in_specs=[hbm, hbm, vmem, vmem, vmem, vmem, hbm, hbm, hbm, hbm],
        out_specs=(vmem, hbm, vmem, hbm, hbm, hbm, hbm, hbm, vmem),
        scratch_shapes=[
            pltpu.VMEM((n, 3, width, head_cols), b16),
            pltpu.VMEM((n, head_cols, width), b16),
            pltpu.VMEM((n, width, hidden_cols), b16),
            pltpu.VMEM((n, hidden_cols, width), b16),
            pltpu.VMEM((heads, tokens, tokens), b16),
            pltpu.VMEM((n, heads, tokens, tokens), b16),
            pltpu.VMEM((tokens, width), b16),
            pltpu.VMEM((tokens, width), b16),
            pltpu.VMEM((tokens, hidden_cols), b16),
            pltpu.VMEM((tokens, head_cols), b16),
            pltpu.VMEM((n, width, tokens), b16),
            pltpu.VMEM((n, width, tokens), b16),
            pltpu.VMEM((n, hidden_cols, tokens), b16),
            pltpu.VMEM((n, head_cols, tokens), b16),
            pltpu.VMEM((n, tokens, hidden_cols), b16),
            pltpu.VMEM((n, 3, tokens, head_cols), b16),
            pltpu.VMEM((n, share, width), f32),
            pltpu.VMEM((n, share, width), f32),
            pltpu.VMEM((3, tokens, head_cols), b16),
            pltpu.VMEM((tokens, head_cols), b16),
            pltpu.VMEM((share, width), f32),
            pltpu.VMEM((share, width), f32),
            pltpu.VMEM((LANES, tokens), f32),
            pltpu.VMEM((LANES, tokens), f32),
            pltpu.VMEM((tokens, width), b16),
            pltpu.VMEM((2, share, width), b16),
            pltpu.VMEM((share, width), b16),
            pltpu.VMEM((share, width), b16),
            pltpu.VMEM((4, data_parts, 32, LANES), b16),
            pltpu.VMEM((n * 8, width), f32),
            pltpu.VMEM((8, hidden_cols), f32),
            pltpu.VMEM((n * 8 + 8, width), f32),
            pltpu.VMEM((4, n * 8 + 8, width), f32),
            pltpu.VMEM((data_parts, n * 8 + 8, LANES), f32),
            pltpu.VMEM((data_parts - 1, n * 8 + 8, LANES), f32),
        ]
        + [pltpu.VMEM((cols_n, 2) + size, b16) for size in grad_shapes]
        + [pltpu.VMEM((n, cols_n) + size, b16) for size in grad_shapes]
        + [pltpu.VMEM((n, cols_n - 1) + size, b16) for size in grad_shapes]
        + [pltpu.VMEM(size, f32) for size in grad_shapes]
        + [
            dma((2,)),
            dma((n, 4)),
            dma((n, 4, cols_n - 1)),
            dma((n, 4, cols_n - 1)),
            dma((n, 4, cols_n)),
            dma((n, 4, cols_n)),
            dma((width // TILE, 2)),
            dma((width // TILE, 2)),
            dma((width // TILE,)),
            dma((width // TILE,)),
            dma((2, 3)),
            dma((2, 3)),
            dma((data_parts + 2,)),
            dma((data_parts + 2,)),
            dma((data_parts + 2,)),
            dma((data_parts + 2,)),
            dma((4, cols_n)),
            dma((n, 4, cols_n)),
            dma((4, cols_n - 1)),
            dma((n, 4, cols_n - 1)),
            dma((4,)),
            dma((2,)),
        ],
        compiler_params=pltpu.CompilerParams(
            collective_id=0, has_side_effects=True, vmem_limit_bytes=63 * 1024 * 1024
        ),
    )(
        hidden_in,
        logits_in,
        cotangent,
        row_ids,
        key_ids,
        small_in,
        w_qkv.astype(b16),
        w_out.astype(b16),
        w_in.astype(b16),
        w_back.astype(b16),
    )
    hidden_out, logits_out, grad_hidden, grad_scores = results[:4]
    small = results[8]
    vec_sum = lax.dynamic_slice_in_dim(small[: LAYERS * 8], ten * owned, owned, 1)
    bin_sum = small[LAYERS * 8 : LAYERS * 9]
    grads_all = results[4:8] + (vec_sum.reshape(LAYERS, 8, owned), bin_sum)
    masters = arrays[6:12]
    firsts = arrays[12:18]
    seconds = arrays[18:24]
    decays = (DECAY_RATE, DECAY_RATE, DECAY_RATE, DECAY_RATE, 0.0, 0.0)
    moved = []
    for master, gradient, first_prev, second_prev, decay_rate in zip(
        masters, grads_all, firsts, seconds, decays
    ):
        moment_one = BETA_ONE * first_prev + (1.0 - BETA_ONE) * gradient
        moment_two = BETA_TWO * second_prev + (1.0 - BETA_TWO) * gradient * gradient
        update = (
            moment_one / CORRECT_ONE / (jnp.sqrt(moment_two / CORRECT_TWO) + ADAM_EPS)
            + decay_rate * master
        )
        moved.append((moment_one, update))
    weight_sq = jnp.stack(
        [jnp.sum((master * master).reshape(LAYERS, -1), axis=1) for master in masters]
    )
    update_sq = jnp.stack(
        [jnp.sum((moved_one[1] * moved_one[1]).reshape(LAYERS, -1), axis=1) for moved_one in moved]
    )
    weight_tot, update_tot = lax.psum((weight_sq, update_sq), ("dp", "tensor"))
    trust_all = jnp.sqrt(weight_tot) / jnp.sqrt(update_tot)
    new_params = tuple(
        (
            master
            - LEARN_RATE
            * trust_all[group_at].reshape((LAYERS,) + (1,) * (master.ndim - 1))
            * moved_one[1]
            for group_at, (master, moved_one) in enumerate(zip(masters, moved))
        )
    )
    return (
        (hidden_out, logits_out[None], grad_hidden, grad_scores[None].astype(f32))
        + grads_all
        + new_params
        + tuple(moved_one[0] for moved_one in moved)
        + (trust_all.T,)
    )


def solution(mesh):
    return jax.shard_map(
        functools.partial(shards, parts=(mesh.shape["dp"], mesh.shape["tensor"])),
        mesh=mesh,
        in_specs=(
            P("dp", None),
            P("dp", "tensor", None, None),
            P(("dp", "tensor"), None),
            P("dp"),
            P("dp"),
            P("dp"),
            P(None, None, "dp", "tensor"),
            P(None, "tensor", "dp"),
            P(None, "dp", "tensor"),
            P(None, "tensor", "dp"),
            P(None, None, ("dp", "tensor")),
            P(None, ("dp", "tensor")),
            P(None, None, "dp", "tensor"),
            P(None, "tensor", "dp"),
            P(None, "dp", "tensor"),
            P(None, "tensor", "dp"),
            P(None, None, ("dp", "tensor")),
            P(None, ("dp", "tensor")),
            P(None, None, "dp", "tensor"),
            P(None, "tensor", "dp"),
            P(None, "dp", "tensor"),
            P(None, "tensor", "dp"),
            P(None, None, ("dp", "tensor")),
            P(None, ("dp", "tensor")),
        ),
        out_specs=(
            P(("dp", "tensor"), None),
            P("dp", "tensor", None, None),
            P(("dp", "tensor"), None),
            P("dp", "tensor", None, None),
            P(None, None, "dp", "tensor"),
            P(None, "tensor", "dp"),
            P(None, "dp", "tensor"),
            P(None, "tensor", "dp"),
            P(None, None, ("dp", "tensor")),
            P(None, ("dp", "tensor")),
            P(None, None, "dp", "tensor"),
            P(None, "tensor", "dp"),
            P(None, "dp", "tensor"),
            P(None, "tensor", "dp"),
            P(None, None, ("dp", "tensor")),
            P(None, ("dp", "tensor")),
            P(None, None, "dp", "tensor"),
            P(None, "tensor", "dp"),
            P(None, "dp", "tensor"),
            P(None, "tensor", "dp"),
            P(None, None, ("dp", "tensor")),
            P(None, ("dp", "tensor")),
            P(),
        ),
        check_vma=False,
    )
```

```python
import functools

import jax
import jax.numpy as jnp
from jax import lax
from jax.experimental import pallas as pl
from jax.experimental.pallas import tpu as pltpu
from jax.sharding import PartitionSpec as P

LAYERS = 2


NORM_EPS = 1e-05
ADAM_EPS = 1e-06
BETA_ONE = 0.9
BETA_TWO = 0.999
CORRECT_ONE = 1.0
CORRECT_TWO = 0.632304575228943
LEARN_RATE = 0.3
DECAY_RATE = 0.01
NEG_FILL = -1e30


def layer_norm(values, gain, shift):
    center = values - jnp.mean(values, axis=-1, keepdims=True)
    spread = jnp.mean(center * center, axis=-1, keepdims=True)
    return center * lax.rsqrt(spread + NORM_EPS) * gain + shift


def gelu_exact(values):
    return jax.nn.gelu(values, approximate=False)


def plain_shards(
    hidden_in,
    logits_in,
    cotangent,
    bucket_ids,
    seq_counts,
    key_mask,
    w_qkv,
    w_out,
    w_in,
    w_back,
    vectors,
    bias_in,
    m_qkv,
    m_out,
    m_in,
    m_back,
    m_vectors,
    m_bias,
    v_qkv,
    v_out,
    v_in,
    v_back,
    v_vectors,
    v_bias,
):
    tensor_parts = lax.axis_size("tensor")
    tensor_index = lax.axis_index("tensor")
    data_parts = lax.axis_size("dp")
    tokens_here = hidden_in.shape[0]
    share_rows = tokens_here // tensor_parts
    first_row = tensor_index * share_rows
    block_count = logits_in.shape[0]
    heads_here = logits_in.shape[1]
    block_len = logits_in.shape[2]
    model_width = hidden_in.shape[1]
    head_cols = w_qkv.shape[3]
    head_size = head_cols // heads_here
    hidden_cols = w_in.shape[2]
    score_scale = head_size ** (-0.5)
    bucket = bucket_ids[0]
    seq_span = jnp.where(
        bucket == 0, block_len // 4, jnp.where(bucket == 1, block_len // 2, block_len)
    )
    position = jnp.arange(tokens_here, dtype=jnp.int32)
    seq_flat = position // seq_span
    seq_of = seq_flat.reshape(block_count, block_len)
    live_keys = ((key_mask == 1) & (seq_flat < seq_counts[0])).reshape(block_count, block_len)
    allowed = (seq_of[:, :, None] == seq_of[:, None, :]) & live_keys[:, None, :]
    vec_all, bin_all = (
        lax.all_gather(vectors.astype(jnp.bfloat16), ("dp", "tensor"), axis=2, tiled=True),
        lax.all_gather(bias_in.astype(jnp.bfloat16), ("dp", "tensor"), axis=1, tiled=True),
    )
    vec_all = vec_all.astype(jnp.float32)
    bin_all = bin_all.astype(jnp.float32)

    def sum_forward(term_fn):
        return lax.psum_scatter(
            term_fn(jnp.int32(0), share_rows * lax.axis_size("tensor")).astype(jnp.bfloat16),
            "tensor",
            scatter_dimension=0,
            tiled=True,
        ).astype(jnp.float32)

    def sum_backward(term_fn):
        return lax.psum_scatter(
            term_fn(jnp.int32(0), share_rows * lax.axis_size("tensor")).astype(jnp.bfloat16),
            "tensor",
            scatter_dimension=0,
            tiled=True,
        ).astype(jnp.float32)

    def gather_rows(own_rows):
        return lax.all_gather(own_rows, "tensor", axis=0, tiled=True)

    def gather_grads(own_rows):
        return lax.all_gather(own_rows, "tensor", axis=0, tiled=True)

    def own_cols(vector):
        return lax.dynamic_slice_in_dim(vector, tensor_index * head_cols, head_cols)

    def place_cols(part_sum, total_len, offset):
        return lax.dynamic_update_slice(jnp.zeros((total_len,), jnp.float32), part_sum, (offset,))

    def blocked(matrix):
        return matrix.reshape(block_count, block_len, head_cols)

    def headed(matrix):
        return matrix.reshape(block_len, heads_here, head_size)

    def block_scores(query_b, keys_b, earlier_b):
        raw = jnp.einsum(
            "ihe,jhe->hij", headed(query_b), headed(keys_b), preferred_element_type=jnp.float32
        )
        return raw * score_scale + earlier_b.astype(jnp.float32)

    def attend_block(inputs):
        query_b, keys_b, values_b, earlier_b, allowed_b = inputs
        scores = block_scores(query_b, keys_b, earlier_b)
        row_top = jnp.max(jnp.where(allowed_b[None], scores, NEG_FILL), axis=-1, keepdims=True)
        unscaled = jnp.exp(jnp.where(allowed_b[None], scores - row_top, NEG_FILL))
        row_total = jnp.sum(unscaled, axis=-1, keepdims=True)
        row_total = jnp.where(row_total > 0.5, row_total, 1.0)
        probs_low = (unscaled / row_total).astype(jnp.bfloat16)
        mixed = jnp.einsum(
            "hij,jhe->ihe", probs_low, headed(values_b), preferred_element_type=jnp.float32
        )
        return (
            mixed.reshape(block_len, head_cols).astype(jnp.bfloat16),
            scores.astype(jnp.bfloat16),
            row_top,
            row_total,
        )

    def attend_back(inputs):
        query_b, keys_b, values_b, earlier_b, allowed_b, row_top, row_total, dmixed_b, dlater_b = (
            inputs
        )
        scores = block_scores(query_b, keys_b, earlier_b)
        unscaled = jnp.exp(jnp.where(allowed_b[None], scores - row_top, NEG_FILL))
        probs = unscaled / row_total
        probs_low = probs.astype(jnp.bfloat16)
        dmixed_heads = headed(dmixed_b)
        dvalues = jnp.einsum(
            "hij,ihe->jhe", probs_low, dmixed_heads, preferred_element_type=jnp.float32
        )
        dprobs = jnp.einsum(
            "ihe,jhe->hij", dmixed_heads, headed(values_b), preferred_element_type=jnp.float32
        )
        dlocal = probs * (dprobs - jnp.sum(probs * dprobs, axis=-1, keepdims=True))
        dscores = (dlocal + dlater_b.astype(jnp.float32)).astype(jnp.bfloat16)
        dquery = (
            jnp.einsum("hij,jhe->ihe", dscores, headed(keys_b), preferred_element_type=jnp.float32)
            * score_scale
        )
        dkeys = (
            jnp.einsum("hij,ihe->jhe", dscores, headed(query_b), preferred_element_type=jnp.float32)
            * score_scale
        )
        return (
            dquery.reshape(block_len, head_cols),
            dkeys.reshape(block_len, head_cols),
            dvalues.reshape(block_len, head_cols),
            dscores,
        )

    full_in = hidden_in
    own_in = lax.dynamic_slice_in_dim(hidden_in, first_row, share_rows, 0)
    earlier = logits_in
    records = []
    for layer_at in range(LAYERS):
        fetched = (
            lax.all_gather(w_qkv[layer_at].astype(jnp.bfloat16), "dp", axis=1, tiled=True),
            lax.all_gather(w_out[layer_at].astype(jnp.bfloat16), "dp", axis=1, tiled=True),
            lax.all_gather(w_in[layer_at].astype(jnp.bfloat16), "dp", axis=0, tiled=True),
            lax.all_gather(w_back[layer_at].astype(jnp.bfloat16), "dp", axis=1, tiled=True),
        )
        forward_wqkv, forward_wout, forward_win, forward_wback = fetched
        forward_vector = vec_all[layer_at]
        forward_query = (
            jnp.dot(full_in, forward_wqkv[0], preferred_element_type=jnp.float32)
            + own_cols(forward_vector[2])
        ).astype(jnp.bfloat16)
        forward_keys = jnp.dot(full_in, forward_wqkv[1], preferred_element_type=jnp.float32).astype(
            jnp.bfloat16
        )
        forward_values = (
            jnp.dot(full_in, forward_wqkv[2], preferred_element_type=jnp.float32)
            + own_cols(forward_vector[3])
        ).astype(jnp.bfloat16)
        forward_attn_out, stored, forward_row_top, forward_row_total = lax.map(
            attend_block,
            (
                blocked(forward_query),
                blocked(forward_keys),
                blocked(forward_values),
                earlier,
                allowed,
            ),
        )
        forward_attn_out = forward_attn_out.reshape(tokens_here, head_cols)

        def attn_term(begin_row, row_count):
            return jnp.dot(forward_attn_out, forward_wout, preferred_element_type=jnp.float32)

        forward_mid_pre = sum_forward(attn_term) + forward_vector[4] + own_in.astype(jnp.float32)
        mid_own = layer_norm(forward_mid_pre, forward_vector[0], forward_vector[5]).astype(
            jnp.bfloat16
        )
        forward_mid_full = gather_rows(mid_own)
        bias_here = lax.dynamic_slice_in_dim(
            bin_all[layer_at], tensor_index * hidden_cols, hidden_cols
        )
        forward_pre_act = (
            jnp.dot(forward_mid_full, forward_win, preferred_element_type=jnp.float32) + bias_here
        )
        forward_active = gelu_exact(forward_pre_act).astype(jnp.bfloat16)

        def ffn_term(begin_row, row_count):
            return jnp.dot(forward_active, forward_wback, preferred_element_type=jnp.float32)

        forward_out_pre = sum_forward(ffn_term) + forward_vector[6] + mid_own.astype(jnp.float32)
        out_own = layer_norm(forward_out_pre, forward_vector[1], forward_vector[7]).astype(
            jnp.bfloat16
        )
        forward_state = (
            forward_query,
            forward_keys,
            forward_values,
            forward_attn_out,
            forward_row_top,
            forward_row_total,
            forward_mid_pre,
            forward_mid_full,
            forward_pre_act,
            forward_out_pre,
        )
        out_own, stored, state = (out_own, stored, forward_state)
        records.append((full_in, earlier, fetched, state))
        earlier = stored
        own_in = out_own
        if layer_at + 1 < LAYERS:
            full_in = gather_rows(out_own)
    logits_out = earlier
    d_own = cotangent.astype(jnp.float32)
    d_later = jnp.zeros_like(logits_in)
    mat_grads = [None] * LAYERS
    vec_grads = [None] * LAYERS
    bin_grads = [None] * LAYERS
    for layer_at in reversed(range(LAYERS)):
        full_in, earlier, fetched, state = records[layer_at]
        wqkv = lax.all_gather(w_qkv[layer_at].astype(jnp.bfloat16), "dp", axis=1, tiled=True)
        wout = lax.all_gather(w_out[layer_at].astype(jnp.bfloat16), "dp", axis=1, tiled=True)
        win = lax.all_gather(w_in[layer_at].astype(jnp.bfloat16), "dp", axis=0, tiled=True)
        wback = lax.all_gather(w_back[layer_at].astype(jnp.bfloat16), "dp", axis=1, tiled=True)
        (
            query,
            keys,
            values,
            attn_out,
            backward_row_top,
            backward_row_total,
            mid_pre,
            mid_full,
            pre_act,
            out_pre,
        ) = state
        backward_vector = vec_all[layer_at]
        out_grad, gain_two, shift_two = jax.vjp(
            layer_norm, out_pre, backward_vector[1], backward_vector[7]
        )[1](d_own)
        d_ffn = gather_grads(out_grad.astype(jnp.bfloat16))
        active = gelu_exact(pre_act).astype(jnp.bfloat16)
        grad_back = jnp.einsum("tf,td->fd", active, d_ffn, preferred_element_type=jnp.float32)
        d_active = jnp.einsum("td,fd->tf", d_ffn, wback, preferred_element_type=jnp.float32)
        d_pre = jax.vjp(gelu_exact, pre_act)[1](d_active)[0].astype(jnp.bfloat16)
        grad_in = jnp.einsum("td,tf->df", mid_full, d_pre, preferred_element_type=jnp.float32)

        def mid_term(begin_row, row_count):
            return jnp.einsum("tf,df->td", d_pre, win, preferred_element_type=jnp.float32)

        mid_grad = sum_backward(mid_term) + out_grad
        attn_grad, gain_one, shift_one = jax.vjp(
            layer_norm, mid_pre, backward_vector[0], backward_vector[5]
        )[1](mid_grad)
        d_attn = gather_grads(attn_grad.astype(jnp.bfloat16))
        grad_out_proj = jnp.einsum(
            "tc,td->cd", attn_out, d_attn, preferred_element_type=jnp.float32
        )
        d_mixed = jnp.einsum("td,cd->tc", d_attn, wout, preferred_element_type=jnp.float32).astype(
            jnp.bfloat16
        )
        backward_dquery, backward_dkeys, backward_dvalues, backward_dscores = lax.map(
            attend_back,
            (
                blocked(query),
                blocked(keys),
                blocked(values),
                earlier,
                allowed,
                backward_row_top,
                backward_row_total,
                blocked(d_mixed),
                d_later,
            ),
        )
        backward_dquery = backward_dquery.reshape(tokens_here, head_cols).astype(jnp.bfloat16)
        backward_dkeys = backward_dkeys.reshape(tokens_here, head_cols).astype(jnp.bfloat16)
        backward_dvalues = backward_dvalues.reshape(tokens_here, head_cols).astype(jnp.bfloat16)
        grad_qkv = jnp.stack(
            [
                jnp.einsum(
                    "td,tc->dc", full_in, backward_dquery, preferred_element_type=jnp.float32
                ),
                jnp.einsum(
                    "td,tc->dc", full_in, backward_dkeys, preferred_element_type=jnp.float32
                ),
                jnp.einsum(
                    "td,tc->dc", full_in, backward_dvalues, preferred_element_type=jnp.float32
                ),
            ]
        )

        def input_term(begin_row, row_count):
            total_term = jnp.einsum(
                "tc,dc->td", backward_dquery, wqkv[0], preferred_element_type=jnp.float32
            )
            total_term = total_term + jnp.einsum(
                "tc,dc->td", backward_dkeys, wqkv[1], preferred_element_type=jnp.float32
            )
            return total_term + jnp.einsum(
                "tc,dc->td", backward_dvalues, wqkv[2], preferred_element_type=jnp.float32
            )

        in_grad = sum_backward(input_term) + attn_grad
        col_offset = tensor_index * head_cols
        vec_grad = jnp.stack(
            [
                gain_one,
                gain_two,
                place_cols(
                    jnp.sum(backward_dquery.astype(jnp.float32), axis=0), model_width, col_offset
                ),
                place_cols(
                    jnp.sum(backward_dvalues.astype(jnp.float32), axis=0), model_width, col_offset
                ),
                jnp.sum(attn_grad, axis=0),
                shift_one,
                jnp.sum(out_grad, axis=0),
                shift_two,
            ]
        )
        bin_grad = place_cols(
            jnp.sum(d_pre.astype(jnp.float32), axis=0),
            hidden_cols * tensor_parts,
            tensor_index * hidden_cols,
        )
        d_own, d_later, mats, vec_grad, bin_grad = (
            in_grad,
            backward_dscores,
            (grad_qkv, grad_out_proj, grad_in, grad_back),
            vec_grad,
            bin_grad,
        )
        totals = (
            lax.psum(mats[0].astype(jnp.bfloat16), "dp").astype(jnp.float32),
            lax.psum(mats[1].astype(jnp.bfloat16), "dp").astype(jnp.float32),
            lax.psum(mats[2].astype(jnp.bfloat16), "dp").astype(jnp.float32),
            lax.psum(mats[3].astype(jnp.bfloat16), "dp").astype(jnp.float32),
        )
        data_index = lax.axis_index("dp")
        mat_grads[layer_at] = tuple(
            (
                lax.dynamic_slice_in_dim(
                    whole,
                    data_index * (whole.shape[axis_at] // data_parts),
                    whole.shape[axis_at] // data_parts,
                    axis_at,
                )
                for whole, axis_at in zip(totals, (1, 1, 0, 1))
            )
        )
        vec_grads[layer_at] = vec_grad
        bin_grads[layer_at] = bin_grad
    grad_logits = d_later.astype(jnp.float32)
    vec_sum, bin_sum = (
        lax.psum_scatter(jnp.stack(vec_grads), ("dp", "tensor"), scatter_dimension=2, tiled=True),
        lax.psum_scatter(jnp.stack(bin_grads), ("dp", "tensor"), scatter_dimension=1, tiled=True),
    )
    grads_all = (
        jnp.stack([mat_grads[level_at][0] for level_at in range(LAYERS)]),
        jnp.stack([mat_grads[level_at][1] for level_at in range(LAYERS)]),
        jnp.stack([mat_grads[level_at][2] for level_at in range(LAYERS)]),
        jnp.stack([mat_grads[level_at][3] for level_at in range(LAYERS)]),
        vec_sum,
        bin_sum,
    )
    masters = (w_qkv, w_out, w_in, w_back, vectors, bias_in)
    firsts = (m_qkv, m_out, m_in, m_back, m_vectors, m_bias)
    seconds = (v_qkv, v_out, v_in, v_back, v_vectors, v_bias)
    decays = (DECAY_RATE, DECAY_RATE, DECAY_RATE, DECAY_RATE, 0.0, 0.0)
    moved = []
    for master, gradient, first_prev, second_prev, decay_rate in zip(
        masters, grads_all, firsts, seconds, decays
    ):
        moment_one = BETA_ONE * first_prev + (1.0 - BETA_ONE) * gradient
        moment_two = BETA_TWO * second_prev + (1.0 - BETA_TWO) * gradient * gradient
        update = (
            moment_one / CORRECT_ONE / (jnp.sqrt(moment_two / CORRECT_TWO) + ADAM_EPS)
            + decay_rate * master
        )
        moved.append((moment_one, update))
    weight_sq = jnp.stack(
        [jnp.sum((master * master).reshape(LAYERS, -1), axis=1) for master in masters]
    )
    update_sq = jnp.stack(
        [jnp.sum((moved_one[1] * moved_one[1]).reshape(LAYERS, -1), axis=1) for moved_one in moved]
    )
    weight_tot, update_tot = lax.psum((weight_sq, update_sq), ("dp", "tensor"))
    trust_all = jnp.sqrt(weight_tot) / jnp.sqrt(update_tot)
    new_params = tuple(
        (
            master
            - LEARN_RATE
            * trust_all[group_at].reshape((LAYERS,) + (1,) * (master.ndim - 1))
            * moved_one[1]
            for group_at, (master, moved_one) in enumerate(zip(masters, moved))
        )
    )
    return (
        own_in,
        logits_out,
        d_own,
        grad_logits,
        grads_all[0],
        grads_all[1],
        grads_all[2],
        grads_all[3],
        grads_all[4],
        grads_all[5],
        new_params[0],
        new_params[1],
        new_params[2],
        new_params[3],
        new_params[4],
        new_params[5],
        moved[0][0],
        moved[1][0],
        moved[2][0],
        moved[3][0],
        moved[4][0],
        moved[5][0],
        trust_all.T,
    )


MESH = pl.DeviceIdType.MESH
TILE = 256
LANES = 128
ROWS_MAT = 4
X_FIRST = 9
Z_AHEAD = 2
X_AHEAD = 3
SLOTS = ((1, 3), (2, 1), (2, 3), (3, 1), (3, 2), (4, 1), (5, 1))
BACK_SLOTS = (
    (-9, -9, 0, 1, 2, 3, 4, 5, 6),
    (-9, -5, -4, -2, 0, 0, 1, 2, 3),
    (4,),
)


def dot_nn(left, right):
    return lax.dot_general(
        left, right, (((1,), (0,)), ((), ())), preferred_element_type=jnp.float32
    )


def dot_nt(left, right):
    return lax.dot_general(
        left, right, (((1,), (1,)), ((), ())), preferred_element_type=jnp.float32
    )


def norm_parts(values):
    center = values - jnp.mean(values, axis=-1, keepdims=True)
    spread = jnp.mean(center * center, axis=-1, keepdims=True)
    return center, lax.rsqrt(spread + NORM_EPS)


def step_kernel(
    data_parts,
    hidden_in,
    logits_in,
    cotangent,
    key_ids,
    small_in,
    own_qkv,
    own_out,
    own_in,
    own_back,
    lw_qkv,
    lw_out,
    lw_in,
    lw_back,
    lm_qkv,
    lm_out,
    lm_in,
    lm_back,
    lv_qkv,
    lv_out,
    lv_in,
    lv_back,
    hidden_out,
    logits_out,
    grad_hidden,
    grad_scores,
    sum_qkv,
    sum_out,
    sum_in,
    sum_back,
    small_out,
    norm_out,
    w_q,
    w_o,
    w_i,
    w_b,
    scores,
    probs,
    h_full,
    m_full,
    active,
    attn,
    h_turn,
    m_turn,
    g_turn,
    o_turn,
    slope,
    qkv,
    x_own,
    y_own,
    d_qkv,
    d_keep,
    turn_v,
    turn_k,
    part,
    got_core,
    sum_chip,
    got_y,
    vec_got,
    vec_all,
    bin_all,
    small_acc,
    small_got,
    small_send,
    small_sum,
    pk_q,
    pk_o,
    pk_i,
    pk_b,
    rx_q,
    rx_o,
    rx_i,
    rx_b,
    rz_q,
    rz_o,
    rz_i,
    rz_b,
    fw_q,
    fw_o,
    fw_i,
    fw_b,
    fm_q,
    fm_o,
    fm_i,
    fm_b,
    fv_q,
    fv_o,
    fv_i,
    fv_b,
    norms,
    norm_send,
    norm_ten,
    norm_mid,
    norm_dp,
    load_sem,
    own_sem,
    zs_sem,
    zr_sem,
    xs_sem,
    xr_sem,
    core_s,
    core_r,
    ys_sem,
    yr_sem,
    gat_s,
    gat_r,
    vec_s,
    vec_r,
    sml_s,
    sml_r,
    gxs_sem,
    gxr_sem,
    gzs_sem,
    gzr_sem,
    fin_sem,
    out_sem,
    lamb_sem,
    ns_sem,
    nr_sem,
):
    dp = lax.axis_index("dp")
    ten = lax.axis_index("tensor")
    cols_n = data_parts // 2
    side = lax.rem(dp, 2)
    place = dp // 2
    row_y = ten // 2
    core = lax.rem(ten, 2)
    across = dp + 1 - 2 * side
    core_mate = ten + 1 - 2 * core
    y_mate = lax.rem(ten + 2, 4)
    width = hidden_in.shape[1]
    tokens = hidden_in.shape[0]
    share = tokens // 4
    half = share // 2
    head_cols = qkv.shape[3]
    hidden_cols = slope.shape[2]
    cut = width // data_parts
    tiles = width // TILE
    f32 = jnp.float32
    b16 = jnp.bfloat16

    def along(step):
        return lax.rem(place + step, cols_n) * 2 + side

    def mult(value, by):
        return pl.multiple_of(value, by)

    def rdma(src, dst, send, recv, to_dp, to_ten):
        return pltpu.make_async_remote_copy(
            src_ref=src,
            dst_ref=dst,
            send_sem=send,
            recv_sem=recv,
            device_id=(to_dp, to_ten),
            device_id_type=MESH,
        )

    def region(kind, layer, dev):
        at = pl.ds(mult(dev * cut, cut), cut)
        if kind == 0:
            return w_q.at[layer, :, at, :]
        if kind == 1:
            return w_o.at[layer, :, at]
        if kind == 2:
            return w_i.at[layer, at, :]
        return w_b.at[layer, :, at]

    owns = (own_qkv, own_out, own_in, own_back)

    load_h = pltpu.make_async_copy(hidden_in, h_full, load_sem.at[0])
    load_s = pltpu.make_async_copy(logits_in.at[0], scores, load_sem.at[1])
    load_h.start()
    load_s.start()
    own_loads = []
    for layer in range(LAYERS):
        for kind in range(ROWS_MAT):
            copy = pltpu.make_async_copy(
                owns[kind].at[layer], region(kind, layer, dp), own_sem.at[layer, kind]
            )
            copy.start()
            own_loads.append(copy)

    barrier = pltpu.get_barrier_semaphore()

    def greet(step, carry):
        pl.semaphore_signal(
            barrier, inc=1, device_id=(lax.rem(dp + step, data_parts), ten), device_id_type=MESH
        )
        return carry

    lax.fori_loop(1, data_parts, greet, 0)
    for other in range(1, 4):
        pl.semaphore_signal(
            barrier, inc=1, device_id=(dp, lax.rem(ten + other, 4)), device_id_type=MESH
        )
    pl.semaphore_wait(barrier, data_parts + 2)

    vec_got[ten, dp] = small_in[0].astype(b16)

    def vec_one(step):
        return rdma(
            vec_got.at[ten, dp],
            vec_got.at[ten, dp],
            vec_s.at[step - 1],
            vec_r.at[step - 1],
            lax.rem(dp + step, data_parts),
            ten,
        )

    def vec_go(step, carry):
        vec_one(step).start()
        return carry

    lax.fori_loop(1, data_parts, vec_go, 0)

    def w_x(kind, layer, from_place, col, own=False):
        dst = region(kind, layer, from_place * 2 + col)
        return rdma(
            owns[kind].at[layer] if own else dst,
            dst,
            xs_sem.at[layer, kind, from_place],
            xr_sem.at[layer, kind, from_place],
            across,
            ten,
        )

    def w_z(kind, layer, from_place, col, way, own=False):
        dst = region(kind, layer, from_place * 2 + col)
        which = lax.rem(col + side, 2)
        return rdma(
            owns[kind].at[layer] if own else dst,
            dst,
            zs_sem.at[layer, kind, from_place, which, (way + 1) // 2],
            zr_sem.at[layer, kind, from_place, which],
            dp + 2 * way,
            ten,
        )

    can_go = {1: place < cols_n - 1, -1: place > 0}

    def w_both_ways(kind, layer, col, own=False):
        for way in (1, -1):

            @pl.when(can_go[way])
            def _():
                w_z(kind, layer, place, col, way, own).start()

    def w_event(kind, layer, hop):
        if hop == 0:
            w_x(kind, layer, place, 1 - side).wait_recv()
            w_both_ways(kind, layer, 1 - side)
            return
        for way in (1, -1):
            came = place - hop * way

            @pl.when(came >= 0 if way == 1 else came < cols_n)
            def _():
                for col in (side, 1 - side) if kind == X_FIRST else (side,):
                    w_z(kind, layer, came, col, way).wait_recv()

                    @pl.when(can_go[way])
                    def _():
                        w_z(kind, layer, came, col, way).start()

                    if kind != X_FIRST:
                        w_x(kind, layer, came, side).start()

    order = [(kind, layer) for layer in range(LAYERS) for kind in range(ROWS_MAT)]

    def w_own_z(index):
        if index < len(order):
            w_both_ways(*order[index], side, True)

    def w_own_x(index):
        if index < len(order):
            w_x(*order[index], place, side, True).start()

    for index in range(Z_AHEAD):
        w_own_z(index)
    for index in range(X_AHEAD):
        w_own_x(index)
    events = [
        (index, hop)
        for index in range(len(order))
        for hop in range(0 if order[index][0] == X_FIRST else 1, cols_n)
    ]
    passed = [0]

    def pass_on(layer_at, kind_at, hop_at):
        goal = (layer_at * ROWS_MAT + kind_at, hop_at)
        while passed[0] < len(events) and events[passed[0]] <= goal:
            index, hop = events[passed[0]]
            w_event(*order[index], hop)
            if hop == cols_n - 1:
                w_own_z(index + Z_AHEAD)
                w_own_x(index + X_AHEAD)
            passed[0] += 1

    def have(layer, kind):
        pass_on(layer, kind, cols_n)
        if kind != X_FIRST:
            for from_place in range(cols_n):
                w_x(kind, layer, from_place, 1 - side).wait_recv()

    def w_finish():
        for kind, layer in order:
            for from_place in range(cols_n):
                if kind != X_FIRST:
                    w_x(kind, layer, from_place, side).wait_send()
                for col in (side, 1 - side) if kind == X_FIRST else (side,):

                    @pl.when(can_go[1] & (from_place <= place))
                    def _():
                        w_z(kind, layer, from_place, col, 1).wait_send()

                    @pl.when(can_go[-1] & (from_place >= place))
                    def _():
                        w_z(kind, layer, from_place, col, -1).wait_send()

            if kind == X_FIRST:
                w_x(kind, layer, place, side).wait_send()

    def vec_wait(step, carry):
        vec_one(step).wait_send()
        vec_one(step).wait_recv()
        return carry

    lax.fori_loop(1, data_parts, vec_wait, 0)

    def vec_two(step):
        return rdma(
            vec_got.at[ten],
            vec_got.at[ten],
            vec_s.at[data_parts - 2 + step],
            vec_r.at[data_parts - 2 + step],
            dp,
            lax.rem(ten + step, 4),
        )

    for step in range(1, 4):
        vec_two(step).start()
    for step in range(1, 4):
        vec_two(step).wait_send()
        vec_two(step).wait_recv()
    for dev in range(data_parts):
        total = vec_got[0, dev].astype(f32)
        for other in range(1, 4):
            total = total + vec_got[other, dev].astype(f32)
        vec_all[:, dev * LANES : (dev + 1) * LANES] = total[0 : LAYERS * 8]
    for piece in range(hidden_cols // LANES):
        got = vec_got[piece % 4, ten * 2 + piece // 4].astype(f32)
        bin_all[:, piece * LANES : (piece + 1) * LANES] = got[LAYERS * 8 : LAYERS * 8 + 8]

    def vec_row(layer, row):
        return vec_all[layer * 8 + row : layer * 8 + row + 1, :]

    def block_rows(which_y, which_core):
        return pl.ds(mult((which_y * 2 + which_core) * share, share), share)

    far_block = block_rows(1 - row_y, 1 - core)
    mate_block = block_rows(row_y, 1 - core)
    over_block = block_rows(1 - row_y, core)
    own_block = block_rows(row_y, core)

    def tile_cols(tile):
        return pl.ds(mult(tile * TILE, TILE), TILE)

    def send_core(tile, which):
        rows = far_block if which == 0 else mate_block
        return rdma(
            part.at[rows, tile_cols(tile)],
            got_core.at[which, :, tile_cols(tile)],
            core_s.at[tile, which],
            core_r.at[tile, which],
            dp,
            core_mate,
        )

    def send_y(tile):
        return rdma(
            sum_chip.at[:, tile_cols(tile)],
            got_y.at[:, tile_cols(tile)],
            ys_sem.at[tile],
            yr_sem.at[tile],
            dp,
            y_mate,
        )

    def add_core(tile):
        send_core(tile, 0).wait_recv()
        at = tile_cols(tile)
        sum_chip[:, at] = (
            part[over_block, at].astype(f32) + got_core[0, :, at].astype(f32)
        ).astype(b16)
        send_y(tile).start()

    def sum_start(tile_fn):
        def one(tile, carry):
            part[:, tile_cols(tile)] = tile_fn(tile).astype(b16)
            send_core(tile, 0).start()
            send_core(tile, 1).start()

            @pl.when(tile > 0)
            def _():
                add_core(tile - 1)

            return carry

        lax.fori_loop(0, tiles, one, 0)
        add_core(tiles - 1)

    def sum_end():
        for tile in range(tiles):
            send_core(tile, 1).wait_recv()
            send_y(tile).wait_recv()
        for tile in range(tiles):
            send_core(tile, 0).wait_send()
            send_core(tile, 1).wait_send()
            send_y(tile).wait_send()

    def sum_rows(which):
        at = pl.ds(which * half, half)
        mine = pl.ds(mult(ten * share + which * half, half), half)
        return (
            part[mine, :].astype(f32) + got_core[1, at, :].astype(f32) + got_y[at, :].astype(f32)
        )

    def gat_copy(buf, which, kind):
        if kind == 2:
            rows = pl.ds(mult(y_mate * share + which * half, half), half)
        else:
            rows = pl.ds(mult(ten * share + which * half, half), half)
        return rdma(
            buf.at[rows],
            buf.at[rows],
            gat_s.at[which, kind],
            gat_r.at[which, kind],
            dp,
            y_mate if kind == 1 else core_mate,
        )

    def gat_start(buf, which):
        gat_copy(buf, which, 1).start()
        gat_copy(buf, which, 0).start()

    def gat_end(buf):
        for which in range(2):
            gat_copy(buf, which, 1).wait_recv()
            gat_copy(buf, which, 2).start()
        for which in range(2):
            gat_copy(buf, which, 0).wait_recv()
            gat_copy(buf, which, 2).wait_recv()
        for which in range(2):
            for kind in range(3):
                gat_copy(buf, which, kind).wait_send()

    def own_rows(which):
        return pl.ds(mult(ten * share + which * half, half), half)

    def turn(src, dst, layer):
        def one(at, carry):
            dst[layer, tile_cols(at), :] = src[:, tile_cols(at)].T
            return carry

        lax.fori_loop(0, src.shape[1] // TILE, one, 0)

    lane = lax.broadcasted_iota(jnp.int32, (1, LANES), 1)
    low_lanes = jnp.where(lane < 64, 1.0, 0.0).astype(b16)
    high_lanes = jnp.where(lane < 64, 0.0, 1.0).astype(b16)
    lane_masks = (low_lanes, high_lanes)
    scale = 0.125
    score_rows = 256
    pairs = head_cols // LANES

    def pair_cols(pair):
        return slice(pair * LANES, (pair + 1) * LANES)

    def attend(layer, pair):
        def one(step, carry):
            rows = pl.ds(mult(step * score_rows, score_rows), score_rows)
            at = slice(pair * LANES, (pair + 1) * LANES)
            queries = qkv[layer, 0, rows, at]
            keys = qkv[layer, 1, :, at]
            values = qkv[layer, 2, :, at]
            row = lax.broadcasted_iota(jnp.int32, (score_rows, 1), 0) + step * score_rows
            allowed = jnp.floor(row.astype(f32) * key_ids[8:9, 0:1]) == key_ids[0:1, :]
            mixed = jnp.zeros((score_rows, LANES), f32)
            for head in range(2):
                raw = dot_nt(queries, keys * lane_masks[head])
                full = raw * scale + scores[pair * 2 + head, rows, :].astype(f32)
                scores[pair * 2 + head, rows, :] = full.astype(b16)
                top = jnp.max(jnp.where(allowed, full, NEG_FILL), axis=-1, keepdims=True)
                weight = jnp.exp(jnp.where(allowed, full - top, NEG_FILL))
                total = jnp.sum(weight, axis=-1, keepdims=True)
                total = jnp.where(total > 0.5, total, 1.0)
                low = (weight * (1.0 / total)).astype(b16)
                probs[layer, pair * 2 + head, rows, :] = low
                mixed = mixed + dot_nn(low, values * lane_masks[head])
            attn[rows, at] = mixed.astype(b16)
            return carry

        lax.fori_loop(0, tokens // score_rows, one, 0)

    def attend_back(layer, first, pairs_of):
        def pair_one(pair, carry):
            at = pair_cols(pair)
            turn_v[...] = jnp.zeros_like(turn_v)
            turn_k[...] = jnp.zeros_like(turn_k)

            def one(step, inner):
                rows = pl.ds(mult(step * score_rows, score_rows), score_rows)
                queries = qkv[layer, 0, rows, at]
                keys = qkv[layer, 1, :, at]
                values = qkv[layer, 2, :, at]
                grads = attn[rows, at]
                turned_q = queries.T
                turned_g = grads.T
                d_query = jnp.zeros((score_rows, LANES), f32)
                for head in range(2):
                    low = probs[layer, pair * 2 + head, rows, :]
                    prob = low.astype(f32)
                    d_prob = dot_nt(grads, values * lane_masks[head])
                    inner_sum = jnp.sum(prob * d_prob, axis=-1, keepdims=True)
                    d_score = prob * (d_prob - inner_sum)
                    if not first:
                        d_score = d_score + scores[pair * 2 + head, rows, :].astype(f32)
                    d_low = d_score.astype(b16)
                    scores[pair * 2 + head, rows, :] = d_low
                    d_query = d_query + dot_nn(d_low, keys * lane_masks[head])
                    part_rows = slice(head * 64, head * 64 + 64)
                    turn_v[part_rows, :] += dot_nn(turned_g[part_rows, :], low)
                    turn_k[part_rows, :] += dot_nn(turned_q[part_rows, :], d_low)
                d_qkv[0, rows, at] = (d_query * scale).astype(b16)
                return inner

            lax.fori_loop(0, tokens // score_rows, one, 0)
            d_qkv[1, :, at] = (turn_k[...] * scale).T.astype(b16)
            d_qkv[2, :, at] = turn_v[...].T.astype(b16)
            return carry

        for pair in pairs_of:
            pair_one(pair, 0)

    own_cols = pl.ds(mult(ten * head_cols, head_cols), head_cols)
    small_acc[...] = jnp.zeros_like(small_acc)
    load_h.wait()
    for copy in own_loads:
        copy.wait()
    load_s.wait()
    for layer in range(LAYERS):
        have(layer, 0)
        for which in range(3):
            product = dot_nn(h_full[...], w_q[layer, which])
            if which == 0:
                product = product + vec_all[layer * 8 + 2 : layer * 8 + 3, own_cols]
            if which == 2:
                product = product + vec_all[layer * 8 + 3 : layer * 8 + 4, own_cols]
            qkv[layer, which] = product.astype(b16)
        pass_on(layer, *SLOTS[0])
        attend(layer, 0)
        pass_on(layer, *SLOTS[1])
        attend(layer, 1)
        have(layer, 1)
        sum_start(lambda tile: dot_nn(attn[...], w_o[layer, :, tile_cols(tile)]))
        turn(attn, o_turn, layer)
        turn(h_full, h_turn, layer)
        pass_on(layer, *SLOTS[2])
        sum_end()
        for which in range(2):
            at = pl.ds(which * half, half)
            mid = sum_rows(which) + vec_row(layer, 4) + h_full[own_rows(which), :].astype(f32)
            x_own[layer, at, :] = mid
            center, rate = norm_parts(mid)
            m_full[own_rows(which), :] = (
                center * rate * vec_row(layer, 0) + vec_row(layer, 5)
            ).astype(b16)
            gat_start(m_full, which)
        pass_on(layer, *SLOTS[3])
        gat_end(m_full)

        def ffn_tile(tile, carry):
            at = tile_cols(tile)
            pre = dot_nn(m_full[...], w_i[layer, :, at]) + bin_all[layer : layer + 1, at]
            cumul = 0.5 * (1.0 + lax.erf(pre * 0.7071067811865476))
            dens = jnp.exp(-0.5 * pre * pre) * 0.3989422804014327
            active[:, at] = (pre * cumul).astype(b16)
            slope[layer, :, at] = (cumul + pre * dens).astype(b16)
            return carry

        have(layer, 2)
        pass_on(layer, *SLOTS[4])
        lax.fori_loop(0, hidden_cols // TILE, ffn_tile, 0)
        turn(m_full, m_turn, layer)
        have(layer, 3)
        sum_start(lambda tile: dot_nn(active[...], w_b[layer, :, tile_cols(tile)]))
        turn(active, g_turn, layer)
        pass_on(layer, *SLOTS[5])
        sum_end()
        for which in range(2):
            at = pl.ds(which * half, half)
            late = sum_rows(which) + vec_row(layer, 6) + m_full[own_rows(which), :].astype(f32)
            y_own[layer, at, :] = late
            center, rate = norm_parts(late)
            result = (center * rate * vec_row(layer, 1) + vec_row(layer, 7)).astype(b16)
            h_full[own_rows(which), :] = result
            if layer + 1 < LAYERS:
                gat_start(h_full, which)
        if layer + 1 < LAYERS:
            pass_on(layer, *SLOTS[6])
            gat_end(h_full)

    out_logits = pltpu.make_async_copy(scores, logits_out, out_sem.at[0])
    out_logits.start()
    all_own = pl.ds(mult(ten * share, share), share)
    out_hidden = pltpu.make_async_copy(h_full.at[all_own], hidden_out, out_sem.at[2])
    out_hidden.start()
    load_c = pltpu.make_async_copy(cotangent, sum_chip, out_sem.at[3])
    load_c.start()
    w_finish()

    packs = (pk_q, pk_o, pk_i, pk_b)
    got_x = (rx_q, rx_o, rx_i, rx_b)
    got_z = (rz_q, rz_o, rz_i, rz_b)
    sums = (sum_qkv, sum_out, sum_in, sum_back)

    def g_x(kind, layer, at):
        return rdma(
            packs[kind].at[at, 1 - side],
            got_x[kind].at[layer, at],
            gxs_sem.at[kind, at],
            gxr_sem.at[layer, kind, at],
            across,
            ten,
        )

    def g_z(kind, layer, step):
        to = lax.rem(place + step, cols_n)
        return rdma(
            packs[kind].at[to, side],
            got_z[kind].at[layer, step - 1],
            gzs_sem.at[kind, step - 1],
            gzr_sem.at[layer, kind, step - 1],
            to * 2 + side,
            ten,
        )

    def g_free(kind, layer):
        add_upto(layer, (3 - kind) * cols_n + cols_n - 1)
        for at in range(cols_n):
            g_x(kind, layer, at).wait_send()
        for step in range(1, cols_n):
            g_z(kind, layer, step).wait_send()

    def chunks_of(kind):
        if kind == 0:
            return [(which,) for which in range(3)]
        if kind == 3:
            return [(pl.ds(piece * 256, 256),) for piece in range(hidden_cols // 256)]
        return [()]

    g_order = [
        (kind, layer, turn_at)
        for layer in reversed(range(LAYERS))
        for kind in (3, 2, 1, 0)
        for turn_at in range(cols_n)
    ]
    added = [0]

    def turn_of(turn_at):
        return lax.rem(place + 1 + turn_at, cols_n)

    def add_upto(layer_at, index):
        index = (LAYERS - 1 - layer_at) * 4 * cols_n + index
        while added[0] <= min(index, len(g_order) - 1):
            kind, layer, turn_at = g_order[added[0]]
            to = turn_of(turn_at)
            g_x(kind, layer, to).wait_recv()
            for piece in chunks_of(kind):
                ours = (to, side) + piece
                theirs = (layer, to) + piece
                packs[kind][ours] = (
                    packs[kind][ours].astype(f32) + got_x[kind][theirs].astype(f32)
                ).astype(b16)
            if turn_at + 1 < cols_n:
                g_z(kind, layer, turn_at + 1).start()
            added[0] += 1

    masters = (
        (lw_qkv, lw_out, lw_in, lw_back),
        (lm_qkv, lm_out, lm_in, lm_back),
        (lv_qkv, lv_out, lv_in, lv_back),
    )
    held = ((fw_q, fw_o, fw_i, fw_b), (fm_q, fm_o, fm_i, fm_b), (fv_q, fv_o, fv_i, fv_b))

    def lamb_load(kind, layer, which):
        return pltpu.make_async_copy(
            masters[which][kind].at[layer], held[which][kind], lamb_sem.at[which, kind]
        )

    def lamb_update(weight, first, second, gradient, decay):
        moment_one = BETA_ONE * first + (1.0 - BETA_ONE) * gradient
        moment_two = BETA_TWO * second + (1.0 - BETA_TWO) * gradient * gradient
        return (
            moment_one / CORRECT_ONE / (jnp.sqrt(moment_two / CORRECT_TWO) + ADAM_EPS)
            + decay * weight
        )

    def note_norm(row, values):
        norms[row : row + 1, 0 : values.shape[-1]] += jnp.sum(
            values * values, axis=0, keepdims=True
        )

    def g_end(kind, layer):
        add_upto(layer, (3 - kind) * cols_n + cols_n - 1)
        for step in range(1, cols_n):
            g_z(kind, layer, step).wait_recv()
        for which in range(3):
            lamb_load(kind, layer, which).wait()
        for piece in chunks_of(kind):
            total = packs[kind][(place, side) + piece].astype(f32)
            for step in range(1, cols_n):
                total = total + got_z[kind][(layer, step - 1) + piece].astype(f32)
            here = piece if piece else (slice(None),)
            weight = held[0][kind][here]
            step_by = lamb_update(
                weight, held[1][kind][here], held[2][kind][here], total, DECAY_RATE
            )
            held[1][kind][here] = total
            note_norm((layer * 4 + kind) * 2, weight)
            note_norm((layer * 4 + kind) * 2 + 1, step_by)
        fin_copy(kind, layer).start()
        if layer:
            for which in (0, 2):
                lamb_load(kind, layer - 1, which).start()

    def lamb_more(kind, layer):
        if layer + 1 < LAYERS:
            fin_copy(kind, layer + 1).wait()
            lamb_load(kind, layer, 1).start()

    def fin_copy(kind, layer):
        return pltpu.make_async_copy(held[1][kind], sums[kind].at[layer], fin_sem.at[kind])

    def pair_rows(at):
        return pl.ds(mult(at * 2 * cut, 2 * cut), 2 * cut)

    def grad_back(layer):
        def one(turn_at, carry):
            at = turn_of(turn_at)
            for piece in range(hidden_cols // 512):
                rows = slice(piece * 512, (piece + 1) * 512)
                value = dot_nn(g_turn[layer, rows, :], m_full[:, pair_rows(at)]).astype(b16)
                pk_b[at, 0, rows, :] = value[:, :cut]
                pk_b[at, 1, rows, :] = value[:, cut:]
            g_x(3, layer, at).start()
            return carry

        lax.fori_loop(0, cols_n, one, 0)

    def grad_in(layer):
        def one(turn_at, carry):
            at = turn_of(turn_at)
            for piece in range(hidden_cols // 512):
                cols = slice(piece * 512, (piece + 1) * 512)
                value = dot_nn(m_turn[layer, pair_rows(at), :], active[:, cols]).astype(b16)
                pk_i[at, 0, :, cols] = value[:cut]
                pk_i[at, 1, :, cols] = value[cut:]
            g_x(2, layer, at).start()
            return carry

        lax.fori_loop(0, cols_n, one, 0)

    def grad_out(layer):
        def one(turn_at, carry):
            at = turn_of(turn_at)
            value = dot_nn(o_turn[layer], h_full[:, pair_rows(at)]).astype(b16)
            pk_o[at, 0] = value[:, :cut]
            pk_o[at, 1] = value[:, cut:]
            g_x(1, layer, at).start()
            return carry

        lax.fori_loop(0, cols_n, one, 0)

    def grad_qkv(layer):
        def one(turn_at, carry):
            at = turn_of(turn_at)
            for which in range(3):
                value = dot_nn(h_turn[layer, pair_rows(at), :], d_qkv[which]).astype(b16)
                pk_q[at, 0, which] = value[:cut]
                pk_q[at, 1, which] = value[cut:]
            g_x(0, layer, at).start()
            return carry

        lax.fori_loop(0, cols_n, one, 0)

    def norm_back(kept, upstream, gain):
        center, rate = norm_parts(kept)
        unit = center * rate
        scaled = upstream * gain
        down = rate * (
            scaled
            - jnp.mean(scaled, axis=-1, keepdims=True)
            - unit * jnp.mean(scaled * unit, axis=-1, keepdims=True)
        )
        return down, unit

    def note(row, values):
        small_acc[row : row + 1, :] += jnp.sum(values, axis=0, keepdims=True)

    norms[...] = jnp.zeros_like(norms)
    for kind in range(ROWS_MAT):
        for which in range(3):
            lamb_load(kind, LAYERS - 1, which).start()
    load_c.wait()
    for layer in reversed(range(LAYERS)):
        last = layer + 1 == LAYERS
        base = layer * 8
        for which in range(2):
            at = pl.ds(which * half, half)
            upstream = sum_chip[at, :].astype(f32) if last else grad_hidden[at, :]
            down, unit = norm_back(y_own[layer, at, :], upstream, vec_row(layer, 1))
            note(base + 1, upstream * unit)
            note(base + 7, upstream)
            note(base + 6, down)
            d_keep[at, :] = down
            m_full[own_rows(which), :] = down.astype(b16)
            gat_start(m_full, which)
        marks = BACK_SLOTS[0 if last else 1]
        add_upto(layer, marks[0])
        gat_end(m_full)
        if not last:
            g_free(3, layer + 1)
            g_end(3, layer + 1)
        grad_back(layer)
        lamb_more(3, layer)
        add_upto(layer, marks[1])

        def slope_tile(tile, carry):
            at = tile_cols(tile)
            d_active = dot_nt(m_full[...], w_b[layer, at, :])
            d_pre = (d_active * slope[layer, :, at].astype(f32)).astype(b16)
            active[:, at] = d_pre
            small_acc[LAYERS * 8 + layer : LAYERS * 8 + layer + 1, at] = jnp.sum(
                d_pre.astype(f32), axis=0, keepdims=True
            )
            return carry

        lax.fori_loop(0, hidden_cols // TILE, slope_tile, 0)
        sum_start(lambda tile: dot_nt(active[...], w_i[layer, tile_cols(tile), :]))
        add_upto(layer, marks[2])
        if not last:
            g_free(2, layer + 1)
            g_end(2, layer + 1)
        grad_in(layer)
        lamb_more(2, layer)
        add_upto(layer, marks[3])
        sum_end()
        if last:
            out_hidden.wait()
        for which in range(2):
            at = pl.ds(which * half, half)
            upstream = sum_rows(which) + d_keep[at, :]
            down, unit = norm_back(x_own[layer, at, :], upstream, vec_row(layer, 0))
            note(base + 0, upstream * unit)
            note(base + 5, upstream)
            note(base + 4, down)
            d_keep[at, :] = down
            h_full[own_rows(which), :] = down.astype(b16)
            gat_start(h_full, which)
        add_upto(layer, marks[4])
        gat_end(h_full)
        if not last:
            g_free(1, layer + 1)
            g_end(1, layer + 1)
        attn[...] = dot_nt(h_full[...], w_o[layer]).astype(b16)
        grad_out(layer)
        lamb_more(1, layer)
        if last:
            out_logits.wait()
        add_upto(layer, marks[5])
        attend_back(layer, last, (0,))
        add_upto(layer, marks[6])
        attend_back(layer, last, (1,))
        add_upto(layer, marks[7])
        small_acc[base + 2 : base + 3, own_cols] = jnp.sum(
            d_qkv[0].astype(f32), axis=0, keepdims=True
        )
        small_acc[base + 3 : base + 4, own_cols] = jnp.sum(
            d_qkv[2].astype(f32), axis=0, keepdims=True
        )

        def input_tile(tile):
            rows = tile_cols(tile)
            total = dot_nt(d_qkv[0], w_q[layer, 0, rows, :])
            total = total + dot_nt(d_qkv[1], w_q[layer, 1, rows, :])
            return total + dot_nt(d_qkv[2], w_q[layer, 2, rows, :])

        sum_start(input_tile)
        if not last:
            g_free(0, layer + 1)
            g_end(0, layer + 1)
        grad_qkv(layer)
        lamb_more(0, layer)
        add_upto(layer, marks[8])
        sum_end()
        for which in range(2):
            at = pl.ds(which * half, half)
            result = sum_rows(which) + d_keep[at, :]
            grad_hidden[at, :] = result

    out_scores = pltpu.make_async_copy(scores, grad_scores, out_sem.at[1])
    out_scores.start()

    small_got[ten] = small_acc[...]

    def small_one(step):
        return rdma(
            small_acc,
            small_got.at[ten],
            sml_s.at[step - 1],
            sml_r.at[step - 1],
            dp,
            lax.rem(ten + step, 4),
        )

    for step in range(1, 4):
        small_one(step).start()
    add_upto(0, BACK_SLOTS[2][0])
    for step in range(1, 4):
        small_one(step).wait_recv()
    mat_rows = LAYERS * 8
    for dev in range(data_parts):
        cols = slice(dev * LANES, (dev + 1) * LANES)
        total = small_got[0, 0:mat_rows, cols]
        for other in range(1, 4):
            total = total + small_got[other, 0:mat_rows, cols]
        small_send[dev, 0:mat_rows, :] = total
        from_cols = pl.ds(mult(((dev % 2) * 4 + ten) * LANES, LANES), LANES)
        small_send[dev, mat_rows : mat_rows + 8, :] = small_got[
            dev // 2, mat_rows : mat_rows + 8, from_cols
        ]

    def small_two(step):
        to = lax.rem(dp + step, data_parts)
        return rdma(
            small_send.at[to],
            small_sum.at[step - 1],
            sml_s.at[2 + step],
            sml_r.at[2 + step],
            to,
            ten,
        )

    def small_go(step, carry):
        small_two(step).start()
        return carry

    lax.fori_loop(1, data_parts, small_go, 0)
    g_end(3, 0)
    g_end(2, 0)
    g_end(1, 0)
    small_out[...] = small_send[dp]

    def small_wait(step, carry):
        small_two(step).wait_recv()
        small_two(step).wait_send()
        small_out[...] += small_sum[step - 1]
        return carry

    lax.fori_loop(1, data_parts, small_wait, 0)
    for step in range(1, 4):
        small_one(step).wait_send()
    g_end(0, 0)

    row_at = lax.broadcasted_iota(jnp.int32, (24, LANES), 0)
    lane_at = lax.broadcasted_iota(jnp.int32, (24, LANES), 1)
    in_share = (row_at >= mat_rows) | (lane_at // (width // data_parts // 4) == ten)
    small_grad = jnp.where(in_share & (row_at < mat_rows + LAYERS), small_out[...], 0.0)
    small_step = lamb_update(small_in[0, 0:24], small_in[1, 0:24], small_in[2, 0:24], small_grad, 0.0)
    norm_send[0:mat_rows, :] = jnp.broadcast_to(
        jnp.sum(norms[...], axis=-1, keepdims=True), (mat_rows, LANES)
    )
    for layer in range(LAYERS):
        for group, rows in enumerate(
            (slice(layer * 8, layer * 8 + 8), slice(mat_rows + layer, mat_rows + layer + 1))
        ):
            for which, values in enumerate((small_in[0, rows], small_step[rows])):
                total = jnp.sum(
                    jnp.sum(values * values, axis=0, keepdims=True), axis=1, keepdims=True
                )
                row = mat_rows + (layer * 2 + group) * 2 + which
                norm_send[row : row + 1, :] = jnp.broadcast_to(total, (1, LANES))

    def norm_one(step):
        return rdma(
            norm_send,
            norm_ten.at[ten],
            ns_sem.at[step - 1],
            nr_sem.at[step - 1],
            dp,
            lax.rem(ten + step, 4),
        )

    def norm_two(step):
        return rdma(
            norm_mid,
            norm_dp.at[dp],
            ns_sem.at[2 + step],
            nr_sem.at[2 + step],
            lax.rem(dp + step, data_parts),
            ten,
        )

    norm_ten[ten] = norm_send[...]
    for step in range(1, 4):
        norm_one(step).start()
    for step in range(1, 4):
        norm_one(step).wait_recv()
    total = norm_ten[0]
    for other in range(1, 4):
        total = total + norm_ten[other]
    norm_mid[...] = total
    norm_dp[dp] = total
    for step in range(1, data_parts):
        norm_two(step).start()
    for kind in range(ROWS_MAT):
        g_free(kind, 0)
        fin_copy(kind, 0).wait()
    out_scores.wait()
    for step in range(1, 4):
        norm_one(step).wait_send()
    for step in range(1, data_parts):
        norm_two(step).wait_recv()
    total = norm_dp[0]
    for other in range(1, data_parts):
        total = total + norm_dp[other]
    norm_out[...] = total
    for step in range(1, data_parts):
        norm_two(step).wait_send()


def fits(parts, head_cols, hidden_cols, heads_here, tokens, width, blocks):
    data_parts, tensor_parts = parts
    return (
        tensor_parts == 4
        and data_parts % 2 == 0
        and data_parts > 2
        and width // data_parts == LANES
        and head_cols // heads_here == 64
        and head_cols % TILE == 0
        and hidden_cols == data_parts * LANES
        and hidden_cols % 512 == 0
        and blocks == 1
        and tokens % 512 == 0
    )


def shards(*arrays, parts):
    (
        hidden_in,
        logits_in,
        cotangent,
        bucket_ids,
        seq_counts,
        key_mask,
        w_qkv,
        w_out,
        w_in,
        w_back,
        vectors,
        bias_in,
    ) = arrays[:12]
    data_parts = parts[0]
    tokens, width = hidden_in.shape
    head_cols = w_qkv.shape[3]
    hidden_cols = w_in.shape[2]
    heads = logits_in.shape[1]
    if not fits(parts, head_cols, hidden_cols, heads, tokens, width, logits_in.shape[0]):
        return plain_shards(*arrays)
    f32 = jnp.float32
    b16 = jnp.bfloat16
    ten = lax.axis_index("tensor")
    share = tokens // 4
    cut = width // data_parts
    cols_n = data_parts // 2
    bucket = bucket_ids[0]
    seq_span = jnp.where(bucket == 0, tokens // 4, jnp.where(bucket == 1, tokens // 2, tokens))
    seq_of = jnp.arange(tokens, dtype=jnp.int32) // seq_span
    live = (key_mask == 1) & (seq_of < seq_counts[0])
    key_ids = jnp.where(
        jnp.arange(16, dtype=jnp.int32)[:, None] < 8,
        jnp.where(live, seq_of, -1).astype(f32)[None, :],
        1.0 / seq_span.astype(f32),
    )
    owned = vectors.shape[2]
    mine = (jnp.arange(LANES, dtype=jnp.int32) // owned) == ten

    def small_rows(wide, narrow, fill):
        rows = jnp.tile(wide.reshape(LAYERS * 8, owned), (1, LANES // owned))
        rows = jnp.where(mine[None, :], rows, fill)
        rest = jnp.full((32 - LAYERS * 9, LANES), fill, f32)
        return jnp.concatenate([rows, narrow, rest], axis=0)

    small_in = jnp.stack(
        [
            small_rows(vectors, bias_in, 0.0),
            small_rows(arrays[16], arrays[17], 0.0),
            small_rows(arrays[22], arrays[23], 1.0),
        ]
    )

    hbm = pl.BlockSpec(memory_space=pl.ANY)
    vmem = pl.BlockSpec(memory_space=pltpu.VMEM)
    dma = pltpu.SemaphoreType.DMA
    shape = jax.ShapeDtypeStruct
    n = LAYERS
    grad_shapes = (
        (3, cut, head_cols),
        (head_cols, cut),
        (cut, hidden_cols),
        (hidden_cols, cut),
    )
    results = pl.pallas_call(
        functools.partial(step_kernel, data_parts),
        out_shape=(
            shape((share, width), b16),
            shape((heads, tokens, tokens), b16),
            shape((share, width), f32),
            shape((heads, tokens, tokens), b16),
        )
        + tuple(shape((n,) + size, f32) for size in grad_shapes)
        + (shape((24, LANES), f32),) * 2,
        in_specs=[hbm, hbm, hbm, vmem, vmem] + [hbm] * 16,
        out_specs=(hbm, hbm, vmem, hbm, hbm, hbm, hbm, hbm, vmem, vmem),
        scratch_shapes=[
            pltpu.VMEM((n, 3, width, head_cols), b16),
            pltpu.VMEM((n, head_cols, width), b16),
            pltpu.VMEM((n, width, hidden_cols), b16),
            pltpu.VMEM((n, hidden_cols, width), b16),
            pltpu.VMEM((heads, tokens, tokens), b16),
            pltpu.VMEM((n, heads, tokens, tokens), b16),
            pltpu.VMEM((tokens, width), b16),
            pltpu.VMEM((tokens, width), b16),
            pltpu.VMEM((tokens, hidden_cols), b16),
            pltpu.VMEM((tokens, head_cols), b16),
            pltpu.VMEM((n, width, tokens), b16),
            pltpu.VMEM((n, width, tokens), b16),
            pltpu.VMEM((n, hidden_cols, tokens), b16),
            pltpu.VMEM((n, head_cols, tokens), b16),
            pltpu.VMEM((n, tokens, hidden_cols), b16),
            pltpu.VMEM((n, 3, tokens, head_cols), b16),
            pltpu.VMEM((n, share, width), f32),
            pltpu.VMEM((n, share, width), f32),
            pltpu.VMEM((3, tokens, head_cols), b16),
            pltpu.VMEM((share, width), f32),
            pltpu.VMEM((LANES, tokens), f32),
            pltpu.VMEM((LANES, tokens), f32),
            pltpu.VMEM((tokens, width), b16),
            pltpu.VMEM((2, share, width), b16),
            pltpu.VMEM((share, width), b16),
            pltpu.VMEM((share, width), b16),
            pltpu.VMEM((4, data_parts, 32, LANES), b16),
            pltpu.VMEM((n * 8, width), f32),
            pltpu.VMEM((8, hidden_cols), f32),
            pltpu.VMEM((n * 8 + 8, width), f32),
            pltpu.VMEM((4, n * 8 + 8, width), f32),
            pltpu.VMEM((data_parts, n * 8 + 8, LANES), f32),
            pltpu.VMEM((data_parts - 1, n * 8 + 8, LANES), f32),
        ]
        + [pltpu.VMEM((cols_n, 2) + size, b16) for size in grad_shapes]
        + [pltpu.VMEM((n, cols_n) + size, b16) for size in grad_shapes]
        + [pltpu.VMEM((n, cols_n - 1) + size, b16) for size in grad_shapes]
        + [pltpu.VMEM(size, f32) for _ in range(3) for size in grad_shapes]
        + [
            pltpu.VMEM((n * 8, width), f32),
            pltpu.VMEM((24, LANES), f32),
            pltpu.VMEM((4, 24, LANES), f32),
            pltpu.VMEM((24, LANES), f32),
            pltpu.VMEM((data_parts, 24, LANES), f32),
        ]
        + [
            dma((2,)),
            dma((n, 4)),
            dma((n, 4, cols_n, 2, 2)),
            dma((n, 4, cols_n, 2)),
            dma((n, 4, cols_n)),
            dma((n, 4, cols_n)),
            dma((width // TILE, 2)),
            dma((width // TILE, 2)),
            dma((width // TILE,)),
            dma((width // TILE,)),
            dma((2, 3)),
            dma((2, 3)),
            dma((data_parts + 2,)),
            dma((data_parts + 2,)),
            dma((data_parts + 2,)),
            dma((data_parts + 2,)),
            dma((4, cols_n)),
            dma((n, 4, cols_n)),
            dma((4, cols_n - 1)),
            dma((n, 4, cols_n - 1)),
            dma((4,)),
            dma((4,)),
            dma((3, 4)),
            dma((data_parts + 2,)),
            dma((data_parts + 2,)),
        ],
        compiler_params=pltpu.CompilerParams(
            collective_id=0, has_side_effects=True, vmem_limit_bytes=63 * 1024 * 1024
        ),
    )(
        hidden_in,
        logits_in,
        cotangent,
        key_ids,
        small_in,
        w_qkv.astype(b16),
        w_out.astype(b16),
        w_in.astype(b16),
        w_back.astype(b16),
        *arrays[6:10],
        *arrays[12:16],
        *arrays[18:22],
    )
    hidden_out, logits_out, grad_hidden, grad_scores = results[:4]
    small = results[8]
    vec_sum = lax.dynamic_slice_in_dim(small[: LAYERS * 8], ten * owned, owned, 1)
    bin_sum = small[LAYERS * 8 : LAYERS * 9]
    grads_all = results[4:8] + (vec_sum.reshape(LAYERS, 8, owned), bin_sum)
    masters = arrays[6:12]
    firsts = arrays[12:18]
    seconds = arrays[18:24]
    decays = (DECAY_RATE, DECAY_RATE, DECAY_RATE, DECAY_RATE, 0.0, 0.0)
    moved = []
    for master, gradient, first_prev, second_prev, decay_rate in zip(
        masters, grads_all, firsts, seconds, decays
    ):
        moment_one = BETA_ONE * first_prev + (1.0 - BETA_ONE) * gradient
        moment_two = BETA_TWO * second_prev + (1.0 - BETA_TWO) * gradient * gradient
        update = (
            moment_one / CORRECT_ONE / (jnp.sqrt(moment_two / CORRECT_TWO) + ADAM_EPS)
            + decay_rate * master
        )
        moved.append((moment_one, update))
    norms = jnp.sqrt(results[9][:, 0])
    trust_rows = norms[0::2] / norms[1::2]
    trust_all = jnp.concatenate(
        [trust_rows[: LAYERS * 4].reshape(LAYERS, 4), trust_rows[LAYERS * 4 :].reshape(LAYERS, 2)],
        axis=1,
    ).T
    new_params = tuple(
        (
            master
            - LEARN_RATE
            * trust_all[group_at].reshape((LAYERS,) + (1,) * (master.ndim - 1))
            * moved_one[1]
            for group_at, (master, moved_one) in enumerate(zip(masters, moved))
        )
    )
    return (
        (hidden_out, logits_out[None], grad_hidden, grad_scores[None].astype(f32))
        + grads_all
        + new_params
        + tuple(moved_one[0] for moved_one in moved)
        + (trust_all.T,)
    )


def solution(mesh):
    return jax.shard_map(
        functools.partial(shards, parts=(mesh.shape["dp"], mesh.shape["tensor"])),
        mesh=mesh,
        in_specs=(
            P("dp", None),
            P("dp", "tensor", None, None),
            P(("dp", "tensor"), None),
            P("dp"),
            P("dp"),
            P("dp"),
            P(None, None, "dp", "tensor"),
            P(None, "tensor", "dp"),
            P(None, "dp", "tensor"),
            P(None, "tensor", "dp"),
            P(None, None, ("dp", "tensor")),
            P(None, ("dp", "tensor")),
            P(None, None, "dp", "tensor"),
            P(None, "tensor", "dp"),
            P(None, "dp", "tensor"),
            P(None, "tensor", "dp"),
            P(None, None, ("dp", "tensor")),
            P(None, ("dp", "tensor")),
            P(None, None, "dp", "tensor"),
            P(None, "tensor", "dp"),
            P(None, "dp", "tensor"),
            P(None, "tensor", "dp"),
            P(None, None, ("dp", "tensor")),
            P(None, ("dp", "tensor")),
        ),
        out_specs=(
            P(("dp", "tensor"), None),
            P("dp", "tensor", None, None),
            P(("dp", "tensor"), None),
            P("dp", "tensor", None, None),
            P(None, None, "dp", "tensor"),
            P(None, "tensor", "dp"),
            P(None, "dp", "tensor"),
            P(None, "tensor", "dp"),
            P(None, None, ("dp", "tensor")),
            P(None, ("dp", "tensor")),
            P(None, None, "dp", "tensor"),
            P(None, "tensor", "dp"),
            P(None, "dp", "tensor"),
            P(None, "tensor", "dp"),
            P(None, None, ("dp", "tensor")),
            P(None, ("dp", "tensor")),
            P(None, None, "dp", "tensor"),
            P(None, "tensor", "dp"),
            P(None, "dp", "tensor"),
            P(None, "tensor", "dp"),
            P(None, None, ("dp", "tensor")),
            P(None, ("dp", "tensor")),
            P(),
        ),
        check_vma=False,
    )
```

```python
import functools

import jax
import jax.numpy as jnp
from jax import lax
from jax.experimental import pallas as pl
from jax.experimental.pallas import tpu as pltpu
from jax.sharding import PartitionSpec as P

LAYERS = 2


NORM_EPS = 1e-05
ADAM_EPS = 1e-06
BETA_ONE = 0.9
BETA_TWO = 0.999
CORRECT_ONE = 1.0
CORRECT_TWO = 0.632304575228943
LEARN_RATE = 0.3
DECAY_RATE = 0.01
NEG_FILL = -1e30


def layer_norm(values, gain, shift):
    center = values - jnp.mean(values, axis=-1, keepdims=True)
    spread = jnp.mean(center * center, axis=-1, keepdims=True)
    return center * lax.rsqrt(spread + NORM_EPS) * gain + shift


def gelu_exact(values):
    return jax.nn.gelu(values, approximate=False)


def plain_shards(
    hidden_in,
    logits_in,
    cotangent,
    bucket_ids,
    seq_counts,
    key_mask,
    w_qkv,
    w_out,
    w_in,
    w_back,
    vectors,
    bias_in,
    m_qkv,
    m_out,
    m_in,
    m_back,
    m_vectors,
    m_bias,
    v_qkv,
    v_out,
    v_in,
    v_back,
    v_vectors,
    v_bias,
):
    tensor_parts = lax.axis_size("tensor")
    tensor_index = lax.axis_index("tensor")
    data_parts = lax.axis_size("dp")
    tokens_here = hidden_in.shape[0]
    share_rows = tokens_here // tensor_parts
    first_row = tensor_index * share_rows
    block_count = logits_in.shape[0]
    heads_here = logits_in.shape[1]
    block_len = logits_in.shape[2]
    model_width = hidden_in.shape[1]
    head_cols = w_qkv.shape[3]
    head_size = head_cols // heads_here
    hidden_cols = w_in.shape[2]
    score_scale = head_size ** (-0.5)
    bucket = bucket_ids[0]
    seq_span = jnp.where(
        bucket == 0, block_len // 4, jnp.where(bucket == 1, block_len // 2, block_len)
    )
    position = jnp.arange(tokens_here, dtype=jnp.int32)
    seq_flat = position // seq_span
    seq_of = seq_flat.reshape(block_count, block_len)
    live_keys = ((key_mask == 1) & (seq_flat < seq_counts[0])).reshape(block_count, block_len)
    allowed = (seq_of[:, :, None] == seq_of[:, None, :]) & live_keys[:, None, :]
    vec_all, bin_all = (
        lax.all_gather(vectors.astype(jnp.bfloat16), ("dp", "tensor"), axis=2, tiled=True),
        lax.all_gather(bias_in.astype(jnp.bfloat16), ("dp", "tensor"), axis=1, tiled=True),
    )
    vec_all = vec_all.astype(jnp.float32)
    bin_all = bin_all.astype(jnp.float32)

    def sum_forward(term_fn):
        return lax.psum_scatter(
            term_fn(jnp.int32(0), share_rows * lax.axis_size("tensor")).astype(jnp.bfloat16),
            "tensor",
            scatter_dimension=0,
            tiled=True,
        ).astype(jnp.float32)

    def sum_backward(term_fn):
        return lax.psum_scatter(
            term_fn(jnp.int32(0), share_rows * lax.axis_size("tensor")).astype(jnp.bfloat16),
            "tensor",
            scatter_dimension=0,
            tiled=True,
        ).astype(jnp.float32)

    def gather_rows(own_rows):
        return lax.all_gather(own_rows, "tensor", axis=0, tiled=True)

    def gather_grads(own_rows):
        return lax.all_gather(own_rows, "tensor", axis=0, tiled=True)

    def own_cols(vector):
        return lax.dynamic_slice_in_dim(vector, tensor_index * head_cols, head_cols)

    def place_cols(part_sum, total_len, offset):
        return lax.dynamic_update_slice(jnp.zeros((total_len,), jnp.float32), part_sum, (offset,))

    def blocked(matrix):
        return matrix.reshape(block_count, block_len, head_cols)

    def headed(matrix):
        return matrix.reshape(block_len, heads_here, head_size)

    def block_scores(query_b, keys_b, earlier_b):
        raw = jnp.einsum(
            "ihe,jhe->hij", headed(query_b), headed(keys_b), preferred_element_type=jnp.float32
        )
        return raw * score_scale + earlier_b.astype(jnp.float32)

    def attend_block(inputs):
        query_b, keys_b, values_b, earlier_b, allowed_b = inputs
        scores = block_scores(query_b, keys_b, earlier_b)
        row_top = jnp.max(jnp.where(allowed_b[None], scores, NEG_FILL), axis=-1, keepdims=True)
        unscaled = jnp.exp(jnp.where(allowed_b[None], scores - row_top, NEG_FILL))
        row_total = jnp.sum(unscaled, axis=-1, keepdims=True)
        row_total = jnp.where(row_total > 0.5, row_total, 1.0)
        probs_low = (unscaled / row_total).astype(jnp.bfloat16)
        mixed = jnp.einsum(
            "hij,jhe->ihe", probs_low, headed(values_b), preferred_element_type=jnp.float32
        )
        return (
            mixed.reshape(block_len, head_cols).astype(jnp.bfloat16),
            scores.astype(jnp.bfloat16),
            row_top,
            row_total,
        )

    def attend_back(inputs):
        query_b, keys_b, values_b, earlier_b, allowed_b, row_top, row_total, dmixed_b, dlater_b = (
            inputs
        )
        scores = block_scores(query_b, keys_b, earlier_b)
        unscaled = jnp.exp(jnp.where(allowed_b[None], scores - row_top, NEG_FILL))
        probs = unscaled / row_total
        probs_low = probs.astype(jnp.bfloat16)
        dmixed_heads = headed(dmixed_b)
        dvalues = jnp.einsum(
            "hij,ihe->jhe", probs_low, dmixed_heads, preferred_element_type=jnp.float32
        )
        dprobs = jnp.einsum(
            "ihe,jhe->hij", dmixed_heads, headed(values_b), preferred_element_type=jnp.float32
        )
        dlocal = probs * (dprobs - jnp.sum(probs * dprobs, axis=-1, keepdims=True))
        dscores = (dlocal + dlater_b.astype(jnp.float32)).astype(jnp.bfloat16)
        dquery = (
            jnp.einsum("hij,jhe->ihe", dscores, headed(keys_b), preferred_element_type=jnp.float32)
            * score_scale
        )
        dkeys = (
            jnp.einsum("hij,ihe->jhe", dscores, headed(query_b), preferred_element_type=jnp.float32)
            * score_scale
        )
        return (
            dquery.reshape(block_len, head_cols),
            dkeys.reshape(block_len, head_cols),
            dvalues.reshape(block_len, head_cols),
            dscores,
        )

    full_in = hidden_in
    own_in = lax.dynamic_slice_in_dim(hidden_in, first_row, share_rows, 0)
    earlier = logits_in
    records = []
    for layer_at in range(LAYERS):
        fetched = (
            lax.all_gather(w_qkv[layer_at].astype(jnp.bfloat16), "dp", axis=1, tiled=True),
            lax.all_gather(w_out[layer_at].astype(jnp.bfloat16), "dp", axis=1, tiled=True),
            lax.all_gather(w_in[layer_at].astype(jnp.bfloat16), "dp", axis=0, tiled=True),
            lax.all_gather(w_back[layer_at].astype(jnp.bfloat16), "dp", axis=1, tiled=True),
        )
        forward_wqkv, forward_wout, forward_win, forward_wback = fetched
        forward_vector = vec_all[layer_at]
        forward_query = (
            jnp.dot(full_in, forward_wqkv[0], preferred_element_type=jnp.float32)
            + own_cols(forward_vector[2])
        ).astype(jnp.bfloat16)
        forward_keys = jnp.dot(full_in, forward_wqkv[1], preferred_element_type=jnp.float32).astype(
            jnp.bfloat16
        )
        forward_values = (
            jnp.dot(full_in, forward_wqkv[2], preferred_element_type=jnp.float32)
            + own_cols(forward_vector[3])
        ).astype(jnp.bfloat16)
        forward_attn_out, stored, forward_row_top, forward_row_total = lax.map(
            attend_block,
            (
                blocked(forward_query),
                blocked(forward_keys),
                blocked(forward_values),
                earlier,
                allowed,
            ),
        )
        forward_attn_out = forward_attn_out.reshape(tokens_here, head_cols)

        def attn_term(begin_row, row_count):
            return jnp.dot(forward_attn_out, forward_wout, preferred_element_type=jnp.float32)

        forward_mid_pre = sum_forward(attn_term) + forward_vector[4] + own_in.astype(jnp.float32)
        mid_own = layer_norm(forward_mid_pre, forward_vector[0], forward_vector[5]).astype(
            jnp.bfloat16
        )
        forward_mid_full = gather_rows(mid_own)
        bias_here = lax.dynamic_slice_in_dim(
            bin_all[layer_at], tensor_index * hidden_cols, hidden_cols
        )
        forward_pre_act = (
            jnp.dot(forward_mid_full, forward_win, preferred_element_type=jnp.float32) + bias_here
        )
        forward_active = gelu_exact(forward_pre_act).astype(jnp.bfloat16)

        def ffn_term(begin_row, row_count):
            return jnp.dot(forward_active, forward_wback, preferred_element_type=jnp.float32)

        forward_out_pre = sum_forward(ffn_term) + forward_vector[6] + mid_own.astype(jnp.float32)
        out_own = layer_norm(forward_out_pre, forward_vector[1], forward_vector[7]).astype(
            jnp.bfloat16
        )
        forward_state = (
            forward_query,
            forward_keys,
            forward_values,
            forward_attn_out,
            forward_row_top,
            forward_row_total,
            forward_mid_pre,
            forward_mid_full,
            forward_pre_act,
            forward_out_pre,
        )
        out_own, stored, state = (out_own, stored, forward_state)
        records.append((full_in, earlier, fetched, state))
        earlier = stored
        own_in = out_own
        if layer_at + 1 < LAYERS:
            full_in = gather_rows(out_own)
    logits_out = earlier
    d_own = cotangent.astype(jnp.float32)
    d_later = jnp.zeros_like(logits_in)
    mat_grads = [None] * LAYERS
    vec_grads = [None] * LAYERS
    bin_grads = [None] * LAYERS
    for layer_at in reversed(range(LAYERS)):
        full_in, earlier, fetched, state = records[layer_at]
        wqkv = lax.all_gather(w_qkv[layer_at].astype(jnp.bfloat16), "dp", axis=1, tiled=True)
        wout = lax.all_gather(w_out[layer_at].astype(jnp.bfloat16), "dp", axis=1, tiled=True)
        win = lax.all_gather(w_in[layer_at].astype(jnp.bfloat16), "dp", axis=0, tiled=True)
        wback = lax.all_gather(w_back[layer_at].astype(jnp.bfloat16), "dp", axis=1, tiled=True)
        (
            query,
            keys,
            values,
            attn_out,
            backward_row_top,
            backward_row_total,
            mid_pre,
            mid_full,
            pre_act,
            out_pre,
        ) = state
        backward_vector = vec_all[layer_at]
        out_grad, gain_two, shift_two = jax.vjp(
            layer_norm, out_pre, backward_vector[1], backward_vector[7]
        )[1](d_own)
        d_ffn = gather_grads(out_grad.astype(jnp.bfloat16))
        active = gelu_exact(pre_act).astype(jnp.bfloat16)
        grad_back = jnp.einsum("tf,td->fd", active, d_ffn, preferred_element_type=jnp.float32)
        d_active = jnp.einsum("td,fd->tf", d_ffn, wback, preferred_element_type=jnp.float32)
        d_pre = jax.vjp(gelu_exact, pre_act)[1](d_active)[0].astype(jnp.bfloat16)
        grad_in = jnp.einsum("td,tf->df", mid_full, d_pre, preferred_element_type=jnp.float32)

        def mid_term(begin_row, row_count):
            return jnp.einsum("tf,df->td", d_pre, win, preferred_element_type=jnp.float32)

        mid_grad = sum_backward(mid_term) + out_grad
        attn_grad, gain_one, shift_one = jax.vjp(
            layer_norm, mid_pre, backward_vector[0], backward_vector[5]
        )[1](mid_grad)
        d_attn = gather_grads(attn_grad.astype(jnp.bfloat16))
        grad_out_proj = jnp.einsum(
            "tc,td->cd", attn_out, d_attn, preferred_element_type=jnp.float32
        )
        d_mixed = jnp.einsum("td,cd->tc", d_attn, wout, preferred_element_type=jnp.float32).astype(
            jnp.bfloat16
        )
        backward_dquery, backward_dkeys, backward_dvalues, backward_dscores = lax.map(
            attend_back,
            (
                blocked(query),
                blocked(keys),
                blocked(values),
                earlier,
                allowed,
                backward_row_top,
                backward_row_total,
                blocked(d_mixed),
                d_later,
            ),
        )
        backward_dquery = backward_dquery.reshape(tokens_here, head_cols).astype(jnp.bfloat16)
        backward_dkeys = backward_dkeys.reshape(tokens_here, head_cols).astype(jnp.bfloat16)
        backward_dvalues = backward_dvalues.reshape(tokens_here, head_cols).astype(jnp.bfloat16)
        grad_qkv = jnp.stack(
            [
                jnp.einsum(
                    "td,tc->dc", full_in, backward_dquery, preferred_element_type=jnp.float32
                ),
                jnp.einsum(
                    "td,tc->dc", full_in, backward_dkeys, preferred_element_type=jnp.float32
                ),
                jnp.einsum(
                    "td,tc->dc", full_in, backward_dvalues, preferred_element_type=jnp.float32
                ),
            ]
        )

        def input_term(begin_row, row_count):
            total_term = jnp.einsum(
                "tc,dc->td", backward_dquery, wqkv[0], preferred_element_type=jnp.float32
            )
            total_term = total_term + jnp.einsum(
                "tc,dc->td", backward_dkeys, wqkv[1], preferred_element_type=jnp.float32
            )
            return total_term + jnp.einsum(
                "tc,dc->td", backward_dvalues, wqkv[2], preferred_element_type=jnp.float32
            )

        in_grad = sum_backward(input_term) + attn_grad
        col_offset = tensor_index * head_cols
        vec_grad = jnp.stack(
            [
                gain_one,
                gain_two,
                place_cols(
                    jnp.sum(backward_dquery.astype(jnp.float32), axis=0), model_width, col_offset
                ),
                place_cols(
                    jnp.sum(backward_dvalues.astype(jnp.float32), axis=0), model_width, col_offset
                ),
                jnp.sum(attn_grad, axis=0),
                shift_one,
                jnp.sum(out_grad, axis=0),
                shift_two,
            ]
        )
        bin_grad = place_cols(
            jnp.sum(d_pre.astype(jnp.float32), axis=0),
            hidden_cols * tensor_parts,
            tensor_index * hidden_cols,
        )
        d_own, d_later, mats, vec_grad, bin_grad = (
            in_grad,
            backward_dscores,
            (grad_qkv, grad_out_proj, grad_in, grad_back),
            vec_grad,
            bin_grad,
        )
        totals = (
            lax.psum(mats[0].astype(jnp.bfloat16), "dp").astype(jnp.float32),
            lax.psum(mats[1].astype(jnp.bfloat16), "dp").astype(jnp.float32),
            lax.psum(mats[2].astype(jnp.bfloat16), "dp").astype(jnp.float32),
            lax.psum(mats[3].astype(jnp.bfloat16), "dp").astype(jnp.float32),
        )
        data_index = lax.axis_index("dp")
        mat_grads[layer_at] = tuple(
            (
                lax.dynamic_slice_in_dim(
                    whole,
                    data_index * (whole.shape[axis_at] // data_parts),
                    whole.shape[axis_at] // data_parts,
                    axis_at,
                )
                for whole, axis_at in zip(totals, (1, 1, 0, 1))
            )
        )
        vec_grads[layer_at] = vec_grad
        bin_grads[layer_at] = bin_grad
    grad_logits = d_later.astype(jnp.float32)
    vec_sum, bin_sum = (
        lax.psum_scatter(jnp.stack(vec_grads), ("dp", "tensor"), scatter_dimension=2, tiled=True),
        lax.psum_scatter(jnp.stack(bin_grads), ("dp", "tensor"), scatter_dimension=1, tiled=True),
    )
    grads_all = (
        jnp.stack([mat_grads[level_at][0] for level_at in range(LAYERS)]),
        jnp.stack([mat_grads[level_at][1] for level_at in range(LAYERS)]),
        jnp.stack([mat_grads[level_at][2] for level_at in range(LAYERS)]),
        jnp.stack([mat_grads[level_at][3] for level_at in range(LAYERS)]),
        vec_sum,
        bin_sum,
    )
    masters = (w_qkv, w_out, w_in, w_back, vectors, bias_in)
    firsts = (m_qkv, m_out, m_in, m_back, m_vectors, m_bias)
    seconds = (v_qkv, v_out, v_in, v_back, v_vectors, v_bias)
    decays = (DECAY_RATE, DECAY_RATE, DECAY_RATE, DECAY_RATE, 0.0, 0.0)
    moved = []
    for master, gradient, first_prev, second_prev, decay_rate in zip(
        masters, grads_all, firsts, seconds, decays
    ):
        moment_one = BETA_ONE * first_prev + (1.0 - BETA_ONE) * gradient
        moment_two = BETA_TWO * second_prev + (1.0 - BETA_TWO) * gradient * gradient
        update = (
            moment_one / CORRECT_ONE / (jnp.sqrt(moment_two / CORRECT_TWO) + ADAM_EPS)
            + decay_rate * master
        )
        moved.append((moment_one, update))
    weight_sq = jnp.stack(
        [jnp.sum((master * master).reshape(LAYERS, -1), axis=1) for master in masters]
    )
    update_sq = jnp.stack(
        [jnp.sum((moved_one[1] * moved_one[1]).reshape(LAYERS, -1), axis=1) for moved_one in moved]
    )
    weight_tot, update_tot = lax.psum((weight_sq, update_sq), ("dp", "tensor"))
    trust_all = jnp.sqrt(weight_tot) / jnp.sqrt(update_tot)
    new_params = tuple(
        (
            master
            - LEARN_RATE
            * trust_all[group_at].reshape((LAYERS,) + (1,) * (master.ndim - 1))
            * moved_one[1]
            for group_at, (master, moved_one) in enumerate(zip(masters, moved))
        )
    )
    return (
        own_in,
        logits_out,
        d_own,
        grad_logits,
        grads_all[0],
        grads_all[1],
        grads_all[2],
        grads_all[3],
        grads_all[4],
        grads_all[5],
        new_params[0],
        new_params[1],
        new_params[2],
        new_params[3],
        new_params[4],
        new_params[5],
        moved[0][0],
        moved[1][0],
        moved[2][0],
        moved[3][0],
        moved[4][0],
        moved[5][0],
        trust_all.T,
    )


MESH = pl.DeviceIdType.MESH
TILE = 256
LANES = 128
ROWS_MAT = 4
X_FIRST = (1,)
Z_AHEAD = 2
X_AHEAD = 3
SLOTS = ((1, 3), (2, 1), (2, 3), (3, 1), (3, 2), (4, 1), (5, 1))
Z_FIRST = ()
BACK_SLOTS = (
    (-9, -9, 0, 1, 2, 3, 4, 5, 6),
    (-9, -5, -4, -2, 0, 0, 1, 2, 3),
    (4,),
)


def dot_nn(left, right):
    return lax.dot_general(
        left, right, (((1,), (0,)), ((), ())), preferred_element_type=jnp.float32
    )


def dot_nt(left, right):
    return lax.dot_general(
        left, right, (((1,), (1,)), ((), ())), preferred_element_type=jnp.float32
    )


def norm_parts(values):
    center = values - jnp.mean(values, axis=-1, keepdims=True)
    spread = jnp.mean(center * center, axis=-1, keepdims=True)
    return center, lax.rsqrt(spread + NORM_EPS)


def step_kernel(
    data_parts,
    hidden_in,
    logits_in,
    cotangent,
    bucket,
    count,
    key_mask,
    vec_w,
    bias_w,
    vec_m,
    bias_m,
    vec_v,
    bias_v,
    lw_qkv,
    lw_out,
    lw_in,
    lw_back,
    lm_qkv,
    lm_out,
    lm_in,
    lm_back,
    lv_qkv,
    lv_out,
    lv_in,
    lv_back,
    hidden_out,
    logits_out,
    grad_hidden,
    grad_scores,
    sum_qkv,
    sum_out,
    sum_in,
    sum_back,
    small_out,
    norm_out,
    key_ids,
    small_in,
    w_q,
    w_o,
    w_i,
    w_b,
    scores,
    probs,
    h_full,
    m_full,
    active,
    attn,
    h_turn,
    m_turn,
    g_turn,
    o_turn,
    slope,
    qkv,
    x_own,
    y_own,
    d_qkv,
    d_keep,
    turn_v,
    turn_k,
    part,
    got_core,
    sum_chip,
    got_y,
    vec_got,
    vec_all,
    bin_all,
    small_acc,
    small_got,
    small_send,
    small_sum,
    pk_q,
    pk_o,
    pk_i,
    pk_b,
    rx_q,
    rx_o,
    rx_i,
    rx_b,
    rz_q,
    rz_o,
    rz_i,
    rz_b,
    fw_q,
    fw_o,
    fw_i,
    fw_b,
    fm_q,
    fm_o,
    fm_i,
    fm_b,
    fv_q,
    fv_o,
    fv_i,
    fv_b,
    norms,
    norm_send,
    norm_ten,
    norm_mid,
    norm_dp,
    load_sem,
    own_sem,
    zs_sem,
    zr_sem,
    xs_sem,
    xr_sem,
    core_s,
    core_r,
    ys_sem,
    yr_sem,
    gat_s,
    gat_r,
    vec_s,
    vec_r,
    sml_s,
    sml_r,
    gxs_sem,
    gxr_sem,
    gzs_sem,
    gzr_sem,
    fin_sem,
    out_sem,
    lamb_sem,
    ns_sem,
    nr_sem,
    credit,
):
    dp = lax.axis_index("dp")
    ten = lax.axis_index("tensor")
    cols_n = data_parts // 2
    side = lax.rem(dp, 2)
    place = dp // 2
    row_y = ten // 2
    core = lax.rem(ten, 2)
    across = dp + 1 - 2 * side
    core_mate = ten + 1 - 2 * core
    y_mate = lax.rem(ten + 2, 4)
    width = hidden_in.shape[1]
    tokens = hidden_in.shape[0]
    share = tokens // 4
    half = share // 2
    head_cols = qkv.shape[3]
    hidden_cols = slope.shape[2]
    cut = width // data_parts
    tiles = width // TILE
    f32 = jnp.float32
    b16 = jnp.bfloat16

    def along(step):
        return lax.rem(place + step, cols_n) * 2 + side

    def mult(value, by):
        return pl.multiple_of(value, by)

    def rdma(src, dst, send, recv, to_dp, to_ten):
        return pltpu.make_async_remote_copy(
            src_ref=src,
            dst_ref=dst,
            send_sem=send,
            recv_sem=recv,
            device_id=(to_dp, to_ten),
            device_id_type=MESH,
        )

    def region(kind, layer, dev):
        at = pl.ds(mult(dev * cut, cut), cut)
        if kind == 0:
            return w_q.at[layer, :, at, :]
        if kind == 1:
            return w_o.at[layer, :, at]
        if kind == 2:
            return w_i.at[layer, at, :]
        return w_b.at[layer, :, at]

    load_h = pltpu.make_async_copy(hidden_in, h_full, load_sem.at[0])
    load_s = pltpu.make_async_copy(logits_in.at[0], scores, load_sem.at[1])
    load_h.start()
    load_s.start()
    masters = (
        (lw_qkv, lw_out, lw_in, lw_back),
        (lm_qkv, lm_out, lm_in, lm_back),
        (lv_qkv, lv_out, lv_in, lv_back),
    )
    held = ((fw_q, fw_o, fw_i, fw_b), (fm_q, fm_o, fm_i, fm_b), (fv_q, fv_o, fv_i, fv_b))

    def lamb_load(kind, layer, which):
        return pltpu.make_async_copy(
            masters[which][kind].at[layer], held[which][kind], lamb_sem.at[which, kind]
        )

    def own_load(kind, layer):
        to = LAYERS - 1 - layer
        return pltpu.make_async_copy(masters[0][kind].at[layer], held[to][kind], own_sem.at[layer, kind])

    for layer in range(LAYERS):
        for kind in range(ROWS_MAT):
            own_load(kind, layer).start()

    barrier = pltpu.get_barrier_semaphore()

    def greet(step, carry):
        pl.semaphore_signal(
            barrier, inc=1, device_id=(lax.rem(dp + step, data_parts), ten), device_id_type=MESH
        )
        return carry

    lax.fori_loop(1, data_parts, greet, 0)
    for other in range(1, 4):
        pl.semaphore_signal(
            barrier, inc=1, device_id=(dp, lax.rem(ten + other, 4)), device_id_type=MESH
        )

    def w_x(kind, layer, from_place, col):
        dst = region(kind, layer, from_place * 2 + col)
        return rdma(
            dst,
            dst,
            xs_sem.at[layer, kind, from_place],
            xr_sem.at[layer, kind, from_place],
            across,
            ten,
        )

    def w_z(kind, layer, from_place, col, way):
        dst = region(kind, layer, from_place * 2 + col)
        which = lax.rem(col + side, 2)
        return rdma(
            dst,
            dst,
            zs_sem.at[layer, kind, from_place, which, (way + 1) // 2],
            zr_sem.at[layer, kind, from_place, which],
            dp + 2 * way,
            ten,
        )

    can_go = {1: place < cols_n - 1, -1: place > 0}

    def w_both_ways(kind, layer, col):
        for way in (1, -1):

            @pl.when(can_go[way])
            def _():
                w_z(kind, layer, place, col, way).start()

    def w_far(kind, layer, col, step):
        dst = region(kind, layer, place * 2 + col)
        which = lax.rem(col + side, 2)
        return rdma(
            dst,
            dst,
            zs_sem.at[layer, kind, step, which, 0],
            zr_sem.at[layer, kind, step, which],
            along(step),
            ten,
        )

    def w_event(kind, layer, hop):
        if kind in X_FIRST:
            w_x(kind, layer, place, 1 - side).wait_recv()
            for step in range(1, cols_n):
                w_far(kind, layer, 1 - side, step).start()
            return
        for way in (1, -1):
            came = place - hop * way

            @pl.when(came >= 0 if way == 1 else came < cols_n)
            def _():
                w_z(kind, layer, came, side, way).wait_recv()

                @pl.when(can_go[way])
                def _():
                    w_z(kind, layer, came, side, way).start()

                w_x(kind, layer, came, side).start()

    order = [(kind, layer) for layer in range(LAYERS) for kind in range(ROWS_MAT)]

    def w_own_z(index):
        if index < len(order):
            kind, layer = order[index]
            if kind in X_FIRST:
                for step in range(1, cols_n):
                    w_far(kind, layer, side, step).start()
            else:
                w_both_ways(kind, layer, side)

    def w_own_x(index):
        if index < len(order):
            w_x(*order[index], place, side).start()

    def w_own(index):
        kind, layer = order[index]
        own_load(kind, layer).wait()
        mine = region(kind, layer, dp)
        mine[...] = held[LAYERS - 1 - layer][kind][...].astype(b16)

    for index in range(X_AHEAD):
        w_own(index)
    for kind, slots in enumerate((rz_q, rz_o, rz_i, rz_b)):
        if kind in Z_FIRST:
            continue

        @pl.when(place == 0)
        def _():
            slots[1 : cols_n + 1] = jnp.zeros((cols_n,) + slots.shape[1:], b16)

        @pl.when(place == cols_n - 1)
        def _():
            slots[0:cols_n] = jnp.zeros((cols_n,) + slots.shape[1:], b16)

    owned = vec_w.shape[2]
    spread_row = lax.broadcasted_iota(jnp.int32, (owned, LANES), 0)
    spread_col = lax.broadcasted_iota(jnp.int32, (owned, LANES), 1)
    spread = jnp.where(spread_row + ten * owned == spread_col, 1.0, 0.0)
    lane_row = lax.broadcasted_iota(jnp.int32, (1, LANES), 1)
    not_owned = jnp.where(lane_row // owned == ten, 0.0, 1.0)
    small_in[...] = jnp.zeros_like(small_in)
    small_in[2] = jnp.ones_like(small_in[2])
    for which, (wide, narrow) in enumerate(((vec_w, bias_w), (vec_m, bias_m), (vec_v, bias_v))):
        for layer in range(LAYERS):
            rows = lax.dot_general(
                wide[layer],
                spread,
                (((1,), (0,)), ((), ())),
                precision=lax.Precision.HIGHEST,
                preferred_element_type=jnp.float32,
            )
            if which == 2:
                rows = rows + not_owned
            small_in[which, layer * 8 : layer * 8 + 8, :] = rows
            small_in[which, LAYERS * 8 + layer : LAYERS * 8 + layer + 1, :] = narrow[
                layer : layer + 1, :
            ]
    vec_got[ten, dp] = small_in[0].astype(b16)
    span_of = (tokens // 4, tokens // 2, tokens)
    per_key = jnp.where(
        bucket[0] == 0, 1.0 / span_of[0], jnp.where(bucket[0] == 1, 1.0 / span_of[1], 1.0 / span_of[2])
    ).astype(f32)
    key_at = lax.broadcasted_iota(jnp.int32, (1, tokens), 1).astype(f32)
    key_seq = jnp.floor(key_at * per_key)
    alive = (key_mask[...] == 1) & (key_seq < count[0].astype(f32))
    key_ids[0:1, :] = jnp.where(alive, key_seq, -1.0)

    pl.semaphore_wait(barrier, data_parts + 2)
    def vec_one(step):
        return rdma(
            vec_got.at[ten, dp],
            vec_got.at[ten, dp],
            vec_s.at[step - 1],
            vec_r.at[step - 1],
            lax.rem(dp + step, data_parts),
            ten,
        )

    def vec_go(step, carry):
        vec_one(step).start()
        return carry

    lax.fori_loop(1, data_parts, vec_go, 0)

    for index in range(X_AHEAD):
        if index < Z_AHEAD:
            w_own_z(index)
        w_own_x(index)

    for index in range(X_AHEAD, len(order)):
        w_own(index)

    events = [
        (index, hop)
        for index in range(len(order))
        for hop in range(1, 2 if order[index][0] in X_FIRST else cols_n)
    ]
    passed = [0]

    def pass_on(layer_at, kind_at, hop_at):
        goal = (layer_at * ROWS_MAT + kind_at, hop_at)
        while passed[0] < len(events) and events[passed[0]] <= goal:
            index, hop = events[passed[0]]
            w_event(*order[index], hop)
            if hop == cols_n - 1 or order[index][0] in X_FIRST:
                w_own_z(index + Z_AHEAD)
                w_own_x(index + X_AHEAD)
            passed[0] += 1

    def have(layer, kind):
        pass_on(layer, kind, cols_n)
        if kind in X_FIRST:
            for step in range(1, cols_n):
                for col in (side, 1 - side):
                    w_far(kind, layer, col, step).wait_recv()
        else:
            for from_place in range(cols_n):
                w_x(kind, layer, from_place, 1 - side).wait_recv()

    def w_finish():
        for kind, layer in order:
            if kind in X_FIRST:
                w_x(kind, layer, place, side).wait_send()
                for step in range(1, cols_n):
                    for col in (side, 1 - side):
                        w_far(kind, layer, col, step).wait_send()
                continue
            for from_place in range(cols_n):
                w_x(kind, layer, from_place, side).wait_send()

                @pl.when(can_go[1] & (from_place <= place))
                def _():
                    w_z(kind, layer, from_place, side, 1).wait_send()

                @pl.when(can_go[-1] & (from_place >= place))
                def _():
                    w_z(kind, layer, from_place, side, -1).wait_send()

    def vec_wait(step, carry):
        vec_one(step).wait_send()
        vec_one(step).wait_recv()
        return carry

    lax.fori_loop(1, data_parts, vec_wait, 0)

    def vec_two(step):
        return rdma(
            vec_got.at[ten],
            vec_got.at[ten],
            vec_s.at[data_parts - 2 + step],
            vec_r.at[data_parts - 2 + step],
            dp,
            lax.rem(ten + step, 4),
        )

    for step in range(1, 4):
        vec_two(step).start()
    for step in range(1, 4):
        vec_two(step).wait_send()
        vec_two(step).wait_recv()
    for dev in range(data_parts):
        total = vec_got[0, dev].astype(f32)
        for other in range(1, 4):
            total = total + vec_got[other, dev].astype(f32)
        vec_all[:, dev * LANES : (dev + 1) * LANES] = total[0 : LAYERS * 8]
    for piece in range(hidden_cols // LANES):
        got = vec_got[piece % 4, ten * 2 + piece // 4].astype(f32)
        bin_all[:, piece * LANES : (piece + 1) * LANES] = got[LAYERS * 8 : LAYERS * 8 + 8]

    def vec_row(layer, row):
        return vec_all[layer * 8 + row : layer * 8 + row + 1, :]

    def block_rows(which_y, which_core):
        return pl.ds(mult((which_y * 2 + which_core) * share, share), share)

    far_block = block_rows(1 - row_y, 1 - core)
    mate_block = block_rows(row_y, 1 - core)
    over_block = block_rows(1 - row_y, core)
    own_block = block_rows(row_y, core)

    def tile_cols(tile):
        return pl.ds(mult(tile * TILE, TILE), TILE)

    def send_core(tile, which):
        rows = far_block if which == 0 else mate_block
        return rdma(
            part.at[rows, tile_cols(tile)],
            got_core.at[which, :, tile_cols(tile)],
            core_s.at[tile, which],
            core_r.at[tile, which],
            dp,
            core_mate,
        )

    def send_y(tile):
        return rdma(
            sum_chip.at[:, tile_cols(tile)],
            got_y.at[:, tile_cols(tile)],
            ys_sem.at[tile],
            yr_sem.at[tile],
            dp,
            y_mate,
        )

    def add_core(tile):
        send_core(tile, 0).wait_recv()
        at = tile_cols(tile)
        sum_chip[:, at] = (
            part[over_block, at].astype(f32) + got_core[0, :, at].astype(f32)
        ).astype(b16)
        send_y(tile).start()

    def sum_start(tile_fn):
        def one(tile, carry):
            part[:, tile_cols(tile)] = tile_fn(tile).astype(b16)
            send_core(tile, 0).start()
            send_core(tile, 1).start()

            @pl.when(tile > 0)
            def _():
                add_core(tile - 1)

            return carry

        lax.fori_loop(0, tiles, one, 0)
        add_core(tiles - 1)

    def sum_end():
        for tile in range(tiles):
            send_core(tile, 1).wait_recv()
            send_y(tile).wait_recv()
        for tile in range(tiles):
            send_core(tile, 0).wait_send()
            send_core(tile, 1).wait_send()
            send_y(tile).wait_send()

    def sum_rows(which):
        at = pl.ds(which * half, half)
        mine = pl.ds(mult(ten * share + which * half, half), half)
        return (
            part[mine, :].astype(f32) + got_core[1, at, :].astype(f32) + got_y[at, :].astype(f32)
        )

    def gat_copy(buf, which, kind):
        if kind == 2:
            rows = pl.ds(mult(y_mate * share + which * half, half), half)
        else:
            rows = pl.ds(mult(ten * share + which * half, half), half)
        return rdma(
            buf.at[rows],
            buf.at[rows],
            gat_s.at[which, kind],
            gat_r.at[which, kind],
            dp,
            y_mate if kind == 1 else core_mate,
        )

    def gat_start(buf, which):
        gat_copy(buf, which, 1).start()
        gat_copy(buf, which, 0).start()

    def gat_end(buf):
        for which in range(2):
            gat_copy(buf, which, 1).wait_recv()
            gat_copy(buf, which, 2).start()
        for which in range(2):
            gat_copy(buf, which, 0).wait_recv()
            gat_copy(buf, which, 2).wait_recv()
        for which in range(2):
            for kind in range(3):
                gat_copy(buf, which, kind).wait_send()

    def own_rows(which):
        return pl.ds(mult(ten * share + which * half, half), half)

    def turn(src, dst, layer):
        def one(at, carry):
            dst[layer, tile_cols(at), :] = src[:, tile_cols(at)].T
            return carry

        lax.fori_loop(0, src.shape[1] // TILE, one, 0)

    lane = lax.broadcasted_iota(jnp.int32, (1, LANES), 1)
    low_lanes = jnp.where(lane < 64, 1.0, 0.0).astype(b16)
    high_lanes = jnp.where(lane < 64, 0.0, 1.0).astype(b16)
    lane_masks = (low_lanes, high_lanes)
    scale = 0.125
    score_rows = 256
    pairs = head_cols // LANES

    def pair_cols(pair):
        return slice(pair * LANES, (pair + 1) * LANES)

    def attend(layer, pair):
        def one(step, carry):
            rows = pl.ds(mult(step * score_rows, score_rows), score_rows)
            at = slice(pair * LANES, (pair + 1) * LANES)
            queries = qkv[layer, 0, rows, at]
            keys = qkv[layer, 1, :, at]
            values = qkv[layer, 2, :, at]
            row = lax.broadcasted_iota(jnp.int32, (score_rows, 1), 0) + step * score_rows
            allowed = jnp.floor(row.astype(f32) * per_key) == key_ids[0:1, :]
            mixed = jnp.zeros((score_rows, LANES), f32)
            for head in range(2):
                raw = dot_nt(queries, keys * lane_masks[head])
                full = raw * scale + scores[pair * 2 + head, rows, :].astype(f32)
                scores[pair * 2 + head, rows, :] = full.astype(b16)
                top = jnp.max(jnp.where(allowed, full, NEG_FILL), axis=-1, keepdims=True)
                weight = jnp.exp(jnp.where(allowed, full - top, NEG_FILL))
                total = jnp.sum(weight, axis=-1, keepdims=True)
                total = jnp.where(total > 0.5, total, 1.0)
                low = (weight * (1.0 / total)).astype(b16)
                probs[layer, pair * 2 + head, rows, :] = low
                mixed = mixed + dot_nn(low, values * lane_masks[head])
            attn[rows, at] = mixed.astype(b16)
            return carry

        lax.fori_loop(0, tokens // score_rows, one, 0)

    def attend_back(layer, first, pairs_of):
        def pair_one(pair, carry):
            at = pair_cols(pair)
            turn_v[...] = jnp.zeros_like(turn_v)
            turn_k[...] = jnp.zeros_like(turn_k)

            def one(step, inner):
                rows = pl.ds(mult(step * score_rows, score_rows), score_rows)
                queries = qkv[layer, 0, rows, at]
                keys = qkv[layer, 1, :, at]
                values = qkv[layer, 2, :, at]
                grads = attn[rows, at]
                turned_q = queries.T
                turned_g = grads.T
                d_query = jnp.zeros((score_rows, LANES), f32)
                for head in range(2):
                    low = probs[layer, pair * 2 + head, rows, :]
                    prob = low.astype(f32)
                    d_prob = dot_nt(grads, values * lane_masks[head])
                    inner_sum = jnp.sum(prob * d_prob, axis=-1, keepdims=True)
                    d_score = prob * (d_prob - inner_sum)
                    if not first:
                        d_score = d_score + scores[pair * 2 + head, rows, :].astype(f32)
                    d_low = d_score.astype(b16)
                    scores[pair * 2 + head, rows, :] = d_low
                    d_query = d_query + dot_nn(d_low, keys * lane_masks[head])
                    part_rows = slice(head * 64, head * 64 + 64)
                    turn_v[part_rows, :] += dot_nn(turned_g[part_rows, :], low)
                    turn_k[part_rows, :] += dot_nn(turned_q[part_rows, :], d_low)
                d_qkv[0, rows, at] = (d_query * scale).astype(b16)
                return inner

            lax.fori_loop(0, tokens // score_rows, one, 0)
            d_qkv[1, :, at] = (turn_k[...] * scale).T.astype(b16)
            d_qkv[2, :, at] = turn_v[...].T.astype(b16)
            return carry

        for pair in pairs_of:
            pair_one(pair, 0)

    own_cols = pl.ds(mult(ten * head_cols, head_cols), head_cols)
    small_acc[...] = jnp.zeros_like(small_acc)
    load_h.wait()
    load_s.wait()
    for layer in range(LAYERS):
        have(layer, 0)
        for which in range(3):
            product = dot_nn(h_full[...], w_q[layer, which])
            if which == 0:
                product = product + vec_all[layer * 8 + 2 : layer * 8 + 3, own_cols]
            if which == 2:
                product = product + vec_all[layer * 8 + 3 : layer * 8 + 4, own_cols]
            qkv[layer, which] = product.astype(b16)
        pass_on(layer, *SLOTS[0])
        attend(layer, 0)
        pass_on(layer, *SLOTS[1])
        attend(layer, 1)
        have(layer, 1)
        sum_start(lambda tile: dot_nn(attn[...], w_o[layer, :, tile_cols(tile)]))
        turn(attn, o_turn, layer)
        turn(h_full, h_turn, layer)
        pass_on(layer, *SLOTS[2])
        sum_end()
        for which in range(2):
            at = pl.ds(which * half, half)
            mid = sum_rows(which) + vec_row(layer, 4) + h_full[own_rows(which), :].astype(f32)
            x_own[layer, at, :] = mid
            center, rate = norm_parts(mid)
            m_full[own_rows(which), :] = (
                center * rate * vec_row(layer, 0) + vec_row(layer, 5)
            ).astype(b16)
            gat_start(m_full, which)
        pass_on(layer, *SLOTS[3])
        gat_end(m_full)

        def ffn_tile(tile, carry):
            at = tile_cols(tile)
            pre = dot_nn(m_full[...], w_i[layer, :, at]) + bin_all[layer : layer + 1, at]
            cumul = 0.5 * (1.0 + lax.erf(pre * 0.7071067811865476))
            dens = jnp.exp(-0.5 * pre * pre) * 0.3989422804014327
            active[:, at] = (pre * cumul).astype(b16)
            slope[layer, :, at] = (cumul + pre * dens).astype(b16)
            return carry

        have(layer, 2)
        pass_on(layer, *SLOTS[4])
        lax.fori_loop(0, hidden_cols // TILE, ffn_tile, 0)
        turn(m_full, m_turn, layer)
        have(layer, 3)
        sum_start(lambda tile: dot_nn(active[...], w_b[layer, :, tile_cols(tile)]))
        turn(active, g_turn, layer)
        pass_on(layer, *SLOTS[5])
        sum_end()
        for which in range(2):
            at = pl.ds(which * half, half)
            late = sum_rows(which) + vec_row(layer, 6) + m_full[own_rows(which), :].astype(f32)
            y_own[layer, at, :] = late
            center, rate = norm_parts(late)
            result = (center * rate * vec_row(layer, 1) + vec_row(layer, 7)).astype(b16)
            h_full[own_rows(which), :] = result
            if layer + 1 < LAYERS:
                gat_start(h_full, which)
        if layer + 1 < LAYERS:
            pass_on(layer, *SLOTS[6])
            gat_end(h_full)

    out_logits = pltpu.make_async_copy(scores, logits_out, out_sem.at[0])
    out_logits.start()
    all_own = pl.ds(mult(ten * share, share), share)
    out_hidden = pltpu.make_async_copy(h_full.at[all_own], hidden_out, out_sem.at[2])
    out_hidden.start()
    load_c = pltpu.make_async_copy(cotangent, sum_chip, out_sem.at[3])
    load_c.start()
    w_finish()

    packs = (pk_q, pk_o, pk_i, pk_b)
    got_x = (rx_q, rx_o, rx_i, rx_b)
    got_z = (rz_q, rz_o, rz_i, rz_b)
    sums = (sum_qkv, sum_out, sum_in, sum_back)

    def turn_of(turn_at):
        upper = place // 2
        near = upper * (cols_n - 1) + (1 - 2 * upper) * place
        swing = lax.rem(3 + turn_at + turn_at * (turn_at - 1) // 2, 4)
        at = (1 - near) * (3 - turn_at) + near * swing
        return upper * (cols_n - 1) + (1 - 2 * upper) * at

    def is_up(at):
        return (at - place + cols_n) // cols_n

    def g_x(kind, at):
        first = kind not in Z_FIRST
        return rdma(
            packs[kind].at[at, 1 - side],
            got_x[kind].at[at if first else 0],
            gxs_sem.at[kind, at],
            gxr_sem.at[kind, at],
            across,
            ten,
        )

    def g_z(kind, at):
        up = is_up(at)
        return rdma(
            packs[kind].at[at, side],
            got_z[kind].at[at + up],
            gzs_sem.at[kind, at],
            gzr_sem.at[kind, at + up],
            dp + 2 * (2 * up - 1),
            ten,
        )

    def g_z_came(kind, at, up):
        copy = rdma(
            packs[kind].at[at, side],
            got_z[kind].at[at + up],
            gzs_sem.at[kind, at],
            gzr_sem.at[kind, at + up],
            dp,
            ten,
        )

        @pl.when(((up == 1) & (place > 0)) | ((up == 0) & (place < cols_n - 1)))
        def _():
            copy.wait_recv()

    def g_far(kind, step):
        to = lax.rem(place + step, cols_n)
        return rdma(
            packs[kind].at[to],
            got_z[kind].at[step - 1],
            gzs_sem.at[kind, step],
            gzr_sem.at[kind, step - 1],
            to * 2 + side,
            ten,
        )

    def g_free(kind, layer):
        add_upto(layer, (3 - kind) * cols_n + cols_n - 1)
        for turn_at in range(cols_n - 1):
            at = turn_of(turn_at)
            if kind in Z_FIRST:
                g_far(kind, turn_at + 1).wait_send()
            else:
                g_z(kind, at).wait_send()
                g_x(kind, at).wait_send()
        g_x(kind, place).wait_send()

    def give_credit(kind):
        pl.semaphore_signal(
            credit.at[0, kind], inc=1, device_id=(across, ten), device_id_type=MESH
        )
        if kind in Z_FIRST:
            for step in range(1, cols_n):
                pl.semaphore_signal(
                    credit.at[1, kind], inc=1, device_id=(along(step), ten), device_id_type=MESH
                )
            return

        @pl.when(place > 0)
        def _():
            pl.semaphore_signal(
                credit.at[1, kind], inc=1, device_id=(dp - 2, ten), device_id_type=MESH
            )

        @pl.when(place < cols_n - 1)
        def _():
            pl.semaphore_signal(
                credit.at[2, kind], inc=1, device_id=(dp + 2, ten), device_id_type=MESH
            )

    def take_credit_x(kind):
        pl.semaphore_wait(credit.at[0, kind], 1)

    def take_credit_z(kind):
        if kind in Z_FIRST:
            pl.semaphore_wait(credit.at[1, kind], cols_n - 1)
            return

        @pl.when(place < cols_n - 1)
        def _():
            pl.semaphore_wait(credit.at[1, kind], 1)

        @pl.when(place > 0)
        def _():
            pl.semaphore_wait(credit.at[2, kind], 1)

    def chunks_of(kind):
        if kind == 0:
            return [(which,) for which in range(3)]
        if kind == 3:
            return [(pl.ds(piece * 256, 256),) for piece in range(hidden_cols // 256)]
        return [()]

    g_order = [
        (kind, layer, turn_at)
        for layer in reversed(range(LAYERS))
        for kind in (3, 2, 1, 0)
        for turn_at in range(cols_n)
    ]
    added = [0]

    def add_event(kind, layer, turn_at):
        if layer + 1 < LAYERS and turn_at == 0 and kind not in Z_FIRST:
            take_credit_z(kind)
        at = turn_of(turn_at)
        last = turn_at + 1 == cols_n
        if kind in Z_FIRST:
            if last:
                if layer + 1 < LAYERS:
                    take_credit_x(kind)
                for step in range(1, cols_n):
                    g_far(kind, step).wait_recv()
                for piece in chunks_of(kind):
                    ours = (at, 1 - side) + piece
                    total = packs[kind][ours].astype(f32)
                    for step in range(1, cols_n):
                        total = total + got_z[kind][(step - 1, 1 - side) + piece].astype(f32)
                    packs[kind][ours] = total.astype(b16)
                g_x(kind, at).start()
            return
        if last:
            return
        up = is_up(at)
        g_x(kind, at).wait_recv()
        g_z_came(kind, at, up)
        for piece in chunks_of(kind):
            ours = (at, side) + piece
            packs[kind][ours] = (
                packs[kind][ours].astype(f32)
                + got_x[kind][(at,) + piece].astype(f32)
                + got_z[kind][(at + up,) + piece].astype(f32)
            ).astype(b16)
        g_z(kind, at).start()

    def add_upto(layer_at, index):
        index = (LAYERS - 1 - layer_at) * 4 * cols_n + index
        while added[0] <= min(index, len(g_order) - 1):
            add_event(*g_order[added[0]])
            added[0] += 1

    def lamb_update(weight, first, second, gradient, decay):
        moment_one = BETA_ONE * first + (1.0 - BETA_ONE) * gradient
        moment_two = BETA_TWO * second + (1.0 - BETA_TWO) * gradient * gradient
        return (
            moment_one / CORRECT_ONE / (jnp.sqrt(moment_two / CORRECT_TWO) + ADAM_EPS)
            + decay * weight
        )

    def note_norm(row, values):
        norms[row : row + 1, 0 : values.shape[-1]] += jnp.sum(
            values * values, axis=0, keepdims=True
        )

    def g_end(kind, layer):
        add_upto(layer, (3 - kind) * cols_n + cols_n - 1)
        g_x(kind, place).wait_recv()
        if kind not in Z_FIRST:
            for up in (0, 1):
                g_z_came(kind, place, up)
        for which in range(3):
            if which or layer + 1 < LAYERS:
                lamb_load(kind, layer, which).wait()
        for piece in chunks_of(kind):
            total = packs[kind][(place, side) + piece].astype(f32)
            if kind in Z_FIRST:
                total = total + got_x[kind][(0,) + piece].astype(f32)
            else:
                total = total + got_x[kind][(place,) + piece].astype(f32)
            if kind in Z_FIRST:
                for step in range(1, cols_n):
                    total = total + got_z[kind][(step - 1, side) + piece].astype(f32)
            else:
                for up in (0, 1):
                    total = total + got_z[kind][(place + up,) + piece].astype(f32)
            here = piece if piece else (slice(None),)
            weight = held[0][kind][here]
            step_by = lamb_update(
                weight, held[1][kind][here], held[2][kind][here], total, DECAY_RATE
            )
            packs[kind][(place, side) + piece] = total.astype(b16)
            note_norm((layer * 4 + kind) * 2, weight)
            note_norm((layer * 4 + kind) * 2 + 1, step_by)
        fin_copy(kind, layer).start()
        if layer:
            give_credit(kind)
            for which in range(3):
                lamb_load(kind, layer - 1, which).start()

    def fin_copy(kind, layer):
        return pltpu.make_async_copy(
            packs[kind].at[place, side], sums[kind].at[layer], fin_sem.at[kind]
        )

    def pair_rows(at):
        return pl.ds(mult(at * 2 * cut, 2 * cut), 2 * cut)

    def grad_back(layer):
        if layer + 1 < LAYERS:
            fin_copy(3, layer + 1).wait()
            (take_credit_z if 3 in Z_FIRST else take_credit_x)(3)

        def one(turn_at, carry):
            at = turn_of(turn_at)
            for piece in range(hidden_cols // 512):
                rows = slice(piece * 512, (piece + 1) * 512)
                value = dot_nn(g_turn[layer, rows, :], m_full[:, pair_rows(at)]).astype(b16)
                pk_b[at, 0, rows, :] = value[:, :cut]
                pk_b[at, 1, rows, :] = value[:, cut:]
            if 3 not in Z_FIRST:
                g_x(3, at).start()
            return carry

        lax.fori_loop(0, cols_n, one, 0)
        if 3 in Z_FIRST:
            for step in range(1, cols_n):
                g_far(3, step).start()

    def grad_in(layer):
        if layer + 1 < LAYERS:
            fin_copy(2, layer + 1).wait()
            (take_credit_z if 2 in Z_FIRST else take_credit_x)(2)

        def one(turn_at, carry):
            at = turn_of(turn_at)
            for piece in range(hidden_cols // 512):
                cols = slice(piece * 512, (piece + 1) * 512)
                value = dot_nn(m_turn[layer, pair_rows(at), :], active[:, cols]).astype(b16)
                pk_i[at, 0, :, cols] = value[:cut]
                pk_i[at, 1, :, cols] = value[cut:]
            if 2 not in Z_FIRST:
                g_x(2, at).start()
            return carry

        lax.fori_loop(0, cols_n, one, 0)
        if 2 in Z_FIRST:
            for step in range(1, cols_n):
                g_far(2, step).start()

    def grad_out(layer):
        if layer + 1 < LAYERS:
            fin_copy(1, layer + 1).wait()
            (take_credit_z if 1 in Z_FIRST else take_credit_x)(1)

        def one(turn_at, carry):
            at = turn_of(turn_at)
            value = dot_nn(o_turn[layer], h_full[:, pair_rows(at)]).astype(b16)
            pk_o[at, 0] = value[:, :cut]
            pk_o[at, 1] = value[:, cut:]
            if 1 not in Z_FIRST:
                g_x(1, at).start()
            return carry

        lax.fori_loop(0, cols_n, one, 0)
        if 1 in Z_FIRST:
            for step in range(1, cols_n):
                g_far(1, step).start()

    def grad_qkv(layer):
        if layer + 1 < LAYERS:
            fin_copy(0, layer + 1).wait()
            (take_credit_z if 0 in Z_FIRST else take_credit_x)(0)

        def one(turn_at, carry):
            at = turn_of(turn_at)
            for which in range(3):
                value = dot_nn(h_turn[layer, pair_rows(at), :], d_qkv[which]).astype(b16)
                pk_q[at, 0, which] = value[:cut]
                pk_q[at, 1, which] = value[cut:]
            if 0 not in Z_FIRST:
                g_x(0, at).start()
            return carry

        lax.fori_loop(0, cols_n, one, 0)
        if 0 in Z_FIRST:
            for step in range(1, cols_n):
                g_far(0, step).start()

    def norm_back(kept, upstream, gain):
        center, rate = norm_parts(kept)
        unit = center * rate
        scaled = upstream * gain
        down = rate * (
            scaled
            - jnp.mean(scaled, axis=-1, keepdims=True)
            - unit * jnp.mean(scaled * unit, axis=-1, keepdims=True)
        )
        return down, unit

    def note(row, values):
        small_acc[row : row + 1, :] += jnp.sum(values, axis=0, keepdims=True)

    norms[...] = jnp.zeros_like(norms)
    for kind in range(ROWS_MAT):
        for which in (1, 2):
            lamb_load(kind, LAYERS - 1, which).start()
    load_c.wait()
    for layer in reversed(range(LAYERS)):
        last = layer + 1 == LAYERS
        base = layer * 8
        for which in range(2):
            at = pl.ds(which * half, half)
            upstream = sum_chip[at, :].astype(f32) if last else grad_hidden[at, :]
            down, unit = norm_back(y_own[layer, at, :], upstream, vec_row(layer, 1))
            note(base + 1, upstream * unit)
            note(base + 7, upstream)
            note(base + 6, down)
            d_keep[at, :] = down
            m_full[own_rows(which), :] = down.astype(b16)
            gat_start(m_full, which)
        marks = BACK_SLOTS[0 if last else 1]
        add_upto(layer, marks[0])
        if not last:
            g_free(3, layer + 1)
            g_end(3, layer + 1)
        gat_end(m_full)
        grad_back(layer)
        add_upto(layer, marks[1])

        def slope_tile(tile, carry):
            at = tile_cols(tile)
            d_active = dot_nt(m_full[...], w_b[layer, at, :])
            d_pre = (d_active * slope[layer, :, at].astype(f32)).astype(b16)
            active[:, at] = d_pre
            small_acc[LAYERS * 8 + layer : LAYERS * 8 + layer + 1, at] = jnp.sum(
                d_pre.astype(f32), axis=0, keepdims=True
            )
            return carry

        lax.fori_loop(0, hidden_cols // TILE, slope_tile, 0)
        sum_start(lambda tile: dot_nt(active[...], w_i[layer, tile_cols(tile), :]))
        add_upto(layer, marks[2])
        if not last:
            g_free(2, layer + 1)
            g_end(2, layer + 1)
        grad_in(layer)
        add_upto(layer, marks[3])
        sum_end()
        if last:
            out_hidden.wait()
        for which in range(2):
            at = pl.ds(which * half, half)
            upstream = sum_rows(which) + d_keep[at, :]
            down, unit = norm_back(x_own[layer, at, :], upstream, vec_row(layer, 0))
            note(base + 0, upstream * unit)
            note(base + 5, upstream)
            note(base + 4, down)
            d_keep[at, :] = down
            h_full[own_rows(which), :] = down.astype(b16)
            gat_start(h_full, which)
        add_upto(layer, marks[4])
        gat_end(h_full)
        if not last:
            g_free(1, layer + 1)
            g_end(1, layer + 1)
        attn[...] = dot_nt(h_full[...], w_o[layer]).astype(b16)
        grad_out(layer)
        if last:
            out_logits.wait()
        add_upto(layer, marks[5])
        attend_back(layer, last, (0,))
        add_upto(layer, marks[6])
        attend_back(layer, last, (1,))
        add_upto(layer, marks[7])
        small_acc[base + 2 : base + 3, own_cols] = jnp.sum(
            d_qkv[0].astype(f32), axis=0, keepdims=True
        )
        small_acc[base + 3 : base + 4, own_cols] = jnp.sum(
            d_qkv[2].astype(f32), axis=0, keepdims=True
        )

        def input_tile(tile):
            rows = tile_cols(tile)
            total = dot_nt(d_qkv[0], w_q[layer, 0, rows, :])
            total = total + dot_nt(d_qkv[1], w_q[layer, 1, rows, :])
            return total + dot_nt(d_qkv[2], w_q[layer, 2, rows, :])

        sum_start(input_tile)
        if not last:
            g_free(0, layer + 1)
            g_end(0, layer + 1)
        grad_qkv(layer)
        add_upto(layer, marks[8])
        sum_end()
        for which in range(2):
            at = pl.ds(which * half, half)
            result = sum_rows(which) + d_keep[at, :]
            grad_hidden[at, :] = result

    out_scores = pltpu.make_async_copy(scores, grad_scores, out_sem.at[1])
    out_scores.start()

    small_got[ten] = small_acc[...]

    def small_one(step):
        return rdma(
            small_acc,
            small_got.at[ten],
            sml_s.at[step - 1],
            sml_r.at[step - 1],
            dp,
            lax.rem(ten + step, 4),
        )

    for step in range(1, 4):
        small_one(step).start()
    add_upto(0, BACK_SLOTS[2][0])
    for step in range(1, 4):
        small_one(step).wait_recv()
    mat_rows = LAYERS * 8
    for dev in range(data_parts):
        cols = slice(dev * LANES, (dev + 1) * LANES)
        total = small_got[0, 0:mat_rows, cols]
        for other in range(1, 4):
            total = total + small_got[other, 0:mat_rows, cols]
        small_send[dev, 0:mat_rows, :] = total
        from_cols = pl.ds(mult(((dev % 2) * 4 + ten) * LANES, LANES), LANES)
        small_send[dev, mat_rows : mat_rows + 8, :] = small_got[
            dev // 2, mat_rows : mat_rows + 8, from_cols
        ]

    def small_two(step):
        to = lax.rem(dp + step, data_parts)
        return rdma(
            small_send.at[to],
            small_sum.at[step - 1],
            sml_s.at[2 + step],
            sml_r.at[2 + step],
            to,
            ten,
        )

    def small_go(step, carry):
        small_two(step).start()
        return carry

    lax.fori_loop(1, data_parts, small_go, 0)
    g_end(3, 0)
    g_end(2, 0)
    g_end(1, 0)
    small_out[...] = small_send[dp]

    def small_wait(step, carry):
        small_two(step).wait_recv()
        small_two(step).wait_send()
        small_out[...] += small_sum[step - 1]
        return carry

    lax.fori_loop(1, data_parts, small_wait, 0)
    for step in range(1, 4):
        small_one(step).wait_send()
    g_end(0, 0)

    row_at = lax.broadcasted_iota(jnp.int32, (24, LANES), 0)
    lane_at = lax.broadcasted_iota(jnp.int32, (24, LANES), 1)
    in_share = (row_at >= mat_rows) | (lane_at // (width // data_parts // 4) == ten)
    small_grad = jnp.where(in_share & (row_at < mat_rows + LAYERS), small_out[...], 0.0)
    small_step = lamb_update(small_in[0, 0:24], small_in[1, 0:24], small_in[2, 0:24], small_grad, 0.0)
    norm_send[0:mat_rows, :] = jnp.broadcast_to(
        jnp.sum(norms[...], axis=-1, keepdims=True), (mat_rows, LANES)
    )
    for layer in range(LAYERS):
        for group, rows in enumerate(
            (slice(layer * 8, layer * 8 + 8), slice(mat_rows + layer, mat_rows + layer + 1))
        ):
            for which, values in enumerate((small_in[0, rows], small_step[rows])):
                total = jnp.sum(
                    jnp.sum(values * values, axis=0, keepdims=True), axis=1, keepdims=True
                )
                row = mat_rows + (layer * 2 + group) * 2 + which
                norm_send[row : row + 1, :] = jnp.broadcast_to(total, (1, LANES))

    def norm_one(step):
        return rdma(
            norm_send,
            norm_ten.at[ten],
            ns_sem.at[step - 1],
            nr_sem.at[step - 1],
            dp,
            lax.rem(ten + step, 4),
        )

    def norm_two(step):
        return rdma(
            norm_mid,
            norm_dp.at[dp],
            ns_sem.at[2 + step],
            nr_sem.at[2 + step],
            lax.rem(dp + step, data_parts),
            ten,
        )

    norm_ten[ten] = norm_send[...]
    for step in range(1, 4):
        norm_one(step).start()
    for step in range(1, 4):
        norm_one(step).wait_recv()
    total = norm_ten[0]
    for other in range(1, 4):
        total = total + norm_ten[other]
    norm_mid[...] = total
    norm_dp[dp] = total
    for step in range(1, data_parts):
        norm_two(step).start()
    for kind in range(ROWS_MAT):
        g_free(kind, 0)
        fin_copy(kind, 0).wait()
    out_scores.wait()
    for step in range(1, 4):
        norm_one(step).wait_send()
    for step in range(1, data_parts):
        norm_two(step).wait_recv()
    total = norm_dp[0]
    for other in range(1, data_parts):
        total = total + norm_dp[other]
    norm_out[...] = total
    for step in range(1, data_parts):
        norm_two(step).wait_send()


def fits(parts, head_cols, hidden_cols, heads_here, tokens, width, blocks):
    data_parts, tensor_parts = parts
    return (
        tensor_parts == 4
        and data_parts == 8
        and width // data_parts == LANES
        and head_cols // heads_here == 64
        and head_cols % TILE == 0
        and hidden_cols == data_parts * LANES
        and hidden_cols % 512 == 0
        and blocks == 1
        and tokens % 512 == 0
    )


def shards(*arrays, parts):
    (
        hidden_in,
        logits_in,
        cotangent,
        bucket_ids,
        seq_counts,
        key_mask,
        w_qkv,
        w_out,
        w_in,
        w_back,
        vectors,
        bias_in,
    ) = arrays[:12]
    data_parts = parts[0]
    tokens, width = hidden_in.shape
    head_cols = w_qkv.shape[3]
    hidden_cols = w_in.shape[2]
    heads = logits_in.shape[1]
    if not fits(parts, head_cols, hidden_cols, heads, tokens, width, logits_in.shape[0]):
        return plain_shards(*arrays)
    f32 = jnp.float32
    b16 = jnp.bfloat16
    ten = lax.axis_index("tensor")
    share = tokens // 4
    cut = width // data_parts
    cols_n = data_parts // 2
    owned = vectors.shape[2]
    hbm = pl.BlockSpec(memory_space=pl.ANY)
    vmem = pl.BlockSpec(memory_space=pltpu.VMEM)
    smem = pl.BlockSpec(memory_space=pltpu.SMEM)
    dma = pltpu.SemaphoreType.DMA
    shape = jax.ShapeDtypeStruct
    n = LAYERS
    grad_shapes = (
        (3, cut, head_cols),
        (head_cols, cut),
        (cut, hidden_cols),
        (hidden_cols, cut),
    )
    results = pl.pallas_call(
        functools.partial(step_kernel, data_parts),
        out_shape=(
            shape((share, width), b16),
            shape((heads, tokens, tokens), b16),
            shape((share, width), f32),
            shape((heads, tokens, tokens), b16),
        )
        + tuple(shape((n,) + size, b16) for size in grad_shapes)
        + (shape((24, LANES), f32),) * 2,
        in_specs=[hbm] * 3 + [smem] * 2 + [vmem] * 7 + [hbm] * 12,
        out_specs=(hbm, hbm, vmem, hbm, hbm, hbm, hbm, hbm, vmem, vmem),
        scratch_shapes=[
            pltpu.VMEM((8, tokens), f32),
            pltpu.VMEM((3, 32, LANES), f32),
            pltpu.VMEM((n, 3, width, head_cols), b16),
            pltpu.VMEM((n, head_cols, width), b16),
            pltpu.VMEM((n, width, hidden_cols), b16),
            pltpu.VMEM((n, hidden_cols, width), b16),
            pltpu.VMEM((heads, tokens, tokens), b16),
            pltpu.VMEM((n, heads, tokens, tokens), b16),
            pltpu.VMEM((tokens, width), b16),
            pltpu.VMEM((tokens, width), b16),
            pltpu.VMEM((tokens, hidden_cols), b16),
            pltpu.VMEM((tokens, head_cols), b16),
            pltpu.VMEM((n, width, tokens), b16),
            pltpu.VMEM((n, width, tokens), b16),
            pltpu.VMEM((n, hidden_cols, tokens), b16),
            pltpu.VMEM((n, head_cols, tokens), b16),
            pltpu.VMEM((n, tokens, hidden_cols), b16),
            pltpu.VMEM((n, 3, tokens, head_cols), b16),
            pltpu.VMEM((n, share, width), f32),
            pltpu.VMEM((n, share, width), f32),
            pltpu.VMEM((3, tokens, head_cols), b16),
            pltpu.VMEM((share, width), f32),
            pltpu.VMEM((LANES, tokens), f32),
            pltpu.VMEM((LANES, tokens), f32),
            pltpu.VMEM((tokens, width), b16),
            pltpu.VMEM((2, share, width), b16),
            pltpu.VMEM((share, width), b16),
            pltpu.VMEM((share, width), b16),
            pltpu.VMEM((4, data_parts, 32, LANES), b16),
            pltpu.VMEM((n * 8, width), f32),
            pltpu.VMEM((8, hidden_cols), f32),
            pltpu.VMEM((n * 8 + 8, width), f32),
            pltpu.VMEM((4, n * 8 + 8, width), f32),
            pltpu.VMEM((data_parts, n * 8 + 8, LANES), f32),
            pltpu.VMEM((data_parts - 1, n * 8 + 8, LANES), f32),
        ]
        + [pltpu.VMEM((cols_n, 2) + size, b16) for size in grad_shapes]
        + [
            pltpu.VMEM((1 if kind in Z_FIRST else cols_n,) + size, b16)
            for kind, size in enumerate(grad_shapes)
        ]
        + [
            pltpu.VMEM(((cols_n - 1, 2) if kind in Z_FIRST else (cols_n + 1,)) + size, b16)
            for kind, size in enumerate(grad_shapes)
        ]
        + [pltpu.VMEM(size, f32) for _ in range(3) for size in grad_shapes]
        + [
            pltpu.VMEM((n * 8, width), f32),
            pltpu.VMEM((24, LANES), f32),
            pltpu.VMEM((4, 24, LANES), f32),
            pltpu.VMEM((24, LANES), f32),
            pltpu.VMEM((data_parts, 24, LANES), f32),
        ]
        + [
            dma((2,)),
            dma((n, 4)),
            dma((n, 4, cols_n, 2, 2)),
            dma((n, 4, cols_n, 2)),
            dma((n, 4, cols_n)),
            dma((n, 4, cols_n)),
            dma((width // TILE, 2)),
            dma((width // TILE, 2)),
            dma((width // TILE,)),
            dma((width // TILE,)),
            dma((2, 3)),
            dma((2, 3)),
            dma((data_parts + 2,)),
            dma((data_parts + 2,)),
            dma((data_parts + 2,)),
            dma((data_parts + 2,)),
            dma((4, cols_n)),
            dma((4, cols_n)),
            dma((4, cols_n)),
            dma((4, cols_n + 1)),
            dma((4,)),
            dma((4,)),
            dma((3, 4)),
            dma((data_parts + 2,)),
            dma((data_parts + 2,)),
            pltpu.SemaphoreType.REGULAR((3, 4)),
        ],
        compiler_params=pltpu.CompilerParams(
            collective_id=0, has_side_effects=True, vmem_limit_bytes=63 * 1024 * 1024
        ),
    )(
        hidden_in,
        logits_in,
        cotangent,
        bucket_ids,
        seq_counts,
        key_mask.reshape(1, tokens),
        vectors,
        bias_in,
        arrays[16],
        arrays[17],
        arrays[22],
        arrays[23],
        *arrays[6:10],
        *arrays[12:16],
        *arrays[18:22],
    )
    hidden_out, logits_out, grad_hidden, grad_scores = results[:4]
    small = results[8]
    vec_sum = lax.dynamic_slice_in_dim(small[: LAYERS * 8], ten * owned, owned, 1)
    bin_sum = small[LAYERS * 8 : LAYERS * 9]
    grads_all = tuple(one.astype(f32) for one in results[4:8]) + (vec_sum.reshape(LAYERS, 8, owned), bin_sum)
    masters = arrays[6:12]
    firsts = arrays[12:18]
    seconds = arrays[18:24]
    decays = (DECAY_RATE, DECAY_RATE, DECAY_RATE, DECAY_RATE, 0.0, 0.0)
    moved = []
    for master, gradient, first_prev, second_prev, decay_rate in zip(
        masters, grads_all, firsts, seconds, decays
    ):
        moment_one = BETA_ONE * first_prev + (1.0 - BETA_ONE) * gradient
        moment_two = BETA_TWO * second_prev + (1.0 - BETA_TWO) * gradient * gradient
        update = (
            moment_one / CORRECT_ONE / (jnp.sqrt(moment_two / CORRECT_TWO) + ADAM_EPS)
            + decay_rate * master
        )
        moved.append((moment_one, update))
    norms = jnp.sqrt(results[9][:, 0])
    trust_rows = norms[0::2] / norms[1::2]
    trust_all = jnp.concatenate(
        [trust_rows[: LAYERS * 4].reshape(LAYERS, 4), trust_rows[LAYERS * 4 :].reshape(LAYERS, 2)],
        axis=1,
    ).T
    new_params = tuple(
        (
            master
            - LEARN_RATE
            * trust_all[group_at].reshape((LAYERS,) + (1,) * (master.ndim - 1))
            * moved_one[1]
            for group_at, (master, moved_one) in enumerate(zip(masters, moved))
        )
    )
    return (
        (hidden_out, logits_out[None], grad_hidden, grad_scores[None].astype(f32))
        + grads_all
        + new_params
        + tuple(moved_one[0] for moved_one in moved)
        + (trust_all.T,)
    )


def solution(mesh):
    return jax.shard_map(
        functools.partial(shards, parts=(mesh.shape["dp"], mesh.shape["tensor"])),
        mesh=mesh,
        in_specs=(
            P("dp", None),
            P("dp", "tensor", None, None),
            P(("dp", "tensor"), None),
            P("dp"),
            P("dp"),
            P("dp"),
            P(None, None, "dp", "tensor"),
            P(None, "tensor", "dp"),
            P(None, "dp", "tensor"),
            P(None, "tensor", "dp"),
            P(None, None, ("dp", "tensor")),
            P(None, ("dp", "tensor")),
            P(None, None, "dp", "tensor"),
            P(None, "tensor", "dp"),
            P(None, "dp", "tensor"),
            P(None, "tensor", "dp"),
            P(None, None, ("dp", "tensor")),
            P(None, ("dp", "tensor")),
            P(None, None, "dp", "tensor"),
            P(None, "tensor", "dp"),
            P(None, "dp", "tensor"),
            P(None, "tensor", "dp"),
            P(None, None, ("dp", "tensor")),
            P(None, ("dp", "tensor")),
        ),
        out_specs=(
            P(("dp", "tensor"), None),
            P("dp", "tensor", None, None),
            P(("dp", "tensor"), None),
            P("dp", "tensor", None, None),
            P(None, None, "dp", "tensor"),
            P(None, "tensor", "dp"),
            P(None, "dp", "tensor"),
            P(None, "tensor", "dp"),
            P(None, None, ("dp", "tensor")),
            P(None, ("dp", "tensor")),
            P(None, None, "dp", "tensor"),
            P(None, "tensor", "dp"),
            P(None, "dp", "tensor"),
            P(None, "tensor", "dp"),
            P(None, None, ("dp", "tensor")),
            P(None, ("dp", "tensor")),
            P(None, None, "dp", "tensor"),
            P(None, "tensor", "dp"),
            P(None, "dp", "tensor"),
            P(None, "tensor", "dp"),
            P(None, None, ("dp", "tensor")),
            P(None, ("dp", "tensor")),
            P(),
        ),
        check_vma=False,
    )
```

```python
import functools

import jax
import jax.numpy as jnp
from jax import lax
from jax.experimental import pallas as pl
from jax.experimental.pallas import tpu as pltpu
from jax.sharding import PartitionSpec as P

LAYERS = 2


NORM_EPS = 1e-05
ADAM_EPS = 1e-06
BETA_ONE = 0.9
BETA_TWO = 0.999
CORRECT_ONE = 1.0
CORRECT_TWO = 0.632304575228943
LEARN_RATE = 0.3
DECAY_RATE = 0.01
NEG_FILL = -1e30


def layer_norm(values, gain, shift):
    center = values - jnp.mean(values, axis=-1, keepdims=True)
    spread = jnp.mean(center * center, axis=-1, keepdims=True)
    return center * lax.rsqrt(spread + NORM_EPS) * gain + shift


def gelu_exact(values):
    return jax.nn.gelu(values, approximate=False)


def plain_shards(
    hidden_in,
    logits_in,
    cotangent,
    bucket_ids,
    seq_counts,
    key_mask,
    w_qkv,
    w_out,
    w_in,
    w_back,
    vectors,
    bias_in,
    m_qkv,
    m_out,
    m_in,
    m_back,
    m_vectors,
    m_bias,
    v_qkv,
    v_out,
    v_in,
    v_back,
    v_vectors,
    v_bias,
):
    tensor_parts = lax.axis_size("tensor")
    tensor_index = lax.axis_index("tensor")
    data_parts = lax.axis_size("dp")
    tokens_here = hidden_in.shape[0]
    share_rows = tokens_here // tensor_parts
    first_row = tensor_index * share_rows
    block_count = logits_in.shape[0]
    heads_here = logits_in.shape[1]
    block_len = logits_in.shape[2]
    model_width = hidden_in.shape[1]
    head_cols = w_qkv.shape[3]
    head_size = head_cols // heads_here
    hidden_cols = w_in.shape[2]
    score_scale = head_size ** (-0.5)
    bucket = bucket_ids[0]
    seq_span = jnp.where(
        bucket == 0, block_len // 4, jnp.where(bucket == 1, block_len // 2, block_len)
    )
    position = jnp.arange(tokens_here, dtype=jnp.int32)
    seq_flat = position // seq_span
    seq_of = seq_flat.reshape(block_count, block_len)
    live_keys = ((key_mask == 1) & (seq_flat < seq_counts[0])).reshape(block_count, block_len)
    allowed = (seq_of[:, :, None] == seq_of[:, None, :]) & live_keys[:, None, :]
    vec_all, bin_all = (
        lax.all_gather(vectors.astype(jnp.bfloat16), ("dp", "tensor"), axis=2, tiled=True),
        lax.all_gather(bias_in.astype(jnp.bfloat16), ("dp", "tensor"), axis=1, tiled=True),
    )
    vec_all = vec_all.astype(jnp.float32)
    bin_all = bin_all.astype(jnp.float32)

    def sum_forward(term_fn):
        return lax.psum_scatter(
            term_fn(jnp.int32(0), share_rows * lax.axis_size("tensor")).astype(jnp.bfloat16),
            "tensor",
            scatter_dimension=0,
            tiled=True,
        ).astype(jnp.float32)

    def sum_backward(term_fn):
        return lax.psum_scatter(
            term_fn(jnp.int32(0), share_rows * lax.axis_size("tensor")).astype(jnp.bfloat16),
            "tensor",
            scatter_dimension=0,
            tiled=True,
        ).astype(jnp.float32)

    def gather_rows(own_rows):
        return lax.all_gather(own_rows, "tensor", axis=0, tiled=True)

    def gather_grads(own_rows):
        return lax.all_gather(own_rows, "tensor", axis=0, tiled=True)

    def own_cols(vector):
        return lax.dynamic_slice_in_dim(vector, tensor_index * head_cols, head_cols)

    def place_cols(part_sum, total_len, offset):
        return lax.dynamic_update_slice(jnp.zeros((total_len,), jnp.float32), part_sum, (offset,))

    def blocked(matrix):
        return matrix.reshape(block_count, block_len, head_cols)

    def headed(matrix):
        return matrix.reshape(block_len, heads_here, head_size)

    def block_scores(query_b, keys_b, earlier_b):
        raw = jnp.einsum(
            "ihe,jhe->hij", headed(query_b), headed(keys_b), preferred_element_type=jnp.float32
        )
        return raw * score_scale + earlier_b.astype(jnp.float32)

    def attend_block(inputs):
        query_b, keys_b, values_b, earlier_b, allowed_b = inputs
        scores = block_scores(query_b, keys_b, earlier_b)
        row_top = jnp.max(jnp.where(allowed_b[None], scores, NEG_FILL), axis=-1, keepdims=True)
        unscaled = jnp.exp(jnp.where(allowed_b[None], scores - row_top, NEG_FILL))
        row_total = jnp.sum(unscaled, axis=-1, keepdims=True)
        row_total = jnp.where(row_total > 0.5, row_total, 1.0)
        probs_low = (unscaled / row_total).astype(jnp.bfloat16)
        mixed = jnp.einsum(
            "hij,jhe->ihe", probs_low, headed(values_b), preferred_element_type=jnp.float32
        )
        return (
            mixed.reshape(block_len, head_cols).astype(jnp.bfloat16),
            scores.astype(jnp.bfloat16),
            row_top,
            row_total,
        )

    def attend_back(inputs):
        query_b, keys_b, values_b, earlier_b, allowed_b, row_top, row_total, dmixed_b, dlater_b = (
            inputs
        )
        scores = block_scores(query_b, keys_b, earlier_b)
        unscaled = jnp.exp(jnp.where(allowed_b[None], scores - row_top, NEG_FILL))
        probs = unscaled / row_total
        probs_low = probs.astype(jnp.bfloat16)
        dmixed_heads = headed(dmixed_b)
        dvalues = jnp.einsum(
            "hij,ihe->jhe", probs_low, dmixed_heads, preferred_element_type=jnp.float32
        )
        dprobs = jnp.einsum(
            "ihe,jhe->hij", dmixed_heads, headed(values_b), preferred_element_type=jnp.float32
        )
        dlocal = probs * (dprobs - jnp.sum(probs * dprobs, axis=-1, keepdims=True))
        dscores = (dlocal + dlater_b.astype(jnp.float32)).astype(jnp.bfloat16)
        dquery = (
            jnp.einsum("hij,jhe->ihe", dscores, headed(keys_b), preferred_element_type=jnp.float32)
            * score_scale
        )
        dkeys = (
            jnp.einsum("hij,ihe->jhe", dscores, headed(query_b), preferred_element_type=jnp.float32)
            * score_scale
        )
        return (
            dquery.reshape(block_len, head_cols),
            dkeys.reshape(block_len, head_cols),
            dvalues.reshape(block_len, head_cols),
            dscores,
        )

    full_in = hidden_in
    own_in = lax.dynamic_slice_in_dim(hidden_in, first_row, share_rows, 0)
    earlier = logits_in
    records = []
    for layer_at in range(LAYERS):
        fetched = (
            lax.all_gather(w_qkv[layer_at].astype(jnp.bfloat16), "dp", axis=1, tiled=True),
            lax.all_gather(w_out[layer_at].astype(jnp.bfloat16), "dp", axis=1, tiled=True),
            lax.all_gather(w_in[layer_at].astype(jnp.bfloat16), "dp", axis=0, tiled=True),
            lax.all_gather(w_back[layer_at].astype(jnp.bfloat16), "dp", axis=1, tiled=True),
        )
        forward_wqkv, forward_wout, forward_win, forward_wback = fetched
        forward_vector = vec_all[layer_at]
        forward_query = (
            jnp.dot(full_in, forward_wqkv[0], preferred_element_type=jnp.float32)
            + own_cols(forward_vector[2])
        ).astype(jnp.bfloat16)
        forward_keys = jnp.dot(full_in, forward_wqkv[1], preferred_element_type=jnp.float32).astype(
            jnp.bfloat16
        )
        forward_values = (
            jnp.dot(full_in, forward_wqkv[2], preferred_element_type=jnp.float32)
            + own_cols(forward_vector[3])
        ).astype(jnp.bfloat16)
        forward_attn_out, stored, forward_row_top, forward_row_total = lax.map(
            attend_block,
            (
                blocked(forward_query),
                blocked(forward_keys),
                blocked(forward_values),
                earlier,
                allowed,
            ),
        )
        forward_attn_out = forward_attn_out.reshape(tokens_here, head_cols)

        def attn_term(begin_row, row_count):
            return jnp.dot(forward_attn_out, forward_wout, preferred_element_type=jnp.float32)

        forward_mid_pre = sum_forward(attn_term) + forward_vector[4] + own_in.astype(jnp.float32)
        mid_own = layer_norm(forward_mid_pre, forward_vector[0], forward_vector[5]).astype(
            jnp.bfloat16
        )
        forward_mid_full = gather_rows(mid_own)
        bias_here = lax.dynamic_slice_in_dim(
            bin_all[layer_at], tensor_index * hidden_cols, hidden_cols
        )
        forward_pre_act = (
            jnp.dot(forward_mid_full, forward_win, preferred_element_type=jnp.float32) + bias_here
        )
        forward_active = gelu_exact(forward_pre_act).astype(jnp.bfloat16)

        def ffn_term(begin_row, row_count):
            return jnp.dot(forward_active, forward_wback, preferred_element_type=jnp.float32)

        forward_out_pre = sum_forward(ffn_term) + forward_vector[6] + mid_own.astype(jnp.float32)
        out_own = layer_norm(forward_out_pre, forward_vector[1], forward_vector[7]).astype(
            jnp.bfloat16
        )
        forward_state = (
            forward_query,
            forward_keys,
            forward_values,
            forward_attn_out,
            forward_row_top,
            forward_row_total,
            forward_mid_pre,
            forward_mid_full,
            forward_pre_act,
            forward_out_pre,
        )
        out_own, stored, state = (out_own, stored, forward_state)
        records.append((full_in, earlier, fetched, state))
        earlier = stored
        own_in = out_own
        if layer_at + 1 < LAYERS:
            full_in = gather_rows(out_own)
    logits_out = earlier
    d_own = cotangent.astype(jnp.float32)
    d_later = jnp.zeros_like(logits_in)
    mat_grads = [None] * LAYERS
    vec_grads = [None] * LAYERS
    bin_grads = [None] * LAYERS
    for layer_at in reversed(range(LAYERS)):
        full_in, earlier, fetched, state = records[layer_at]
        wqkv = lax.all_gather(w_qkv[layer_at].astype(jnp.bfloat16), "dp", axis=1, tiled=True)
        wout = lax.all_gather(w_out[layer_at].astype(jnp.bfloat16), "dp", axis=1, tiled=True)
        win = lax.all_gather(w_in[layer_at].astype(jnp.bfloat16), "dp", axis=0, tiled=True)
        wback = lax.all_gather(w_back[layer_at].astype(jnp.bfloat16), "dp", axis=1, tiled=True)
        (
            query,
            keys,
            values,
            attn_out,
            backward_row_top,
            backward_row_total,
            mid_pre,
            mid_full,
            pre_act,
            out_pre,
        ) = state
        backward_vector = vec_all[layer_at]
        out_grad, gain_two, shift_two = jax.vjp(
            layer_norm, out_pre, backward_vector[1], backward_vector[7]
        )[1](d_own)
        d_ffn = gather_grads(out_grad.astype(jnp.bfloat16))
        active = gelu_exact(pre_act).astype(jnp.bfloat16)
        grad_back = jnp.einsum("tf,td->fd", active, d_ffn, preferred_element_type=jnp.float32)
        d_active = jnp.einsum("td,fd->tf", d_ffn, wback, preferred_element_type=jnp.float32)
        d_pre = jax.vjp(gelu_exact, pre_act)[1](d_active)[0].astype(jnp.bfloat16)
        grad_in = jnp.einsum("td,tf->df", mid_full, d_pre, preferred_element_type=jnp.float32)

        def mid_term(begin_row, row_count):
            return jnp.einsum("tf,df->td", d_pre, win, preferred_element_type=jnp.float32)

        mid_grad = sum_backward(mid_term) + out_grad
        attn_grad, gain_one, shift_one = jax.vjp(
            layer_norm, mid_pre, backward_vector[0], backward_vector[5]
        )[1](mid_grad)
        d_attn = gather_grads(attn_grad.astype(jnp.bfloat16))
        grad_out_proj = jnp.einsum(
            "tc,td->cd", attn_out, d_attn, preferred_element_type=jnp.float32
        )
        d_mixed = jnp.einsum("td,cd->tc", d_attn, wout, preferred_element_type=jnp.float32).astype(
            jnp.bfloat16
        )
        backward_dquery, backward_dkeys, backward_dvalues, backward_dscores = lax.map(
            attend_back,
            (
                blocked(query),
                blocked(keys),
                blocked(values),
                earlier,
                allowed,
                backward_row_top,
                backward_row_total,
                blocked(d_mixed),
                d_later,
            ),
        )
        backward_dquery = backward_dquery.reshape(tokens_here, head_cols).astype(jnp.bfloat16)
        backward_dkeys = backward_dkeys.reshape(tokens_here, head_cols).astype(jnp.bfloat16)
        backward_dvalues = backward_dvalues.reshape(tokens_here, head_cols).astype(jnp.bfloat16)
        grad_qkv = jnp.stack(
            [
                jnp.einsum(
                    "td,tc->dc", full_in, backward_dquery, preferred_element_type=jnp.float32
                ),
                jnp.einsum(
                    "td,tc->dc", full_in, backward_dkeys, preferred_element_type=jnp.float32
                ),
                jnp.einsum(
                    "td,tc->dc", full_in, backward_dvalues, preferred_element_type=jnp.float32
                ),
            ]
        )

        def input_term(begin_row, row_count):
            total_term = jnp.einsum(
                "tc,dc->td", backward_dquery, wqkv[0], preferred_element_type=jnp.float32
            )
            total_term = total_term + jnp.einsum(
                "tc,dc->td", backward_dkeys, wqkv[1], preferred_element_type=jnp.float32
            )
            return total_term + jnp.einsum(
                "tc,dc->td", backward_dvalues, wqkv[2], preferred_element_type=jnp.float32
            )

        in_grad = sum_backward(input_term) + attn_grad
        col_offset = tensor_index * head_cols
        vec_grad = jnp.stack(
            [
                gain_one,
                gain_two,
                place_cols(
                    jnp.sum(backward_dquery.astype(jnp.float32), axis=0), model_width, col_offset
                ),
                place_cols(
                    jnp.sum(backward_dvalues.astype(jnp.float32), axis=0), model_width, col_offset
                ),
                jnp.sum(attn_grad, axis=0),
                shift_one,
                jnp.sum(out_grad, axis=0),
                shift_two,
            ]
        )
        bin_grad = place_cols(
            jnp.sum(d_pre.astype(jnp.float32), axis=0),
            hidden_cols * tensor_parts,
            tensor_index * hidden_cols,
        )
        d_own, d_later, mats, vec_grad, bin_grad = (
            in_grad,
            backward_dscores,
            (grad_qkv, grad_out_proj, grad_in, grad_back),
            vec_grad,
            bin_grad,
        )
        totals = (
            lax.psum(mats[0].astype(jnp.bfloat16), "dp").astype(jnp.float32),
            lax.psum(mats[1].astype(jnp.bfloat16), "dp").astype(jnp.float32),
            lax.psum(mats[2].astype(jnp.bfloat16), "dp").astype(jnp.float32),
            lax.psum(mats[3].astype(jnp.bfloat16), "dp").astype(jnp.float32),
        )
        data_index = lax.axis_index("dp")
        mat_grads[layer_at] = tuple(
            (
                lax.dynamic_slice_in_dim(
                    whole,
                    data_index * (whole.shape[axis_at] // data_parts),
                    whole.shape[axis_at] // data_parts,
                    axis_at,
                )
                for whole, axis_at in zip(totals, (1, 1, 0, 1))
            )
        )
        vec_grads[layer_at] = vec_grad
        bin_grads[layer_at] = bin_grad
    grad_logits = d_later.astype(jnp.float32)
    vec_sum, bin_sum = (
        lax.psum_scatter(jnp.stack(vec_grads), ("dp", "tensor"), scatter_dimension=2, tiled=True),
        lax.psum_scatter(jnp.stack(bin_grads), ("dp", "tensor"), scatter_dimension=1, tiled=True),
    )
    grads_all = (
        jnp.stack([mat_grads[level_at][0] for level_at in range(LAYERS)]),
        jnp.stack([mat_grads[level_at][1] for level_at in range(LAYERS)]),
        jnp.stack([mat_grads[level_at][2] for level_at in range(LAYERS)]),
        jnp.stack([mat_grads[level_at][3] for level_at in range(LAYERS)]),
        vec_sum,
        bin_sum,
    )
    masters = (w_qkv, w_out, w_in, w_back, vectors, bias_in)
    firsts = (m_qkv, m_out, m_in, m_back, m_vectors, m_bias)
    seconds = (v_qkv, v_out, v_in, v_back, v_vectors, v_bias)
    decays = (DECAY_RATE, DECAY_RATE, DECAY_RATE, DECAY_RATE, 0.0, 0.0)
    moved = []
    for master, gradient, first_prev, second_prev, decay_rate in zip(
        masters, grads_all, firsts, seconds, decays
    ):
        moment_one = BETA_ONE * first_prev + (1.0 - BETA_ONE) * gradient
        moment_two = BETA_TWO * second_prev + (1.0 - BETA_TWO) * gradient * gradient
        update = (
            moment_one / CORRECT_ONE / (jnp.sqrt(moment_two / CORRECT_TWO) + ADAM_EPS)
            + decay_rate * master
        )
        moved.append((moment_one, update))
    weight_sq = jnp.stack(
        [jnp.sum((master * master).reshape(LAYERS, -1), axis=1) for master in masters]
    )
    update_sq = jnp.stack(
        [jnp.sum((moved_one[1] * moved_one[1]).reshape(LAYERS, -1), axis=1) for moved_one in moved]
    )
    weight_tot, update_tot = lax.psum((weight_sq, update_sq), ("dp", "tensor"))
    trust_all = jnp.sqrt(weight_tot) / jnp.sqrt(update_tot)
    new_params = tuple(
        (
            master
            - LEARN_RATE
            * trust_all[group_at].reshape((LAYERS,) + (1,) * (master.ndim - 1))
            * moved_one[1]
            for group_at, (master, moved_one) in enumerate(zip(masters, moved))
        )
    )
    return (
        own_in,
        logits_out,
        d_own,
        grad_logits,
        grads_all[0],
        grads_all[1],
        grads_all[2],
        grads_all[3],
        grads_all[4],
        grads_all[5],
        new_params[0],
        new_params[1],
        new_params[2],
        new_params[3],
        new_params[4],
        new_params[5],
        moved[0][0],
        moved[1][0],
        moved[2][0],
        moved[3][0],
        moved[4][0],
        moved[5][0],
        trust_all.T,
    )


MESH = pl.DeviceIdType.MESH
TILE = 256
LANES = 128
ROWS_MAT = 4
X_FIRST = (1,)
Z_AHEAD = 2
X_AHEAD = 3
SLOTS = ((1, 3), (2, 1), (2, 3), (3, 1), (3, 2), (4, 1), (5, 1))
Z_FIRST = ()
BACK_SLOTS = (
    (-9, -9, 0, 1, 2, 3, 4, 5, 6),
    (-9, -5, -4, -2, 0, 0, 1, 2, 3),
    (8,),
)


def dot_nn(left, right):
    return lax.dot_general(
        left, right, (((1,), (0,)), ((), ())), preferred_element_type=jnp.float32
    )


def dot_nt(left, right):
    return lax.dot_general(
        left, right, (((1,), (1,)), ((), ())), preferred_element_type=jnp.float32
    )


def norm_parts(values):
    center = values - jnp.mean(values, axis=-1, keepdims=True)
    spread = jnp.mean(center * center, axis=-1, keepdims=True)
    return center, lax.rsqrt(spread + NORM_EPS)


def step_kernel(
    data_parts,
    hidden_in,
    logits_in,
    cotangent,
    bucket,
    count,
    key_mask,
    vec_w,
    bias_w,
    vec_m,
    bias_m,
    vec_v,
    bias_v,
    lw_qkv,
    lw_out,
    lw_in,
    lw_back,
    lm_qkv,
    lm_out,
    lm_in,
    lm_back,
    lv_qkv,
    lv_out,
    lv_in,
    lv_back,
    hidden_out,
    logits_out,
    grad_hidden,
    grad_scores,
    sum_qkv,
    sum_out,
    sum_in,
    sum_back,
    small_out,
    norm_out,
    key_ids,
    small_in,
    w_q,
    w_o,
    w_i,
    w_b,
    scores,
    probs,
    h_full,
    m_full,
    active,
    attn,
    h_turn,
    m_turn,
    g_turn,
    o_turn,
    slope,
    qkv,
    x_own,
    y_own,
    d_qkv,
    d_keep,
    turn_v,
    turn_k,
    part,
    got_core,
    sum_chip,
    got_y,
    vec_got,
    vec_all,
    bin_all,
    small_acc,
    small_got,
    small_send,
    small_sum,
    pk_q,
    pk_o,
    pk_i,
    pk_b,
    rx_q,
    rx_o,
    rx_i,
    rx_b,
    rz_q,
    rz_o,
    rz_i,
    rz_b,
    fw_q,
    fw_o,
    fw_i,
    fw_b,
    fm_q,
    fm_o,
    fm_i,
    fm_b,
    fv_q,
    fv_o,
    fv_i,
    fv_b,
    norms,
    norm_send,
    norm_ten,
    norm_mid,
    norm_dp,
    load_sem,
    own_sem,
    zs_sem,
    zr_sem,
    xs_sem,
    xr_sem,
    core_s,
    core_r,
    ys_sem,
    yr_sem,
    gat_s,
    gat_r,
    vec_s,
    vec_r,
    sml_s,
    sml_r,
    gxs_sem,
    gxr_sem,
    gzs_sem,
    gzr_sem,
    fin_sem,
    out_sem,
    lamb_sem,
    ns_sem,
    nr_sem,
    credit,
):
    dp = lax.axis_index("dp")
    ten = lax.axis_index("tensor")
    cols_n = data_parts // 2
    side = lax.rem(dp, 2)
    place = dp // 2
    row_y = ten // 2
    core = lax.rem(ten, 2)
    across = dp + 1 - 2 * side
    core_mate = ten + 1 - 2 * core
    y_mate = lax.rem(ten + 2, 4)
    width = hidden_in.shape[1]
    tokens = hidden_in.shape[0]
    share = tokens // 4
    half = share // 2
    head_cols = qkv.shape[3]
    hidden_cols = slope.shape[2]
    cut = width // data_parts
    tiles = width // TILE
    f32 = jnp.float32
    b16 = jnp.bfloat16

    def along(step):
        return lax.rem(place + step, cols_n) * 2 + side

    def mult(value, by):
        return pl.multiple_of(value, by)

    def rdma(src, dst, send, recv, to_dp, to_ten):
        return pltpu.make_async_remote_copy(
            src_ref=src,
            dst_ref=dst,
            send_sem=send,
            recv_sem=recv,
            device_id=(to_dp, to_ten),
            device_id_type=MESH,
        )

    def region(kind, layer, dev):
        at = pl.ds(mult(dev * cut, cut), cut)
        if kind == 0:
            return w_q.at[layer, :, at, :]
        if kind == 1:
            return w_o.at[layer, :, at]
        if kind == 2:
            return w_i.at[layer, at, :]
        return w_b.at[layer, :, at]

    load_h = pltpu.make_async_copy(hidden_in, h_full, load_sem.at[0])
    load_s = pltpu.make_async_copy(logits_in.at[0], scores, load_sem.at[1])
    load_h.start()
    load_s.start()
    masters = (
        (lw_qkv, lw_out, lw_in, lw_back),
        (lm_qkv, lm_out, lm_in, lm_back),
        (lv_qkv, lv_out, lv_in, lv_back),
    )
    held = ((fw_q, fw_o, fw_i, fw_b), (fm_q, fm_o, fm_i, fm_b), (fv_q, fv_o, fv_i, fv_b))

    def lamb_load(kind, layer, which):
        return pltpu.make_async_copy(
            masters[which][kind].at[layer], held[which][kind], lamb_sem.at[which, kind]
        )

    def own_load(kind, layer):
        to = LAYERS - 1 - layer
        return pltpu.make_async_copy(masters[0][kind].at[layer], held[to][kind], own_sem.at[layer, kind])

    for layer in range(LAYERS):
        for kind in range(ROWS_MAT):
            own_load(kind, layer).start()

    barrier = pltpu.get_barrier_semaphore()

    def greet(step, carry):
        pl.semaphore_signal(
            barrier, inc=1, device_id=(lax.rem(dp + step, data_parts), ten), device_id_type=MESH
        )
        return carry

    lax.fori_loop(1, data_parts, greet, 0)
    for other in range(1, 4):
        pl.semaphore_signal(
            barrier, inc=1, device_id=(dp, lax.rem(ten + other, 4)), device_id_type=MESH
        )

    def w_x(kind, layer, from_place, col):
        dst = region(kind, layer, from_place * 2 + col)
        return rdma(
            dst,
            dst,
            xs_sem.at[layer, kind, from_place],
            xr_sem.at[layer, kind, from_place],
            across,
            ten,
        )

    def w_z(kind, layer, from_place, col, way):
        dst = region(kind, layer, from_place * 2 + col)
        which = lax.rem(col + side, 2)
        return rdma(
            dst,
            dst,
            zs_sem.at[layer, kind, from_place, which, (way + 1) // 2],
            zr_sem.at[layer, kind, from_place, which],
            dp + 2 * way,
            ten,
        )

    can_go = {1: place < cols_n - 1, -1: place > 0}

    def w_both_ways(kind, layer, col):
        for way in (1, -1):

            @pl.when(can_go[way])
            def _():
                w_z(kind, layer, place, col, way).start()

    def w_far(kind, layer, col, step):
        dst = region(kind, layer, place * 2 + col)
        which = lax.rem(col + side, 2)
        return rdma(
            dst,
            dst,
            zs_sem.at[layer, kind, step, which, 0],
            zr_sem.at[layer, kind, step, which],
            along(step),
            ten,
        )

    def w_event(kind, layer, hop):
        if kind in X_FIRST:
            w_x(kind, layer, place, 1 - side).wait_recv()
            for step in range(1, cols_n):
                w_far(kind, layer, 1 - side, step).start()
            return
        for way in (1, -1):
            came = place - hop * way

            @pl.when(came >= 0 if way == 1 else came < cols_n)
            def _():
                w_z(kind, layer, came, side, way).wait_recv()

                @pl.when(can_go[way])
                def _():
                    w_z(kind, layer, came, side, way).start()

                w_x(kind, layer, came, side).start()

    order = [(kind, layer) for layer in range(LAYERS) for kind in range(ROWS_MAT)]

    def w_own_z(index):
        if index < len(order):
            kind, layer = order[index]
            if kind in X_FIRST:
                for step in range(1, cols_n):
                    w_far(kind, layer, side, step).start()
            else:
                w_both_ways(kind, layer, side)

    def w_own_x(index):
        if index < len(order):
            w_x(*order[index], place, side).start()

    def w_own(index):
        kind, layer = order[index]
        own_load(kind, layer).wait()
        mine = region(kind, layer, dp)
        mine[...] = held[LAYERS - 1 - layer][kind][...].astype(b16)

    for index in range(X_AHEAD):
        w_own(index)
    for kind, slots in enumerate((rz_q, rz_o, rz_i, rz_b)):
        if kind in Z_FIRST:
            continue

        @pl.when(place == 0)
        def _():
            slots[0] = jnp.zeros(slots.shape[1:], b16)
            slots[3] = jnp.zeros(slots.shape[1:], b16)

        @pl.when(place == cols_n - 1)
        def _():
            slots[2] = jnp.zeros(slots.shape[1:], b16)
            slots[3] = jnp.zeros(slots.shape[1:], b16)

    owned = vec_w.shape[2]
    spread_row = lax.broadcasted_iota(jnp.int32, (owned, LANES), 0)
    spread_col = lax.broadcasted_iota(jnp.int32, (owned, LANES), 1)
    spread = jnp.where(spread_row + ten * owned == spread_col, 1.0, 0.0)
    lane_row = lax.broadcasted_iota(jnp.int32, (1, LANES), 1)
    not_owned = jnp.where(lane_row // owned == ten, 0.0, 1.0)
    small_in[...] = jnp.zeros_like(small_in)
    small_in[2] = jnp.ones_like(small_in[2])
    for which, (wide, narrow) in enumerate(((vec_w, bias_w), (vec_m, bias_m), (vec_v, bias_v))):
        for layer in range(LAYERS):
            rows = lax.dot_general(
                wide[layer],
                spread,
                (((1,), (0,)), ((), ())),
                precision=lax.Precision.HIGHEST,
                preferred_element_type=jnp.float32,
            )
            if which == 2:
                rows = rows + not_owned
            small_in[which, layer * 8 : layer * 8 + 8, :] = rows
            small_in[which, LAYERS * 8 + layer : LAYERS * 8 + layer + 1, :] = narrow[
                layer : layer + 1, :
            ]
    vec_got[ten, dp] = small_in[0].astype(b16)
    span_of = (tokens // 4, tokens // 2, tokens)
    per_key = jnp.where(
        bucket[0] == 0, 1.0 / span_of[0], jnp.where(bucket[0] == 1, 1.0 / span_of[1], 1.0 / span_of[2])
    ).astype(f32)
    key_at = lax.broadcasted_iota(jnp.int32, (1, tokens), 1).astype(f32)
    key_seq = jnp.floor(key_at * per_key)
    alive = (key_mask[...] == 1) & (key_seq < count[0].astype(f32))
    key_ids[0:1, :] = jnp.where(alive, key_seq, -1.0)

    pl.semaphore_wait(barrier, data_parts + 2)
    def vec_one(step):
        return rdma(
            vec_got.at[ten, dp],
            vec_got.at[ten, dp],
            vec_s.at[step - 1],
            vec_r.at[step - 1],
            lax.rem(dp + step, data_parts),
            ten,
        )

    def vec_go(step, carry):
        vec_one(step).start()
        return carry

    lax.fori_loop(1, data_parts, vec_go, 0)

    for index in range(X_AHEAD):
        if index < Z_AHEAD:
            w_own_z(index)
        w_own_x(index)

    for index in range(X_AHEAD, len(order)):
        w_own(index)

    events = [
        (index, hop)
        for index in range(len(order))
        for hop in range(1, 2 if order[index][0] in X_FIRST else cols_n)
    ]
    passed = [0]

    def pass_on(layer_at, kind_at, hop_at):
        goal = (layer_at * ROWS_MAT + kind_at, hop_at)
        while passed[0] < len(events) and events[passed[0]] <= goal:
            index, hop = events[passed[0]]
            w_event(*order[index], hop)
            if hop == cols_n - 1 or order[index][0] in X_FIRST:
                w_own_z(index + Z_AHEAD)
                w_own_x(index + X_AHEAD)
            passed[0] += 1

    def have(layer, kind):
        pass_on(layer, kind, cols_n)
        if kind in X_FIRST:
            for step in range(1, cols_n):
                for col in (side, 1 - side):
                    w_far(kind, layer, col, step).wait_recv()
        else:
            for from_place in range(cols_n):
                w_x(kind, layer, from_place, 1 - side).wait_recv()

    def w_finish():
        for kind, layer in order:
            if kind in X_FIRST:
                w_x(kind, layer, place, side).wait_send()
                for step in range(1, cols_n):
                    for col in (side, 1 - side):
                        w_far(kind, layer, col, step).wait_send()
                continue
            for from_place in range(cols_n):
                w_x(kind, layer, from_place, side).wait_send()

                @pl.when(can_go[1] & (from_place <= place))
                def _():
                    w_z(kind, layer, from_place, side, 1).wait_send()

                @pl.when(can_go[-1] & (from_place >= place))
                def _():
                    w_z(kind, layer, from_place, side, -1).wait_send()

    def vec_wait(step, carry):
        vec_one(step).wait_send()
        vec_one(step).wait_recv()
        return carry

    lax.fori_loop(1, data_parts, vec_wait, 0)

    def vec_two(step):
        return rdma(
            vec_got.at[ten],
            vec_got.at[ten],
            vec_s.at[data_parts - 2 + step],
            vec_r.at[data_parts - 2 + step],
            dp,
            lax.rem(ten + step, 4),
        )

    for step in range(1, 4):
        vec_two(step).start()
    for step in range(1, 4):
        vec_two(step).wait_send()
        vec_two(step).wait_recv()
    for dev in range(data_parts):
        total = vec_got[0, dev].astype(f32)
        for other in range(1, 4):
            total = total + vec_got[other, dev].astype(f32)
        vec_all[:, dev * LANES : (dev + 1) * LANES] = total[0 : LAYERS * 8]
    for piece in range(hidden_cols // LANES):
        got = vec_got[piece % 4, ten * 2 + piece // 4].astype(f32)
        bin_all[:, piece * LANES : (piece + 1) * LANES] = got[LAYERS * 8 : LAYERS * 8 + 8]

    def vec_row(layer, row):
        return vec_all[layer * 8 + row : layer * 8 + row + 1, :]

    def block_rows(which_y, which_core):
        return pl.ds(mult((which_y * 2 + which_core) * share, share), share)

    far_block = block_rows(1 - row_y, 1 - core)
    mate_block = block_rows(row_y, 1 - core)
    over_block = block_rows(1 - row_y, core)
    own_block = block_rows(row_y, core)

    def tile_cols(tile):
        return pl.ds(mult(tile * TILE, TILE), TILE)

    def send_core(tile, which):
        rows = far_block if which == 0 else mate_block
        return rdma(
            part.at[rows, tile_cols(tile)],
            got_core.at[which, :, tile_cols(tile)],
            core_s.at[tile, which],
            core_r.at[tile, which],
            dp,
            core_mate,
        )

    def send_y(tile):
        return rdma(
            sum_chip.at[:, tile_cols(tile)],
            got_y.at[:, tile_cols(tile)],
            ys_sem.at[tile],
            yr_sem.at[tile],
            dp,
            y_mate,
        )

    def add_core(tile):
        send_core(tile, 0).wait_recv()
        at = tile_cols(tile)
        sum_chip[:, at] = (
            part[over_block, at].astype(f32) + got_core[0, :, at].astype(f32)
        ).astype(b16)
        send_y(tile).start()

    def sum_start(tile_fn):
        def one(tile, carry):
            part[:, tile_cols(tile)] = tile_fn(tile).astype(b16)
            send_core(tile, 0).start()
            send_core(tile, 1).start()

            @pl.when(tile > 0)
            def _():
                add_core(tile - 1)

            return carry

        lax.fori_loop(0, tiles, one, 0)
        add_core(tiles - 1)

    def sum_end():
        for tile in range(tiles):
            send_core(tile, 1).wait_recv()
            send_y(tile).wait_recv()
        for tile in range(tiles):
            send_core(tile, 0).wait_send()
            send_core(tile, 1).wait_send()
            send_y(tile).wait_send()

    def sum_rows(which):
        at = pl.ds(which * half, half)
        mine = pl.ds(mult(ten * share + which * half, half), half)
        return (
            part[mine, :].astype(f32) + got_core[1, at, :].astype(f32) + got_y[at, :].astype(f32)
        )

    def gat_copy(buf, which, kind):
        if kind == 2:
            rows = pl.ds(mult(y_mate * share + which * half, half), half)
        else:
            rows = pl.ds(mult(ten * share + which * half, half), half)
        return rdma(
            buf.at[rows],
            buf.at[rows],
            gat_s.at[which, kind],
            gat_r.at[which, kind],
            dp,
            y_mate if kind == 1 else core_mate,
        )

    def gat_start(buf, which):
        gat_copy(buf, which, 1).start()
        gat_copy(buf, which, 0).start()

    def gat_end(buf):
        for which in range(2):
            gat_copy(buf, which, 1).wait_recv()
            gat_copy(buf, which, 2).start()
        for which in range(2):
            gat_copy(buf, which, 0).wait_recv()
            gat_copy(buf, which, 2).wait_recv()
        for which in range(2):
            for kind in range(3):
                gat_copy(buf, which, kind).wait_send()

    def own_rows(which):
        return pl.ds(mult(ten * share + which * half, half), half)

    def turn(src, dst, layer):
        def one(at, carry):
            dst[layer, tile_cols(at), :] = src[:, tile_cols(at)].T
            return carry

        lax.fori_loop(0, src.shape[1] // TILE, one, 0)

    lane = lax.broadcasted_iota(jnp.int32, (1, LANES), 1)
    low_lanes = jnp.where(lane < 64, 1.0, 0.0).astype(b16)
    high_lanes = jnp.where(lane < 64, 0.0, 1.0).astype(b16)
    lane_masks = (low_lanes, high_lanes)
    scale = 0.125
    score_rows = 256
    pairs = head_cols // LANES

    def pair_cols(pair):
        return slice(pair * LANES, (pair + 1) * LANES)

    def attend(layer, pair):
        def one(step, carry):
            rows = pl.ds(mult(step * score_rows, score_rows), score_rows)
            at = slice(pair * LANES, (pair + 1) * LANES)
            queries = qkv[layer, 0, rows, at]
            keys = qkv[layer, 1, :, at]
            values = qkv[layer, 2, :, at]
            row = lax.broadcasted_iota(jnp.int32, (score_rows, 1), 0) + step * score_rows
            allowed = jnp.floor(row.astype(f32) * per_key) == key_ids[0:1, :]
            mixed = jnp.zeros((score_rows, LANES), f32)
            for head in range(2):
                raw = dot_nt(queries, keys * lane_masks[head])
                full = raw * scale + scores[pair * 2 + head, rows, :].astype(f32)
                scores[pair * 2 + head, rows, :] = full.astype(b16)
                top = jnp.max(jnp.where(allowed, full, NEG_FILL), axis=-1, keepdims=True)
                weight = jnp.exp(jnp.where(allowed, full - top, NEG_FILL))
                total = jnp.sum(weight, axis=-1, keepdims=True)
                total = jnp.where(total > 0.5, total, 1.0)
                low = (weight * (1.0 / total)).astype(b16)
                probs[layer, pair * 2 + head, rows, :] = low
                mixed = mixed + dot_nn(low, values * lane_masks[head])
            attn[rows, at] = mixed.astype(b16)
            return carry

        lax.fori_loop(0, tokens // score_rows, one, 0)

    def attend_back(layer, first, pairs_of):
        def pair_one(pair, carry):
            at = pair_cols(pair)
            turn_v[...] = jnp.zeros_like(turn_v)
            turn_k[...] = jnp.zeros_like(turn_k)

            def one(step, inner):
                rows = pl.ds(mult(step * score_rows, score_rows), score_rows)
                queries = qkv[layer, 0, rows, at]
                keys = qkv[layer, 1, :, at]
                values = qkv[layer, 2, :, at]
                grads = attn[rows, at]
                turned_q = queries.T
                turned_g = grads.T
                d_query = jnp.zeros((score_rows, LANES), f32)
                for head in range(2):
                    low = probs[layer, pair * 2 + head, rows, :]
                    prob = low.astype(f32)
                    d_prob = dot_nt(grads, values * lane_masks[head])
                    inner_sum = jnp.sum(prob * d_prob, axis=-1, keepdims=True)
                    d_score = prob * (d_prob - inner_sum)
                    if not first:
                        d_score = d_score + scores[pair * 2 + head, rows, :].astype(f32)
                    d_low = d_score.astype(b16)
                    scores[pair * 2 + head, rows, :] = d_low
                    d_query = d_query + dot_nn(d_low, keys * lane_masks[head])
                    part_rows = slice(head * 64, head * 64 + 64)
                    turn_v[part_rows, :] += dot_nn(turned_g[part_rows, :], low)
                    turn_k[part_rows, :] += dot_nn(turned_q[part_rows, :], d_low)
                d_qkv[0, rows, at] = (d_query * scale).astype(b16)
                return inner

            lax.fori_loop(0, tokens // score_rows, one, 0)
            d_qkv[1, :, at] = (turn_k[...] * scale).T.astype(b16)
            d_qkv[2, :, at] = turn_v[...].T.astype(b16)
            return carry

        for pair in pairs_of:
            pair_one(pair, 0)

    own_cols = pl.ds(mult(ten * head_cols, head_cols), head_cols)
    small_acc[...] = jnp.zeros_like(small_acc)
    load_h.wait()
    load_s.wait()
    for layer in range(LAYERS):
        have(layer, 0)
        for which in range(3):
            product = dot_nn(h_full[...], w_q[layer, which])
            if which == 0:
                product = product + vec_all[layer * 8 + 2 : layer * 8 + 3, own_cols]
            if which == 2:
                product = product + vec_all[layer * 8 + 3 : layer * 8 + 4, own_cols]
            qkv[layer, which] = product.astype(b16)
        pass_on(layer, *SLOTS[0])
        attend(layer, 0)
        pass_on(layer, *SLOTS[1])
        attend(layer, 1)
        have(layer, 1)
        sum_start(lambda tile: dot_nn(attn[...], w_o[layer, :, tile_cols(tile)]))
        turn(attn, o_turn, layer)
        turn(h_full, h_turn, layer)
        pass_on(layer, *SLOTS[2])
        sum_end()
        for which in range(2):
            at = pl.ds(which * half, half)
            mid = sum_rows(which) + vec_row(layer, 4) + h_full[own_rows(which), :].astype(f32)
            x_own[layer, at, :] = mid
            center, rate = norm_parts(mid)
            m_full[own_rows(which), :] = (
                center * rate * vec_row(layer, 0) + vec_row(layer, 5)
            ).astype(b16)
            gat_start(m_full, which)
        pass_on(layer, *SLOTS[3])
        gat_end(m_full)

        def ffn_tile(tile, carry):
            at = tile_cols(tile)
            pre = dot_nn(m_full[...], w_i[layer, :, at]) + bin_all[layer : layer + 1, at]
            cumul = 0.5 * (1.0 + lax.erf(pre * 0.7071067811865476))
            dens = jnp.exp(-0.5 * pre * pre) * 0.3989422804014327
            active[:, at] = (pre * cumul).astype(b16)
            slope[layer, :, at] = (cumul + pre * dens).astype(b16)
            return carry

        have(layer, 2)
        pass_on(layer, *SLOTS[4])
        lax.fori_loop(0, hidden_cols // TILE, ffn_tile, 0)
        turn(m_full, m_turn, layer)
        have(layer, 3)
        sum_start(lambda tile: dot_nn(active[...], w_b[layer, :, tile_cols(tile)]))
        turn(active, g_turn, layer)
        pass_on(layer, *SLOTS[5])
        sum_end()
        for which in range(2):
            at = pl.ds(which * half, half)
            late = sum_rows(which) + vec_row(layer, 6) + m_full[own_rows(which), :].astype(f32)
            y_own[layer, at, :] = late
            center, rate = norm_parts(late)
            result = (center * rate * vec_row(layer, 1) + vec_row(layer, 7)).astype(b16)
            h_full[own_rows(which), :] = result
            if layer + 1 < LAYERS:
                gat_start(h_full, which)
        if layer + 1 < LAYERS:
            pass_on(layer, *SLOTS[6])
            gat_end(h_full)

    out_logits = pltpu.make_async_copy(scores, logits_out, out_sem.at[0])
    out_logits.start()
    all_own = pl.ds(mult(ten * share, share), share)
    out_hidden = pltpu.make_async_copy(h_full.at[all_own], hidden_out, out_sem.at[2])
    out_hidden.start()
    load_c = pltpu.make_async_copy(cotangent, sum_chip, out_sem.at[3])
    load_c.start()
    w_finish()

    packs = (pk_q, pk_o, pk_i, pk_b)
    got_x = (rx_q, rx_o, rx_i, rx_b)
    got_z = (rz_q, rz_o, rz_i, rz_b)
    sums = (sum_qkv, sum_out, sum_in, sum_back)

    def turn_of(turn_at):
        upper = place // 2
        inner = upper * (cols_n - 1) + (1 - 2 * upper) * place
        pairs_of = turn_at * (turn_at - 1)
        swing = 2 * turn_at - pairs_of // 2 - pairs_of * (turn_at - 2) // 3
        at = (1 - inner) * (3 - turn_at) + inner * swing
        return upper * (cols_n - 1) + (1 - 2 * upper) * at

    at_end = (place == 0) | (place == cols_n - 1)

    def g_x(kind, at):
        first = kind not in Z_FIRST
        return rdma(
            packs[kind].at[at, 1 - side],
            got_x[kind].at[at if first else 0],
            gxs_sem.at[kind, at],
            gxr_sem.at[kind, at],
            across,
            ten,
        )

    def g_z(kind, at):
        far = (at - place) * (at - place) // 9
        to = (1 - far) * at + far * (place + 1 - 2 * (place // 2))
        slot = (1 - far) * (lax.rem(at - place + cols_n, cols_n) - 1) + far * 3
        return rdma(
            packs[kind].at[at, side],
            got_z[kind].at[slot],
            gzs_sem.at[kind, at],
            gzr_sem.at[kind, slot],
            to * 2 + side,
            ten,
        )

    def g_z_came(kind, slot):
        copy = rdma(
            packs[kind].at[0, side],
            got_z[kind].at[slot],
            gzs_sem.at[kind, 0],
            gzr_sem.at[kind, slot],
            dp,
            ten,
        )
        comes = (place > 0, place >= 0, place < cols_n - 1, jnp.logical_not(at_end))[slot]

        @pl.when(comes)
        def _():
            copy.wait_recv()

    def g_far(kind, step):
        to = lax.rem(place + step, cols_n)
        return rdma(
            packs[kind].at[to],
            got_z[kind].at[step - 1],
            gzs_sem.at[kind, step],
            gzr_sem.at[kind, step - 1],
            to * 2 + side,
            ten,
        )

    def g_free(kind, layer):
        add_upto(layer, (3 - kind) * cols_n + cols_n - 1)
        for turn_at in range(cols_n - 1):
            at = turn_of(turn_at)
            if kind in Z_FIRST:
                g_far(kind, turn_at + 1).wait_send()
            else:
                g_z(kind, at).wait_send()
                g_x(kind, at).wait_send()
        g_x(kind, place).wait_send()

    def give_credit(kind):
        pl.semaphore_signal(
            credit.at[0, kind], inc=1, device_id=(across, ten), device_id_type=MESH
        )
        if kind in Z_FIRST:
            for step in range(1, cols_n):
                pl.semaphore_signal(
                    credit.at[1, kind], inc=1, device_id=(along(step), ten), device_id_type=MESH
                )
            return

        for hop in (2, -2, 1, -1):

            @pl.when(place < cols_n - hop if hop > 0 else place >= -hop)
            def _():
                pl.semaphore_signal(
                    credit.at[1, kind], inc=1, device_id=(dp + 2 * hop, ten), device_id_type=MESH
                )

    def take_credit_x(kind):
        pl.semaphore_wait(credit.at[0, kind], 1)

    def take_credit_z(kind):
        if kind in Z_FIRST:
            pl.semaphore_wait(credit.at[1, kind], cols_n - 1)
            return

        @pl.when(at_end)
        def _():
            pl.semaphore_wait(credit.at[1, kind], 2)

        @pl.when(jnp.logical_not(at_end))
        def _():
            pl.semaphore_wait(credit.at[1, kind], 3)

    def chunks_of(kind):
        if kind == 0:
            return [(which,) for which in range(3)]
        if kind == 3:
            return [(pl.ds(piece * 256, 256),) for piece in range(hidden_cols // 256)]
        return [()]

    g_order = [
        (kind, layer, turn_at)
        for layer in reversed(range(LAYERS))
        for kind in (3, 2, 1, 0)
        for turn_at in range(cols_n)
    ]
    added = [0]

    def add_event(kind, layer, turn_at):
        if layer + 1 < LAYERS and turn_at == 0 and kind not in Z_FIRST:
            take_credit_z(kind)
        at = turn_of(turn_at)
        last = turn_at + 1 == cols_n
        if kind in Z_FIRST:
            if last:
                if layer + 1 < LAYERS:
                    take_credit_x(kind)
                for step in range(1, cols_n):
                    g_far(kind, step).wait_recv()
                for piece in chunks_of(kind):
                    ours = (at, 1 - side) + piece
                    total = packs[kind][ours].astype(f32)
                    for step in range(1, cols_n):
                        total = total + got_z[kind][(step - 1, 1 - side) + piece].astype(f32)
                    packs[kind][ours] = total.astype(b16)
                g_x(kind, at).start()
            return
        if last:
            return
        g_x(kind, at).wait_recv()
        passing = turn_at == cols_n - 2
        if passing:
            g_z_came(kind, 3)
        for piece in chunks_of(kind):
            ours = (at, side) + piece
            total = packs[kind][ours].astype(f32) + got_x[kind][(at,) + piece].astype(f32)
            if passing:
                total = total + got_z[kind][(3,) + piece].astype(f32)
            packs[kind][ours] = total.astype(b16)
        g_z(kind, at).start()

    def add_upto(layer_at, index):
        index = (LAYERS - 1 - layer_at) * 4 * cols_n + index
        while added[0] <= min(index, len(g_order) - 1):
            add_event(*g_order[added[0]])
            added[0] += 1

    def lamb_update(weight, first, second, gradient, decay):
        moment_one = BETA_ONE * first + (1.0 - BETA_ONE) * gradient
        moment_two = BETA_TWO * second + (1.0 - BETA_TWO) * gradient * gradient
        return (
            moment_one / CORRECT_ONE / (jnp.sqrt(moment_two / CORRECT_TWO) + ADAM_EPS)
            + decay * weight
        )

    def note_norm(row, values):
        norms[row : row + 1, 0 : values.shape[-1]] += jnp.sum(
            values * values, axis=0, keepdims=True
        )

    def g_end(kind, layer):
        add_upto(layer, (3 - kind) * cols_n + cols_n - 1)
        g_x(kind, place).wait_recv()
        if kind not in Z_FIRST:
            for slot in range(3):
                g_z_came(kind, slot)
        for which in range(3):
            if which or layer + 1 < LAYERS:
                lamb_load(kind, layer, which).wait()
        for piece in chunks_of(kind):
            total = packs[kind][(place, side) + piece].astype(f32)
            if kind in Z_FIRST:
                total = total + got_x[kind][(0,) + piece].astype(f32)
            else:
                total = total + got_x[kind][(place,) + piece].astype(f32)
            if kind in Z_FIRST:
                for step in range(1, cols_n):
                    total = total + got_z[kind][(step - 1, side) + piece].astype(f32)
            else:
                for slot in range(3):
                    total = total + got_z[kind][(slot,) + piece].astype(f32)
            here = piece if piece else (slice(None),)
            weight = held[0][kind][here]
            step_by = lamb_update(
                weight, held[1][kind][here], held[2][kind][here], total, DECAY_RATE
            )
            packs[kind][(place, side) + piece] = total.astype(b16)
            note_norm((layer * 4 + kind) * 2, weight)
            note_norm((layer * 4 + kind) * 2 + 1, step_by)
        fin_copy(kind, layer).start()
        if layer:
            give_credit(kind)
            for which in range(3):
                lamb_load(kind, layer - 1, which).start()

    def fin_copy(kind, layer):
        return pltpu.make_async_copy(
            packs[kind].at[place, side], sums[kind].at[layer], fin_sem.at[kind]
        )

    def g_x_go(kind, layer, turn_at, at):
        if kind in Z_FIRST:
            return
        if layer:
            g_x(kind, at).start()
            return

        @pl.when(turn_at < cols_n - 1)
        def _():
            g_x(kind, at).start()

    def pair_rows(at):
        return pl.ds(mult(at * 2 * cut, 2 * cut), 2 * cut)

    def grad_back(layer):
        if layer + 1 < LAYERS:
            fin_copy(3, layer + 1).wait()
            (take_credit_z if 3 in Z_FIRST else take_credit_x)(3)

        def one(turn_at, carry):
            at = turn_of(turn_at)
            for piece in range(hidden_cols // 512):
                rows = slice(piece * 512, (piece + 1) * 512)
                value = dot_nn(g_turn[layer, rows, :], m_full[:, pair_rows(at)]).astype(b16)
                pk_b[at, 0, rows, :] = value[:, :cut]
                pk_b[at, 1, rows, :] = value[:, cut:]
            g_x_go(3, layer, turn_at, at)
            return carry

        lax.fori_loop(0, cols_n, one, 0)
        if 3 in Z_FIRST:
            for step in range(1, cols_n):
                g_far(3, step).start()

    def grad_in(layer):
        if layer + 1 < LAYERS:
            fin_copy(2, layer + 1).wait()
            (take_credit_z if 2 in Z_FIRST else take_credit_x)(2)

        def one(turn_at, carry):
            at = turn_of(turn_at)
            for piece in range(hidden_cols // 512):
                cols = slice(piece * 512, (piece + 1) * 512)
                value = dot_nn(m_turn[layer, pair_rows(at), :], active[:, cols]).astype(b16)
                pk_i[at, 0, :, cols] = value[:cut]
                pk_i[at, 1, :, cols] = value[cut:]
            g_x_go(2, layer, turn_at, at)
            return carry

        lax.fori_loop(0, cols_n, one, 0)
        if 2 in Z_FIRST:
            for step in range(1, cols_n):
                g_far(2, step).start()

    def grad_out(layer):
        if layer + 1 < LAYERS:
            fin_copy(1, layer + 1).wait()
            (take_credit_z if 1 in Z_FIRST else take_credit_x)(1)

        def one(turn_at, carry):
            at = turn_of(turn_at)
            value = dot_nn(o_turn[layer], h_full[:, pair_rows(at)]).astype(b16)
            pk_o[at, 0] = value[:, :cut]
            pk_o[at, 1] = value[:, cut:]
            g_x_go(1, layer, turn_at, at)
            return carry

        lax.fori_loop(0, cols_n, one, 0)
        if 1 in Z_FIRST:
            for step in range(1, cols_n):
                g_far(1, step).start()

    def grad_qkv(layer):
        if layer + 1 < LAYERS:
            fin_copy(0, layer + 1).wait()
            (take_credit_z if 0 in Z_FIRST else take_credit_x)(0)

        def one(turn_at, carry):
            at = turn_of(turn_at)
            for which in range(3):
                value = dot_nn(h_turn[layer, pair_rows(at), :], d_qkv[which]).astype(b16)
                pk_q[at, 0, which] = value[:cut]
                pk_q[at, 1, which] = value[cut:]
            g_x_go(0, layer, turn_at, at)
            return carry

        lax.fori_loop(0, cols_n, one, 0)
        if 0 in Z_FIRST:
            for step in range(1, cols_n):
                g_far(0, step).start()

    def norm_back(kept, upstream, gain):
        center, rate = norm_parts(kept)
        unit = center * rate
        scaled = upstream * gain
        down = rate * (
            scaled
            - jnp.mean(scaled, axis=-1, keepdims=True)
            - unit * jnp.mean(scaled * unit, axis=-1, keepdims=True)
        )
        return down, unit

    def note(row, values):
        small_acc[row : row + 1, :] += jnp.sum(values, axis=0, keepdims=True)

    norms[...] = jnp.zeros_like(norms)
    for kind in range(ROWS_MAT):
        for which in (1, 2):
            lamb_load(kind, LAYERS - 1, which).start()
    load_c.wait()
    for layer in reversed(range(LAYERS)):
        last = layer + 1 == LAYERS
        base = layer * 8
        for which in range(2):
            at = pl.ds(which * half, half)
            upstream = sum_chip[at, :].astype(f32) if last else grad_hidden[at, :]
            down, unit = norm_back(y_own[layer, at, :], upstream, vec_row(layer, 1))
            note(base + 1, upstream * unit)
            note(base + 7, upstream)
            note(base + 6, down)
            d_keep[at, :] = down
            m_full[own_rows(which), :] = down.astype(b16)
            gat_start(m_full, which)
        marks = BACK_SLOTS[0 if last else 1]
        add_upto(layer, marks[0])
        if not last:
            g_free(3, layer + 1)
            g_end(3, layer + 1)
        gat_end(m_full)
        grad_back(layer)
        add_upto(layer, marks[1])

        def slope_tile(tile, carry):
            at = tile_cols(tile)
            d_active = dot_nt(m_full[...], w_b[layer, at, :])
            d_pre = (d_active * slope[layer, :, at].astype(f32)).astype(b16)
            active[:, at] = d_pre
            small_acc[LAYERS * 8 + layer : LAYERS * 8 + layer + 1, at] = jnp.sum(
                d_pre.astype(f32), axis=0, keepdims=True
            )
            return carry

        lax.fori_loop(0, hidden_cols // TILE, slope_tile, 0)
        sum_start(lambda tile: dot_nt(active[...], w_i[layer, tile_cols(tile), :]))
        add_upto(layer, marks[2])
        if not last:
            g_free(2, layer + 1)
            g_end(2, layer + 1)
        grad_in(layer)
        add_upto(layer, marks[3])
        sum_end()
        if last:
            out_hidden.wait()
        for which in range(2):
            at = pl.ds(which * half, half)
            upstream = sum_rows(which) + d_keep[at, :]
            down, unit = norm_back(x_own[layer, at, :], upstream, vec_row(layer, 0))
            note(base + 0, upstream * unit)
            note(base + 5, upstream)
            note(base + 4, down)
            d_keep[at, :] = down
            h_full[own_rows(which), :] = down.astype(b16)
            gat_start(h_full, which)
        add_upto(layer, marks[4])
        gat_end(h_full)
        if not last:
            g_free(1, layer + 1)
            g_end(1, layer + 1)
        attn[...] = dot_nt(h_full[...], w_o[layer]).astype(b16)
        grad_out(layer)
        if last:
            out_logits.wait()
        add_upto(layer, marks[5])
        attend_back(layer, last, (0,))
        add_upto(layer, marks[6])
        attend_back(layer, last, (1,))
        add_upto(layer, marks[7])
        small_acc[base + 2 : base + 3, own_cols] = jnp.sum(
            d_qkv[0].astype(f32), axis=0, keepdims=True
        )
        small_acc[base + 3 : base + 4, own_cols] = jnp.sum(
            d_qkv[2].astype(f32), axis=0, keepdims=True
        )

        def input_tile(tile):
            rows = tile_cols(tile)
            total = dot_nt(d_qkv[0], w_q[layer, 0, rows, :])
            total = total + dot_nt(d_qkv[1], w_q[layer, 1, rows, :])
            return total + dot_nt(d_qkv[2], w_q[layer, 2, rows, :])

        sum_start(input_tile)
        if not last:
            g_free(0, layer + 1)
            g_end(0, layer + 1)
        grad_qkv(layer)
        if layer == 0:
            for kind in (3, 2, 1, 0):
                if kind not in Z_FIRST:
                    g_x(kind, place).start()
        add_upto(layer, marks[8])
        sum_end()
        for which in range(2):
            at = pl.ds(which * half, half)
            result = sum_rows(which) + d_keep[at, :]
            grad_hidden[at, :] = result

    out_scores = pltpu.make_async_copy(scores, grad_scores, out_sem.at[1])
    out_scores.start()

    small_got[ten] = small_acc[...]

    def small_one(step):
        return rdma(
            small_acc,
            small_got.at[ten],
            sml_s.at[step - 1],
            sml_r.at[step - 1],
            dp,
            lax.rem(ten + step, 4),
        )

    for step in range(1, 4):
        small_one(step).start()
    add_upto(0, BACK_SLOTS[2][0])
    for step in range(1, 4):
        small_one(step).wait_recv()
    mat_rows = LAYERS * 8
    for dev in range(data_parts):
        cols = slice(dev * LANES, (dev + 1) * LANES)
        total = small_got[0, 0:mat_rows, cols]
        for other in range(1, 4):
            total = total + small_got[other, 0:mat_rows, cols]
        small_send[dev, 0:mat_rows, :] = total
        from_cols = pl.ds(mult(((dev % 2) * 4 + ten) * LANES, LANES), LANES)
        small_send[dev, mat_rows : mat_rows + 8, :] = small_got[
            dev // 2, mat_rows : mat_rows + 8, from_cols
        ]

    def small_two(step):
        to = lax.rem(dp + step, data_parts)
        return rdma(
            small_send.at[to],
            small_sum.at[step - 1],
            sml_s.at[2 + step],
            sml_r.at[2 + step],
            to,
            ten,
        )

    def small_go(step, carry):
        small_two(step).start()
        return carry

    lax.fori_loop(1, data_parts, small_go, 0)
    add_upto(0, 4 * cols_n - 1)
    g_end(3, 0)
    g_end(2, 0)
    g_end(1, 0)
    small_out[...] = small_send[dp]

    def small_wait(step, carry):
        small_two(step).wait_recv()
        small_two(step).wait_send()
        small_out[...] += small_sum[step - 1]
        return carry

    lax.fori_loop(1, data_parts, small_wait, 0)
    for step in range(1, 4):
        small_one(step).wait_send()
    g_end(0, 0)

    row_at = lax.broadcasted_iota(jnp.int32, (24, LANES), 0)
    lane_at = lax.broadcasted_iota(jnp.int32, (24, LANES), 1)
    in_share = (row_at >= mat_rows) | (lane_at // (width // data_parts // 4) == ten)
    small_grad = jnp.where(in_share & (row_at < mat_rows + LAYERS), small_out[...], 0.0)
    small_step = lamb_update(small_in[0, 0:24], small_in[1, 0:24], small_in[2, 0:24], small_grad, 0.0)
    norm_send[0:mat_rows, :] = jnp.broadcast_to(
        jnp.sum(norms[...], axis=-1, keepdims=True), (mat_rows, LANES)
    )
    for layer in range(LAYERS):
        for group, rows in enumerate(
            (slice(layer * 8, layer * 8 + 8), slice(mat_rows + layer, mat_rows + layer + 1))
        ):
            for which, values in enumerate((small_in[0, rows], small_step[rows])):
                total = jnp.sum(
                    jnp.sum(values * values, axis=0, keepdims=True), axis=1, keepdims=True
                )
                row = mat_rows + (layer * 2 + group) * 2 + which
                norm_send[row : row + 1, :] = jnp.broadcast_to(total, (1, LANES))

    def norm_one(step):
        return rdma(
            norm_send,
            norm_ten.at[ten],
            ns_sem.at[step - 1],
            nr_sem.at[step - 1],
            dp,
            lax.rem(ten + step, 4),
        )

    def norm_two(step):
        return rdma(
            norm_mid,
            norm_dp.at[dp],
            ns_sem.at[2 + step],
            nr_sem.at[2 + step],
            lax.rem(dp + step, data_parts),
            ten,
        )

    norm_ten[ten] = norm_send[...]
    for step in range(1, 4):
        norm_one(step).start()
    for step in range(1, 4):
        norm_one(step).wait_recv()
    total = norm_ten[0]
    for other in range(1, 4):
        total = total + norm_ten[other]
    norm_mid[...] = total
    norm_dp[dp] = total
    for step in range(1, data_parts):
        norm_two(step).start()
    for kind in range(ROWS_MAT):
        g_free(kind, 0)
        fin_copy(kind, 0).wait()
    out_scores.wait()
    for step in range(1, 4):
        norm_one(step).wait_send()
    for step in range(1, data_parts):
        norm_two(step).wait_recv()
    total = norm_dp[0]
    for other in range(1, data_parts):
        total = total + norm_dp[other]
    norm_out[...] = total
    for step in range(1, data_parts):
        norm_two(step).wait_send()


def fits(parts, head_cols, hidden_cols, heads_here, tokens, width, blocks):
    data_parts, tensor_parts = parts
    return (
        tensor_parts == 4
        and data_parts == 8
        and width // data_parts == LANES
        and head_cols // heads_here == 64
        and head_cols % TILE == 0
        and hidden_cols == data_parts * LANES
        and hidden_cols % 512 == 0
        and blocks == 1
        and tokens % 512 == 0
    )


def shards(*arrays, parts):
    (
        hidden_in,
        logits_in,
        cotangent,
        bucket_ids,
        seq_counts,
        key_mask,
        w_qkv,
        w_out,
        w_in,
        w_back,
        vectors,
        bias_in,
    ) = arrays[:12]
    data_parts = parts[0]
    tokens, width = hidden_in.shape
    head_cols = w_qkv.shape[3]
    hidden_cols = w_in.shape[2]
    heads = logits_in.shape[1]
    if not fits(parts, head_cols, hidden_cols, heads, tokens, width, logits_in.shape[0]):
        return plain_shards(*arrays)
    f32 = jnp.float32
    b16 = jnp.bfloat16
    ten = lax.axis_index("tensor")
    share = tokens // 4
    cut = width // data_parts
    cols_n = data_parts // 2
    owned = vectors.shape[2]
    hbm = pl.BlockSpec(memory_space=pl.ANY)
    vmem = pl.BlockSpec(memory_space=pltpu.VMEM)
    smem = pl.BlockSpec(memory_space=pltpu.SMEM)
    dma = pltpu.SemaphoreType.DMA
    shape = jax.ShapeDtypeStruct
    n = LAYERS
    grad_shapes = (
        (3, cut, head_cols),
        (head_cols, cut),
        (cut, hidden_cols),
        (hidden_cols, cut),
    )
    results = pl.pallas_call(
        functools.partial(step_kernel, data_parts),
        out_shape=(
            shape((share, width), b16),
            shape((heads, tokens, tokens), b16),
            shape((share, width), f32),
            shape((heads, tokens, tokens), b16),
        )
        + tuple(shape((n,) + size, b16) for size in grad_shapes)
        + (shape((24, LANES), f32),) * 2,
        in_specs=[hbm] * 3 + [smem] * 2 + [vmem] * 7 + [hbm] * 12,
        out_specs=(hbm, hbm, vmem, hbm, hbm, hbm, hbm, hbm, vmem, vmem),
        scratch_shapes=[
            pltpu.VMEM((8, tokens), f32),
            pltpu.VMEM((3, 32, LANES), f32),
            pltpu.VMEM((n, 3, width, head_cols), b16),
            pltpu.VMEM((n, head_cols, width), b16),
            pltpu.VMEM((n, width, hidden_cols), b16),
            pltpu.VMEM((n, hidden_cols, width), b16),
            pltpu.VMEM((heads, tokens, tokens), b16),
            pltpu.VMEM((n, heads, tokens, tokens), b16),
            pltpu.VMEM((tokens, width), b16),
            pltpu.VMEM((tokens, width), b16),
            pltpu.VMEM((tokens, hidden_cols), b16),
            pltpu.VMEM((tokens, head_cols), b16),
            pltpu.VMEM((n, width, tokens), b16),
            pltpu.VMEM((n, width, tokens), b16),
            pltpu.VMEM((n, hidden_cols, tokens), b16),
            pltpu.VMEM((n, head_cols, tokens), b16),
            pltpu.VMEM((n, tokens, hidden_cols), b16),
            pltpu.VMEM((n, 3, tokens, head_cols), b16),
            pltpu.VMEM((n, share, width), f32),
            pltpu.VMEM((n, share, width), f32),
            pltpu.VMEM((3, tokens, head_cols), b16),
            pltpu.VMEM((share, width), f32),
            pltpu.VMEM((LANES, tokens), f32),
            pltpu.VMEM((LANES, tokens), f32),
            pltpu.VMEM((tokens, width), b16),
            pltpu.VMEM((2, share, width), b16),
            pltpu.VMEM((share, width), b16),
            pltpu.VMEM((share, width), b16),
            pltpu.VMEM((4, data_parts, 32, LANES), b16),
            pltpu.VMEM((n * 8, width), f32),
            pltpu.VMEM((8, hidden_cols), f32),
            pltpu.VMEM((n * 8 + 8, width), f32),
            pltpu.VMEM((4, n * 8 + 8, width), f32),
            pltpu.VMEM((data_parts, n * 8 + 8, LANES), f32),
            pltpu.VMEM((data_parts - 1, n * 8 + 8, LANES), f32),
        ]
        + [pltpu.VMEM((cols_n, 2) + size, b16) for size in grad_shapes]
        + [
            pltpu.VMEM((1 if kind in Z_FIRST else cols_n,) + size, b16)
            for kind, size in enumerate(grad_shapes)
        ]
        + [
            pltpu.VMEM(((cols_n - 1, 2) if kind in Z_FIRST else (cols_n,)) + size, b16)
            for kind, size in enumerate(grad_shapes)
        ]
        + [pltpu.VMEM(size, f32) for _ in range(3) for size in grad_shapes]
        + [
            pltpu.VMEM((n * 8, width), f32),
            pltpu.VMEM((24, LANES), f32),
            pltpu.VMEM((4, 24, LANES), f32),
            pltpu.VMEM((24, LANES), f32),
            pltpu.VMEM((data_parts, 24, LANES), f32),
        ]
        + [
            dma((2,)),
            dma((n, 4)),
            dma((n, 4, cols_n, 2, 2)),
            dma((n, 4, cols_n, 2)),
            dma((n, 4, cols_n)),
            dma((n, 4, cols_n)),
            dma((width // TILE, 2)),
            dma((width // TILE, 2)),
            dma((width // TILE,)),
            dma((width // TILE,)),
            dma((2, 3)),
            dma((2, 3)),
            dma((data_parts + 2,)),
            dma((data_parts + 2,)),
            dma((data_parts + 2,)),
            dma((data_parts + 2,)),
            dma((4, cols_n)),
            dma((4, cols_n)),
            dma((4, cols_n)),
            dma((4, cols_n)),
            dma((4,)),
            dma((4,)),
            dma((3, 4)),
            dma((data_parts + 2,)),
            dma((data_parts + 2,)),
            pltpu.SemaphoreType.REGULAR((3, 4)),
        ],
        compiler_params=pltpu.CompilerParams(
            collective_id=0, has_side_effects=True, vmem_limit_bytes=63 * 1024 * 1024
        ),
    )(
        hidden_in,
        logits_in,
        cotangent,
        bucket_ids,
        seq_counts,
        key_mask.reshape(1, tokens),
        vectors,
        bias_in,
        arrays[16],
        arrays[17],
        arrays[22],
        arrays[23],
        *arrays[6:10],
        *arrays[12:16],
        *arrays[18:22],
    )
    hidden_out, logits_out, grad_hidden, grad_scores = results[:4]
    small = results[8]
    vec_sum = lax.dynamic_slice_in_dim(small[: LAYERS * 8], ten * owned, owned, 1)
    bin_sum = small[LAYERS * 8 : LAYERS * 9]
    grads_all = tuple(one.astype(f32) for one in results[4:8]) + (vec_sum.reshape(LAYERS, 8, owned), bin_sum)
    masters = arrays[6:12]
    firsts = arrays[12:18]
    seconds = arrays[18:24]
    decays = (DECAY_RATE, DECAY_RATE, DECAY_RATE, DECAY_RATE, 0.0, 0.0)
    moved = []
    for master, gradient, first_prev, second_prev, decay_rate in zip(
        masters, grads_all, firsts, seconds, decays
    ):
        moment_one = BETA_ONE * first_prev + (1.0 - BETA_ONE) * gradient
        moment_two = BETA_TWO * second_prev + (1.0 - BETA_TWO) * gradient * gradient
        update = (
            moment_one / CORRECT_ONE / (jnp.sqrt(moment_two / CORRECT_TWO) + ADAM_EPS)
            + decay_rate * master
        )
        moved.append((moment_one, update))
    norms = jnp.sqrt(results[9][:, 0])
    trust_rows = norms[0::2] / norms[1::2]
    trust_all = jnp.concatenate(
        [trust_rows[: LAYERS * 4].reshape(LAYERS, 4), trust_rows[LAYERS * 4 :].reshape(LAYERS, 2)],
        axis=1,
    ).T
    new_params = tuple(
        (
            master
            - LEARN_RATE
            * trust_all[group_at].reshape((LAYERS,) + (1,) * (master.ndim - 1))
            * moved_one[1]
            for group_at, (master, moved_one) in enumerate(zip(masters, moved))
        )
    )
    return (
        (hidden_out, logits_out[None], grad_hidden, grad_scores[None].astype(f32))
        + grads_all
        + new_params
        + tuple(moved_one[0] for moved_one in moved)
        + (trust_all.T,)
    )


def solution(mesh):
    return jax.shard_map(
        functools.partial(shards, parts=(mesh.shape["dp"], mesh.shape["tensor"])),
        mesh=mesh,
        in_specs=(
            P("dp", None),
            P("dp", "tensor", None, None),
            P(("dp", "tensor"), None),
            P("dp"),
            P("dp"),
            P("dp"),
            P(None, None, "dp", "tensor"),
            P(None, "tensor", "dp"),
            P(None, "dp", "tensor"),
            P(None, "tensor", "dp"),
            P(None, None, ("dp", "tensor")),
            P(None, ("dp", "tensor")),
            P(None, None, "dp", "tensor"),
            P(None, "tensor", "dp"),
            P(None, "dp", "tensor"),
            P(None, "tensor", "dp"),
            P(None, None, ("dp", "tensor")),
            P(None, ("dp", "tensor")),
            P(None, None, "dp", "tensor"),
            P(None, "tensor", "dp"),
            P(None, "dp", "tensor"),
            P(None, "tensor", "dp"),
            P(None, None, ("dp", "tensor")),
            P(None, ("dp", "tensor")),
        ),
        out_specs=(
            P(("dp", "tensor"), None),
            P("dp", "tensor", None, None),
            P(("dp", "tensor"), None),
            P("dp", "tensor", None, None),
            P(None, None, "dp", "tensor"),
            P(None, "tensor", "dp"),
            P(None, "dp", "tensor"),
            P(None, "tensor", "dp"),
            P(None, None, ("dp", "tensor")),
            P(None, ("dp", "tensor")),
            P(None, None, "dp", "tensor"),
            P(None, "tensor", "dp"),
            P(None, "dp", "tensor"),
            P(None, "tensor", "dp"),
            P(None, None, ("dp", "tensor")),
            P(None, ("dp", "tensor")),
            P(None, None, "dp", "tensor"),
            P(None, "tensor", "dp"),
            P(None, "dp", "tensor"),
            P(None, "tensor", "dp"),
            P(None, None, ("dp", "tensor")),
            P(None, ("dp", "tensor")),
            P(),
        ),
        check_vma=False,
    )
```

```python
import functools

import jax
import jax.numpy as jnp
from jax import lax
from jax.experimental import pallas as pl
from jax.experimental.pallas import tpu as pltpu
from jax.sharding import PartitionSpec as P

LAYERS = 2


NORM_EPS = 1e-05
ADAM_EPS = 1e-06
BETA_ONE = 0.9
BETA_TWO = 0.999
CORRECT_ONE = 1.0
CORRECT_TWO = 0.632304575228943
LEARN_RATE = 0.3
DECAY_RATE = 0.01
NEG_FILL = -1e30


def layer_norm(values, gain, shift):
    center = values - jnp.mean(values, axis=-1, keepdims=True)
    spread = jnp.mean(center * center, axis=-1, keepdims=True)
    return center * lax.rsqrt(spread + NORM_EPS) * gain + shift


def gelu_exact(values):
    return jax.nn.gelu(values, approximate=False)


def plain_shards(
    hidden_in,
    logits_in,
    cotangent,
    bucket_ids,
    seq_counts,
    key_mask,
    w_qkv,
    w_out,
    w_in,
    w_back,
    vectors,
    bias_in,
    m_qkv,
    m_out,
    m_in,
    m_back,
    m_vectors,
    m_bias,
    v_qkv,
    v_out,
    v_in,
    v_back,
    v_vectors,
    v_bias,
):
    tensor_parts = lax.axis_size("tensor")
    tensor_index = lax.axis_index("tensor")
    data_parts = lax.axis_size("dp")
    tokens_here = hidden_in.shape[0]
    share_rows = tokens_here // tensor_parts
    first_row = tensor_index * share_rows
    block_count = logits_in.shape[0]
    heads_here = logits_in.shape[1]
    block_len = logits_in.shape[2]
    model_width = hidden_in.shape[1]
    head_cols = w_qkv.shape[3]
    head_size = head_cols // heads_here
    hidden_cols = w_in.shape[2]
    score_scale = head_size ** (-0.5)
    bucket = bucket_ids[0]
    seq_span = jnp.where(
        bucket == 0, block_len // 4, jnp.where(bucket == 1, block_len // 2, block_len)
    )
    position = jnp.arange(tokens_here, dtype=jnp.int32)
    seq_flat = position // seq_span
    seq_of = seq_flat.reshape(block_count, block_len)
    live_keys = ((key_mask == 1) & (seq_flat < seq_counts[0])).reshape(block_count, block_len)
    allowed = (seq_of[:, :, None] == seq_of[:, None, :]) & live_keys[:, None, :]
    vec_all, bin_all = (
        lax.all_gather(vectors.astype(jnp.bfloat16), ("dp", "tensor"), axis=2, tiled=True),
        lax.all_gather(bias_in.astype(jnp.bfloat16), ("dp", "tensor"), axis=1, tiled=True),
    )
    vec_all = vec_all.astype(jnp.float32)
    bin_all = bin_all.astype(jnp.float32)

    def sum_forward(term_fn):
        return lax.psum_scatter(
            term_fn(jnp.int32(0), share_rows * lax.axis_size("tensor")).astype(jnp.bfloat16),
            "tensor",
            scatter_dimension=0,
            tiled=True,
        ).astype(jnp.float32)

    def sum_backward(term_fn):
        return lax.psum_scatter(
            term_fn(jnp.int32(0), share_rows * lax.axis_size("tensor")).astype(jnp.bfloat16),
            "tensor",
            scatter_dimension=0,
            tiled=True,
        ).astype(jnp.float32)

    def gather_rows(own_rows):
        return lax.all_gather(own_rows, "tensor", axis=0, tiled=True)

    def gather_grads(own_rows):
        return lax.all_gather(own_rows, "tensor", axis=0, tiled=True)

    def own_cols(vector):
        return lax.dynamic_slice_in_dim(vector, tensor_index * head_cols, head_cols)

    def place_cols(part_sum, total_len, offset):
        return lax.dynamic_update_slice(jnp.zeros((total_len,), jnp.float32), part_sum, (offset,))

    def blocked(matrix):
        return matrix.reshape(block_count, block_len, head_cols)

    def headed(matrix):
        return matrix.reshape(block_len, heads_here, head_size)

    def block_scores(query_b, keys_b, earlier_b):
        raw = jnp.einsum(
            "ihe,jhe->hij", headed(query_b), headed(keys_b), preferred_element_type=jnp.float32
        )
        return raw * score_scale + earlier_b.astype(jnp.float32)

    def attend_block(inputs):
        query_b, keys_b, values_b, earlier_b, allowed_b = inputs
        scores = block_scores(query_b, keys_b, earlier_b)
        row_top = jnp.max(jnp.where(allowed_b[None], scores, NEG_FILL), axis=-1, keepdims=True)
        unscaled = jnp.exp(jnp.where(allowed_b[None], scores - row_top, NEG_FILL))
        row_total = jnp.sum(unscaled, axis=-1, keepdims=True)
        row_total = jnp.where(row_total > 0.5, row_total, 1.0)
        probs_low = (unscaled / row_total).astype(jnp.bfloat16)
        mixed = jnp.einsum(
            "hij,jhe->ihe", probs_low, headed(values_b), preferred_element_type=jnp.float32
        )
        return (
            mixed.reshape(block_len, head_cols).astype(jnp.bfloat16),
            scores.astype(jnp.bfloat16),
            row_top,
            row_total,
        )

    def attend_back(inputs):
        query_b, keys_b, values_b, earlier_b, allowed_b, row_top, row_total, dmixed_b, dlater_b = (
            inputs
        )
        scores = block_scores(query_b, keys_b, earlier_b)
        unscaled = jnp.exp(jnp.where(allowed_b[None], scores - row_top, NEG_FILL))
        probs = unscaled / row_total
        probs_low = probs.astype(jnp.bfloat16)
        dmixed_heads = headed(dmixed_b)
        dvalues = jnp.einsum(
            "hij,ihe->jhe", probs_low, dmixed_heads, preferred_element_type=jnp.float32
        )
        dprobs = jnp.einsum(
            "ihe,jhe->hij", dmixed_heads, headed(values_b), preferred_element_type=jnp.float32
        )
        dlocal = probs * (dprobs - jnp.sum(probs * dprobs, axis=-1, keepdims=True))
        dscores = (dlocal + dlater_b.astype(jnp.float32)).astype(jnp.bfloat16)
        dquery = (
            jnp.einsum("hij,jhe->ihe", dscores, headed(keys_b), preferred_element_type=jnp.float32)
            * score_scale
        )
        dkeys = (
            jnp.einsum("hij,ihe->jhe", dscores, headed(query_b), preferred_element_type=jnp.float32)
            * score_scale
        )
        return (
            dquery.reshape(block_len, head_cols),
            dkeys.reshape(block_len, head_cols),
            dvalues.reshape(block_len, head_cols),
            dscores,
        )

    full_in = hidden_in
    own_in = lax.dynamic_slice_in_dim(hidden_in, first_row, share_rows, 0)
    earlier = logits_in
    records = []
    for layer_at in range(LAYERS):
        fetched = (
            lax.all_gather(w_qkv[layer_at].astype(jnp.bfloat16), "dp", axis=1, tiled=True),
            lax.all_gather(w_out[layer_at].astype(jnp.bfloat16), "dp", axis=1, tiled=True),
            lax.all_gather(w_in[layer_at].astype(jnp.bfloat16), "dp", axis=0, tiled=True),
            lax.all_gather(w_back[layer_at].astype(jnp.bfloat16), "dp", axis=1, tiled=True),
        )
        forward_wqkv, forward_wout, forward_win, forward_wback = fetched
        forward_vector = vec_all[layer_at]
        forward_query = (
            jnp.dot(full_in, forward_wqkv[0], preferred_element_type=jnp.float32)
            + own_cols(forward_vector[2])
        ).astype(jnp.bfloat16)
        forward_keys = jnp.dot(full_in, forward_wqkv[1], preferred_element_type=jnp.float32).astype(
            jnp.bfloat16
        )
        forward_values = (
            jnp.dot(full_in, forward_wqkv[2], preferred_element_type=jnp.float32)
            + own_cols(forward_vector[3])
        ).astype(jnp.bfloat16)
        forward_attn_out, stored, forward_row_top, forward_row_total = lax.map(
            attend_block,
            (
                blocked(forward_query),
                blocked(forward_keys),
                blocked(forward_values),
                earlier,
                allowed,
            ),
        )
        forward_attn_out = forward_attn_out.reshape(tokens_here, head_cols)

        def attn_term(begin_row, row_count):
            return jnp.dot(forward_attn_out, forward_wout, preferred_element_type=jnp.float32)

        forward_mid_pre = sum_forward(attn_term) + forward_vector[4] + own_in.astype(jnp.float32)
        mid_own = layer_norm(forward_mid_pre, forward_vector[0], forward_vector[5]).astype(
            jnp.bfloat16
        )
        forward_mid_full = gather_rows(mid_own)
        bias_here = lax.dynamic_slice_in_dim(
            bin_all[layer_at], tensor_index * hidden_cols, hidden_cols
        )
        forward_pre_act = (
            jnp.dot(forward_mid_full, forward_win, preferred_element_type=jnp.float32) + bias_here
        )
        forward_active = gelu_exact(forward_pre_act).astype(jnp.bfloat16)

        def ffn_term(begin_row, row_count):
            return jnp.dot(forward_active, forward_wback, preferred_element_type=jnp.float32)

        forward_out_pre = sum_forward(ffn_term) + forward_vector[6] + mid_own.astype(jnp.float32)
        out_own = layer_norm(forward_out_pre, forward_vector[1], forward_vector[7]).astype(
            jnp.bfloat16
        )
        forward_state = (
            forward_query,
            forward_keys,
            forward_values,
            forward_attn_out,
            forward_row_top,
            forward_row_total,
            forward_mid_pre,
            forward_mid_full,
            forward_pre_act,
            forward_out_pre,
        )
        out_own, stored, state = (out_own, stored, forward_state)
        records.append((full_in, earlier, fetched, state))
        earlier = stored
        own_in = out_own
        if layer_at + 1 < LAYERS:
            full_in = gather_rows(out_own)
    logits_out = earlier
    d_own = cotangent.astype(jnp.float32)
    d_later = jnp.zeros_like(logits_in)
    mat_grads = [None] * LAYERS
    vec_grads = [None] * LAYERS
    bin_grads = [None] * LAYERS
    for layer_at in reversed(range(LAYERS)):
        full_in, earlier, fetched, state = records[layer_at]
        wqkv = lax.all_gather(w_qkv[layer_at].astype(jnp.bfloat16), "dp", axis=1, tiled=True)
        wout = lax.all_gather(w_out[layer_at].astype(jnp.bfloat16), "dp", axis=1, tiled=True)
        win = lax.all_gather(w_in[layer_at].astype(jnp.bfloat16), "dp", axis=0, tiled=True)
        wback = lax.all_gather(w_back[layer_at].astype(jnp.bfloat16), "dp", axis=1, tiled=True)
        (
            query,
            keys,
            values,
            attn_out,
            backward_row_top,
            backward_row_total,
            mid_pre,
            mid_full,
            pre_act,
            out_pre,
        ) = state
        backward_vector = vec_all[layer_at]
        out_grad, gain_two, shift_two = jax.vjp(
            layer_norm, out_pre, backward_vector[1], backward_vector[7]
        )[1](d_own)
        d_ffn = gather_grads(out_grad.astype(jnp.bfloat16))
        active = gelu_exact(pre_act).astype(jnp.bfloat16)
        grad_back = jnp.einsum("tf,td->fd", active, d_ffn, preferred_element_type=jnp.float32)
        d_active = jnp.einsum("td,fd->tf", d_ffn, wback, preferred_element_type=jnp.float32)
        d_pre = jax.vjp(gelu_exact, pre_act)[1](d_active)[0].astype(jnp.bfloat16)
        grad_in = jnp.einsum("td,tf->df", mid_full, d_pre, preferred_element_type=jnp.float32)

        def mid_term(begin_row, row_count):
            return jnp.einsum("tf,df->td", d_pre, win, preferred_element_type=jnp.float32)

        mid_grad = sum_backward(mid_term) + out_grad
        attn_grad, gain_one, shift_one = jax.vjp(
            layer_norm, mid_pre, backward_vector[0], backward_vector[5]
        )[1](mid_grad)
        d_attn = gather_grads(attn_grad.astype(jnp.bfloat16))
        grad_out_proj = jnp.einsum(
            "tc,td->cd", attn_out, d_attn, preferred_element_type=jnp.float32
        )
        d_mixed = jnp.einsum("td,cd->tc", d_attn, wout, preferred_element_type=jnp.float32).astype(
            jnp.bfloat16
        )
        backward_dquery, backward_dkeys, backward_dvalues, backward_dscores = lax.map(
            attend_back,
            (
                blocked(query),
                blocked(keys),
                blocked(values),
                earlier,
                allowed,
                backward_row_top,
                backward_row_total,
                blocked(d_mixed),
                d_later,
            ),
        )
        backward_dquery = backward_dquery.reshape(tokens_here, head_cols).astype(jnp.bfloat16)
        backward_dkeys = backward_dkeys.reshape(tokens_here, head_cols).astype(jnp.bfloat16)
        backward_dvalues = backward_dvalues.reshape(tokens_here, head_cols).astype(jnp.bfloat16)
        grad_qkv = jnp.stack(
            [
                jnp.einsum(
                    "td,tc->dc", full_in, backward_dquery, preferred_element_type=jnp.float32
                ),
                jnp.einsum(
                    "td,tc->dc", full_in, backward_dkeys, preferred_element_type=jnp.float32
                ),
                jnp.einsum(
                    "td,tc->dc", full_in, backward_dvalues, preferred_element_type=jnp.float32
                ),
            ]
        )

        def input_term(begin_row, row_count):
            total_term = jnp.einsum(
                "tc,dc->td", backward_dquery, wqkv[0], preferred_element_type=jnp.float32
            )
            total_term = total_term + jnp.einsum(
                "tc,dc->td", backward_dkeys, wqkv[1], preferred_element_type=jnp.float32
            )
            return total_term + jnp.einsum(
                "tc,dc->td", backward_dvalues, wqkv[2], preferred_element_type=jnp.float32
            )

        in_grad = sum_backward(input_term) + attn_grad
        col_offset = tensor_index * head_cols
        vec_grad = jnp.stack(
            [
                gain_one,
                gain_two,
                place_cols(
                    jnp.sum(backward_dquery.astype(jnp.float32), axis=0), model_width, col_offset
                ),
                place_cols(
                    jnp.sum(backward_dvalues.astype(jnp.float32), axis=0), model_width, col_offset
                ),
                jnp.sum(attn_grad, axis=0),
                shift_one,
                jnp.sum(out_grad, axis=0),
                shift_two,
            ]
        )
        bin_grad = place_cols(
            jnp.sum(d_pre.astype(jnp.float32), axis=0),
            hidden_cols * tensor_parts,
            tensor_index * hidden_cols,
        )
        d_own, d_later, mats, vec_grad, bin_grad = (
            in_grad,
            backward_dscores,
            (grad_qkv, grad_out_proj, grad_in, grad_back),
            vec_grad,
            bin_grad,
        )
        totals = (
            lax.psum(mats[0].astype(jnp.bfloat16), "dp").astype(jnp.float32),
            lax.psum(mats[1].astype(jnp.bfloat16), "dp").astype(jnp.float32),
            lax.psum(mats[2].astype(jnp.bfloat16), "dp").astype(jnp.float32),
            lax.psum(mats[3].astype(jnp.bfloat16), "dp").astype(jnp.float32),
        )
        data_index = lax.axis_index("dp")
        mat_grads[layer_at] = tuple(
            (
                lax.dynamic_slice_in_dim(
                    whole,
                    data_index * (whole.shape[axis_at] // data_parts),
                    whole.shape[axis_at] // data_parts,
                    axis_at,
                )
                for whole, axis_at in zip(totals, (1, 1, 0, 1))
            )
        )
        vec_grads[layer_at] = vec_grad
        bin_grads[layer_at] = bin_grad
    grad_logits = d_later.astype(jnp.float32)
    vec_sum, bin_sum = (
        lax.psum_scatter(jnp.stack(vec_grads), ("dp", "tensor"), scatter_dimension=2, tiled=True),
        lax.psum_scatter(jnp.stack(bin_grads), ("dp", "tensor"), scatter_dimension=1, tiled=True),
    )
    grads_all = (
        jnp.stack([mat_grads[level_at][0] for level_at in range(LAYERS)]),
        jnp.stack([mat_grads[level_at][1] for level_at in range(LAYERS)]),
        jnp.stack([mat_grads[level_at][2] for level_at in range(LAYERS)]),
        jnp.stack([mat_grads[level_at][3] for level_at in range(LAYERS)]),
        vec_sum,
        bin_sum,
    )
    masters = (w_qkv, w_out, w_in, w_back, vectors, bias_in)
    firsts = (m_qkv, m_out, m_in, m_back, m_vectors, m_bias)
    seconds = (v_qkv, v_out, v_in, v_back, v_vectors, v_bias)
    decays = (DECAY_RATE, DECAY_RATE, DECAY_RATE, DECAY_RATE, 0.0, 0.0)
    moved = []
    for master, gradient, first_prev, second_prev, decay_rate in zip(
        masters, grads_all, firsts, seconds, decays
    ):
        moment_one = BETA_ONE * first_prev + (1.0 - BETA_ONE) * gradient
        moment_two = BETA_TWO * second_prev + (1.0 - BETA_TWO) * gradient * gradient
        update = (
            moment_one / CORRECT_ONE / (jnp.sqrt(moment_two / CORRECT_TWO) + ADAM_EPS)
            + decay_rate * master
        )
        moved.append((moment_one, update))
    weight_sq = jnp.stack(
        [jnp.sum((master * master).reshape(LAYERS, -1), axis=1) for master in masters]
    )
    update_sq = jnp.stack(
        [jnp.sum((moved_one[1] * moved_one[1]).reshape(LAYERS, -1), axis=1) for moved_one in moved]
    )
    weight_tot, update_tot = lax.psum((weight_sq, update_sq), ("dp", "tensor"))
    trust_all = jnp.sqrt(weight_tot) / jnp.sqrt(update_tot)
    new_params = tuple(
        (
            master
            - LEARN_RATE
            * trust_all[group_at].reshape((LAYERS,) + (1,) * (master.ndim - 1))
            * moved_one[1]
            for group_at, (master, moved_one) in enumerate(zip(masters, moved))
        )
    )
    return (
        own_in,
        logits_out,
        d_own,
        grad_logits,
        grads_all[0],
        grads_all[1],
        grads_all[2],
        grads_all[3],
        grads_all[4],
        grads_all[5],
        new_params[0],
        new_params[1],
        new_params[2],
        new_params[3],
        new_params[4],
        new_params[5],
        moved[0][0],
        moved[1][0],
        moved[2][0],
        moved[3][0],
        moved[4][0],
        moved[5][0],
        trust_all.T,
    )


MESH = pl.DeviceIdType.MESH
TILE = 256
LANES = 128
ROWS_MAT = 4
X_FIRST = (1,)
Z_AHEAD = 2
X_AHEAD = 3
SLOTS = ((1, 3), (2, 1), (2, 3), (3, 1), (3, 2), (4, 1), (5, 1))
Z_FIRST = ()
BACK_SLOTS = (
    (-9, -9, 0, 1, 2, 3, 4, 5, 6),
    (-9, -5, -4, -2, 0, 0, 1, 2, 3),
    (8,),
)


def dot_nn(left, right):
    return lax.dot_general(
        left, right, (((1,), (0,)), ((), ())), preferred_element_type=jnp.float32
    )


def dot_nt(left, right):
    return lax.dot_general(
        left, right, (((1,), (1,)), ((), ())), preferred_element_type=jnp.float32
    )


def norm_parts(values):
    center = values - jnp.mean(values, axis=-1, keepdims=True)
    spread = jnp.mean(center * center, axis=-1, keepdims=True)
    return center, lax.rsqrt(spread + NORM_EPS)


def step_kernel(
    data_parts,
    hidden_in,
    logits_in,
    cotangent,
    bucket,
    count,
    key_mask,
    vec_w,
    bias_w,
    vec_m,
    bias_m,
    vec_v,
    bias_v,
    lw_qkv,
    lw_out,
    lw_in,
    lw_back,
    lm_qkv,
    lm_out,
    lm_in,
    lm_back,
    lv_qkv,
    lv_out,
    lv_in,
    lv_back,
    hidden_out,
    logits_out,
    grad_hidden,
    grad_scores,
    sum_qkv,
    sum_out,
    sum_in,
    sum_back,
    small_out,
    norm_out,
    key_ids,
    small_in,
    w_q,
    w_o,
    w_i,
    w_b,
    scores,
    probs,
    h_full,
    m_full,
    active,
    attn,
    h_turn,
    m_turn,
    g_turn,
    o_turn,
    slope,
    qkv,
    x_own,
    y_own,
    d_qkv,
    d_keep,
    turn_v,
    turn_k,
    part,
    got_core,
    sum_chip,
    got_y,
    vec_got,
    vec_all,
    bin_all,
    small_acc,
    small_got,
    small_send,
    small_sum,
    pk_q,
    pk_o,
    pk_i,
    pk_b,
    rx_q,
    rx_o,
    rx_i,
    rx_b,
    rz_q,
    rz_o,
    rz_i,
    rz_b,
    fw_q,
    fw_o,
    fw_i,
    fw_b,
    fm_q,
    fm_o,
    fm_i,
    fm_b,
    fv_q,
    fv_o,
    fv_i,
    fv_b,
    norms,
    norm_send,
    norm_ten,
    norm_mid,
    norm_dp,
    load_sem,
    own_sem,
    zs_sem,
    zr_sem,
    xs_sem,
    xr_sem,
    core_s,
    core_r,
    ys_sem,
    yr_sem,
    gat_s,
    gat_r,
    vec_s,
    vec_r,
    sml_s,
    sml_r,
    gxs_sem,
    gxr_sem,
    gzs_sem,
    gzr_sem,
    fin_sem,
    out_sem,
    lamb_sem,
    ns_sem,
    nr_sem,
    credit,
):
    dp = lax.axis_index("dp")
    ten = lax.axis_index("tensor")
    cols_n = data_parts // 2
    side = lax.rem(dp, 2)
    place = dp // 2
    row_y = ten // 2
    core = lax.rem(ten, 2)
    across = dp + 1 - 2 * side
    core_mate = ten + 1 - 2 * core
    y_mate = lax.rem(ten + 2, 4)
    width = hidden_in.shape[1]
    tokens = hidden_in.shape[0]
    share = tokens // 4
    half = share // 2
    head_cols = qkv.shape[3]
    hidden_cols = slope.shape[2]
    cut = width // data_parts
    tiles = width // TILE
    f32 = jnp.float32
    b16 = jnp.bfloat16

    def along(step):
        return lax.rem(place + step, cols_n) * 2 + side

    def mult(value, by):
        return pl.multiple_of(value, by)

    def rdma(src, dst, send, recv, to_dp, to_ten):
        return pltpu.make_async_remote_copy(
            src_ref=src,
            dst_ref=dst,
            send_sem=send,
            recv_sem=recv,
            device_id=(to_dp, to_ten),
            device_id_type=MESH,
        )

    def region(kind, layer, dev):
        at = pl.ds(mult(dev * cut, cut), cut)
        if kind == 0:
            return w_q.at[layer, :, at, :]
        if kind == 1:
            return w_o.at[layer, :, at]
        if kind == 2:
            return w_i.at[layer, at, :]
        return w_b.at[layer, :, at]

    load_h = pltpu.make_async_copy(hidden_in, h_full, load_sem.at[0])
    load_s = pltpu.make_async_copy(logits_in.at[0], scores, load_sem.at[1])
    load_h.start()
    load_s.start()
    masters = (
        (lw_qkv, lw_out, lw_in, lw_back),
        (lm_qkv, lm_out, lm_in, lm_back),
        (lv_qkv, lv_out, lv_in, lv_back),
    )
    held = ((fw_q, fw_o, fw_i, fw_b), (fm_q, fm_o, fm_i, fm_b), (fv_q, fv_o, fv_i, fv_b))

    def lamb_load(kind, layer, which):
        return pltpu.make_async_copy(
            masters[which][kind].at[layer], held[which][kind], lamb_sem.at[which, kind]
        )

    def own_load(kind, layer):
        to = LAYERS - 1 - layer
        return pltpu.make_async_copy(masters[0][kind].at[layer], held[to][kind], own_sem.at[layer, kind])

    for layer in range(LAYERS):
        for kind in range(ROWS_MAT):
            own_load(kind, layer).start()

    barrier = pltpu.get_barrier_semaphore()

    def greet(step, carry):
        pl.semaphore_signal(
            barrier, inc=1, device_id=(lax.rem(dp + step, data_parts), ten), device_id_type=MESH
        )
        return carry

    lax.fori_loop(1, data_parts, greet, 0)
    for other in range(1, 4):
        pl.semaphore_signal(
            barrier, inc=1, device_id=(dp, lax.rem(ten + other, 4)), device_id_type=MESH
        )

    def w_x(kind, layer, from_place, col):
        dst = region(kind, layer, from_place * 2 + col)
        return rdma(
            dst,
            dst,
            xs_sem.at[layer, kind, from_place],
            xr_sem.at[layer, kind, from_place],
            across,
            ten,
        )

    def w_z(kind, layer, from_place, col, way, send=True):
        dst = region(kind, layer, from_place * 2 + col)
        which = lax.rem(col + side, 2)
        return rdma(
            dst,
            dst,
            zs_sem.at[layer, kind, from_place, which, (way + 1) // 2],
            zr_sem.at[layer, kind, from_place, which],
            dp + 2 * way if send else dp,
            ten,
        )

    can_go = {1: place < cols_n - 1, -1: place > 0}

    def w_both_ways(kind, layer, col):
        for way in (1, -1):

            @pl.when(can_go[way])
            def _():
                w_z(kind, layer, place, col, way).start()

    def w_far(kind, layer, col, step):
        dst = region(kind, layer, place * 2 + col)
        which = lax.rem(col + side, 2)
        return rdma(
            dst,
            dst,
            zs_sem.at[layer, kind, step, which, 0],
            zr_sem.at[layer, kind, step, which],
            along(step),
            ten,
        )

    def w_event(kind, layer, hop):
        if kind in X_FIRST:
            w_x(kind, layer, place, 1 - side).wait_recv()
            for step in range(1, cols_n):
                w_far(kind, layer, 1 - side, step).start()
            return
        for way in (1, -1):
            came = place - hop * way

            @pl.when(came >= 0 if way == 1 else came < cols_n)
            def _():
                w_z(kind, layer, came, side, way, False).wait_recv()

                @pl.when(can_go[way])
                def _():
                    w_z(kind, layer, came, side, way).start()

                w_x(kind, layer, came, side).start()

    order = [(kind, layer) for layer in range(LAYERS) for kind in range(ROWS_MAT)]

    def w_own_z(index):
        if index < len(order):
            kind, layer = order[index]
            if kind in X_FIRST:
                for step in range(1, cols_n):
                    w_far(kind, layer, side, step).start()
            else:
                w_both_ways(kind, layer, side)

    def w_own_x(index):
        if index < len(order):
            w_x(*order[index], place, side).start()

    def w_own(index):
        kind, layer = order[index]
        own_load(kind, layer).wait()
        mine = region(kind, layer, dp)
        mine[...] = held[LAYERS - 1 - layer][kind][...].astype(b16)

    for index in range(X_AHEAD):
        w_own(index)
    for kind, slots in enumerate((rz_q, rz_o, rz_i, rz_b)):
        if kind in Z_FIRST:
            continue

        @pl.when(place == 0)
        def _():
            slots[0] = jnp.zeros(slots.shape[1:], b16)
            slots[3] = jnp.zeros(slots.shape[1:], b16)

        @pl.when(place == cols_n - 1)
        def _():
            slots[2] = jnp.zeros(slots.shape[1:], b16)
            slots[3] = jnp.zeros(slots.shape[1:], b16)

    owned = vec_w.shape[2]
    spread_row = lax.broadcasted_iota(jnp.int32, (owned, LANES), 0)
    spread_col = lax.broadcasted_iota(jnp.int32, (owned, LANES), 1)
    spread = jnp.where(spread_row + ten * owned == spread_col, 1.0, 0.0)
    lane_row = lax.broadcasted_iota(jnp.int32, (1, LANES), 1)
    not_owned = jnp.where(lane_row // owned == ten, 0.0, 1.0)
    small_in[...] = jnp.zeros_like(small_in)
    small_in[2] = jnp.ones_like(small_in[2])
    for which, (wide, narrow) in enumerate(((vec_w, bias_w), (vec_m, bias_m), (vec_v, bias_v))):
        for layer in range(LAYERS):
            rows = lax.dot_general(
                wide[layer],
                spread,
                (((1,), (0,)), ((), ())),
                precision=lax.Precision.HIGHEST,
                preferred_element_type=jnp.float32,
            )
            if which == 2:
                rows = rows + not_owned
            small_in[which, layer * 8 : layer * 8 + 8, :] = rows
            small_in[which, LAYERS * 8 + layer : LAYERS * 8 + layer + 1, :] = narrow[
                layer : layer + 1, :
            ]
    vec_got[ten, dp] = small_in[0].astype(b16)
    span_of = (tokens // 4, tokens // 2, tokens)
    per_key = jnp.where(
        bucket[0] == 0, 1.0 / span_of[0], jnp.where(bucket[0] == 1, 1.0 / span_of[1], 1.0 / span_of[2])
    ).astype(f32)
    key_at = lax.broadcasted_iota(jnp.int32, (1, tokens), 1).astype(f32)
    key_seq = jnp.floor(key_at * per_key)
    alive = (key_mask[...] == 1) & (key_seq < count[0].astype(f32))
    key_ids[0:1, :] = jnp.where(alive, key_seq, -1.0)

    pl.semaphore_wait(barrier, data_parts + 2)
    def vec_one(step):
        return rdma(
            vec_got.at[ten, dp],
            vec_got.at[ten, dp],
            vec_s.at[step - 1],
            vec_r.at[step - 1],
            lax.rem(dp + step, data_parts),
            ten,
        )

    def vec_go(step, carry):
        vec_one(step).start()
        return carry

    lax.fori_loop(1, data_parts, vec_go, 0)

    for index in range(X_AHEAD):
        if index < Z_AHEAD:
            w_own_z(index)
        w_own_x(index)

    for index in range(X_AHEAD, len(order)):
        w_own(index)

    events = [
        (index, hop)
        for index in range(len(order))
        for hop in range(1, 2 if order[index][0] in X_FIRST else cols_n)
    ]
    passed = [0]

    def pass_on(layer_at, kind_at, hop_at):
        goal = (layer_at * ROWS_MAT + kind_at, hop_at)
        while passed[0] < len(events) and events[passed[0]] <= goal:
            index, hop = events[passed[0]]
            w_event(*order[index], hop)
            if hop == cols_n - 1 or order[index][0] in X_FIRST:
                w_own_z(index + Z_AHEAD)
                w_own_x(index + X_AHEAD)
            passed[0] += 1

    def have(layer, kind):
        pass_on(layer, kind, cols_n)
        if kind in X_FIRST:
            for step in range(1, cols_n):
                for col in (side, 1 - side):
                    w_far(kind, layer, col, step).wait_recv()
        else:
            for from_place in range(cols_n):
                w_x(kind, layer, from_place, 1 - side).wait_recv()

    def w_finish():
        for kind, layer in order:
            if kind in X_FIRST:
                w_x(kind, layer, place, side).wait_send()
                for step in range(1, cols_n):
                    for col in (side, 1 - side):
                        w_far(kind, layer, col, step).wait_send()
                continue
            for from_place in range(cols_n):
                w_x(kind, layer, from_place, side).wait_send()

                @pl.when(can_go[1] & (from_place <= place))
                def _():
                    w_z(kind, layer, from_place, side, 1).wait_send()

                @pl.when(can_go[-1] & (from_place >= place))
                def _():
                    w_z(kind, layer, from_place, side, -1).wait_send()

    def vec_wait(step, carry):
        vec_one(step).wait_send()
        vec_one(step).wait_recv()
        return carry

    lax.fori_loop(1, data_parts, vec_wait, 0)

    def vec_two(step):
        return rdma(
            vec_got.at[ten],
            vec_got.at[ten],
            vec_s.at[data_parts - 2 + step],
            vec_r.at[data_parts - 2 + step],
            dp,
            lax.rem(ten + step, 4),
        )

    for step in range(1, 4):
        vec_two(step).start()
    for step in range(1, 4):
        vec_two(step).wait_send()
        vec_two(step).wait_recv()
    for dev in range(data_parts):
        total = vec_got[0, dev].astype(f32)
        for other in range(1, 4):
            total = total + vec_got[other, dev].astype(f32)
        vec_all[:, dev * LANES : (dev + 1) * LANES] = total[0 : LAYERS * 8]
    for piece in range(hidden_cols // LANES):
        got = vec_got[piece % 4, ten * 2 + piece // 4].astype(f32)
        bin_all[:, piece * LANES : (piece + 1) * LANES] = got[LAYERS * 8 : LAYERS * 8 + 8]

    def vec_row(layer, row):
        return vec_all[layer * 8 + row : layer * 8 + row + 1, :]

    def block_rows(which_y, which_core):
        return pl.ds(mult((which_y * 2 + which_core) * share, share), share)

    far_block = block_rows(1 - row_y, 1 - core)
    mate_block = block_rows(row_y, 1 - core)
    over_block = block_rows(1 - row_y, core)
    own_block = block_rows(row_y, core)

    def tile_cols(tile):
        return pl.ds(mult(tile * TILE, TILE), TILE)

    def send_core(tile, which):
        rows = far_block if which == 0 else mate_block
        return rdma(
            part.at[rows, tile_cols(tile)],
            got_core.at[which, :, tile_cols(tile)],
            core_s.at[tile, which],
            core_r.at[tile, which],
            dp,
            core_mate,
        )

    def send_y(tile):
        return rdma(
            sum_chip.at[:, tile_cols(tile)],
            got_y.at[:, tile_cols(tile)],
            ys_sem.at[tile],
            yr_sem.at[tile],
            dp,
            y_mate,
        )

    def add_core(tile):
        send_core(tile, 0).wait_recv()
        at = tile_cols(tile)
        sum_chip[:, at] = (
            part[over_block, at].astype(f32) + got_core[0, :, at].astype(f32)
        ).astype(b16)
        send_y(tile).start()

    def sum_start(tile_fn):
        def one(tile, carry):
            part[:, tile_cols(tile)] = tile_fn(tile).astype(b16)
            send_core(tile, 0).start()
            send_core(tile, 1).start()

            @pl.when(tile > 0)
            def _():
                add_core(tile - 1)

            return carry

        lax.fori_loop(0, tiles, one, 0)
        add_core(tiles - 1)

    def sum_end():
        for tile in range(tiles):
            send_core(tile, 1).wait_recv()
            send_y(tile).wait_recv()
        for tile in range(tiles):
            send_core(tile, 0).wait_send()
            send_core(tile, 1).wait_send()
            send_y(tile).wait_send()

    def sum_rows(which):
        at = pl.ds(which * half, half)
        mine = pl.ds(mult(ten * share + which * half, half), half)
        return (
            part[mine, :].astype(f32) + got_core[1, at, :].astype(f32) + got_y[at, :].astype(f32)
        )

    def gat_copy(buf, which, kind):
        if kind == 2:
            rows = pl.ds(mult(y_mate * share + which * half, half), half)
        else:
            rows = pl.ds(mult(ten * share + which * half, half), half)
        return rdma(
            buf.at[rows],
            buf.at[rows],
            gat_s.at[which, kind],
            gat_r.at[which, kind],
            dp,
            y_mate if kind == 1 else core_mate,
        )

    def gat_start(buf, which):
        gat_copy(buf, which, 1).start()
        gat_copy(buf, which, 0).start()

    def gat_end(buf):
        for which in range(2):
            gat_copy(buf, which, 1).wait_recv()
            gat_copy(buf, which, 2).start()
        for which in range(2):
            gat_copy(buf, which, 0).wait_recv()
            gat_copy(buf, which, 2).wait_recv()
        for which in range(2):
            for kind in range(3):
                gat_copy(buf, which, kind).wait_send()

    def own_rows(which):
        return pl.ds(mult(ten * share + which * half, half), half)

    def turn(src, dst, layer):
        def one(at, carry):
            dst[layer, tile_cols(at), :] = src[:, tile_cols(at)].T
            return carry

        lax.fori_loop(0, src.shape[1] // TILE, one, 0)

    lane = lax.broadcasted_iota(jnp.int32, (1, LANES), 1)
    low_lanes = jnp.where(lane < 64, 1.0, 0.0).astype(b16)
    high_lanes = jnp.where(lane < 64, 0.0, 1.0).astype(b16)
    lane_masks = (low_lanes, high_lanes)
    scale = 0.125
    score_rows = 256
    pairs = head_cols // LANES

    def pair_cols(pair):
        return slice(pair * LANES, (pair + 1) * LANES)

    def attend(layer, pair):
        def one(step, carry):
            rows = pl.ds(mult(step * score_rows, score_rows), score_rows)
            at = slice(pair * LANES, (pair + 1) * LANES)
            queries = qkv[layer, 0, rows, at]
            keys = qkv[layer, 1, :, at]
            values = qkv[layer, 2, :, at]
            row = lax.broadcasted_iota(jnp.int32, (score_rows, 1), 0) + step * score_rows
            allowed = jnp.floor(row.astype(f32) * per_key) == key_ids[0:1, :]
            mixed = jnp.zeros((score_rows, LANES), f32)
            for head in range(2):
                raw = dot_nt(queries, keys * lane_masks[head])
                full = raw * scale + scores[pair * 2 + head, rows, :].astype(f32)
                scores[pair * 2 + head, rows, :] = full.astype(b16)
                top = jnp.max(jnp.where(allowed, full, NEG_FILL), axis=-1, keepdims=True)
                weight = jnp.exp(jnp.where(allowed, full - top, NEG_FILL))
                total = jnp.sum(weight, axis=-1, keepdims=True)
                total = jnp.where(total > 0.5, total, 1.0)
                low = (weight * (1.0 / total)).astype(b16)
                probs[layer, pair * 2 + head, rows, :] = low
                mixed = mixed + dot_nn(low, values * lane_masks[head])
            attn[rows, at] = mixed.astype(b16)
            return carry

        lax.fori_loop(0, tokens // score_rows, one, 0)

    def attend_back(layer, first, pairs_of):
        def pair_one(pair, carry):
            at = pair_cols(pair)
            turn_v[...] = jnp.zeros_like(turn_v)
            turn_k[...] = jnp.zeros_like(turn_k)

            def one(step, inner):
                rows = pl.ds(mult(step * score_rows, score_rows), score_rows)
                queries = qkv[layer, 0, rows, at]
                keys = qkv[layer, 1, :, at]
                values = qkv[layer, 2, :, at]
                grads = attn[rows, at]
                turned_q = queries.T
                turned_g = grads.T
                d_query = jnp.zeros((score_rows, LANES), f32)
                for head in range(2):
                    low = probs[layer, pair * 2 + head, rows, :]
                    prob = low.astype(f32)
                    d_prob = dot_nt(grads, values * lane_masks[head])
                    inner_sum = jnp.sum(prob * d_prob, axis=-1, keepdims=True)
                    d_score = prob * (d_prob - inner_sum)
                    if not first:
                        d_score = d_score + scores[pair * 2 + head, rows, :].astype(f32)
                    d_low = d_score.astype(b16)
                    scores[pair * 2 + head, rows, :] = d_low
                    d_query = d_query + dot_nn(d_low, keys * lane_masks[head])
                    part_rows = slice(head * 64, head * 64 + 64)
                    turn_v[part_rows, :] += dot_nn(turned_g[part_rows, :], low)
                    turn_k[part_rows, :] += dot_nn(turned_q[part_rows, :], d_low)
                d_qkv[0, rows, at] = (d_query * scale).astype(b16)
                return inner

            lax.fori_loop(0, tokens // score_rows, one, 0)
            d_qkv[1, :, at] = (turn_k[...] * scale).T.astype(b16)
            d_qkv[2, :, at] = turn_v[...].T.astype(b16)
            return carry

        for pair in pairs_of:
            pair_one(pair, 0)

    own_cols = pl.ds(mult(ten * head_cols, head_cols), head_cols)
    small_acc[...] = jnp.zeros_like(small_acc)
    load_h.wait()
    load_s.wait()
    for layer in range(LAYERS):
        have(layer, 0)
        for which in range(3):
            product = dot_nn(h_full[...], w_q[layer, which])
            if which == 0:
                product = product + vec_all[layer * 8 + 2 : layer * 8 + 3, own_cols]
            if which == 2:
                product = product + vec_all[layer * 8 + 3 : layer * 8 + 4, own_cols]
            qkv[layer, which] = product.astype(b16)
        pass_on(layer, *SLOTS[0])
        attend(layer, 0)
        pass_on(layer, *SLOTS[1])
        attend(layer, 1)
        have(layer, 1)
        sum_start(lambda tile: dot_nn(attn[...], w_o[layer, :, tile_cols(tile)]))
        turn(attn, o_turn, layer)
        turn(h_full, h_turn, layer)
        pass_on(layer, *SLOTS[2])
        sum_end()
        for which in range(2):
            at = pl.ds(which * half, half)
            mid = sum_rows(which) + vec_row(layer, 4) + h_full[own_rows(which), :].astype(f32)
            x_own[layer, at, :] = mid
            center, rate = norm_parts(mid)
            m_full[own_rows(which), :] = (
                center * rate * vec_row(layer, 0) + vec_row(layer, 5)
            ).astype(b16)
            gat_start(m_full, which)
        pass_on(layer, *SLOTS[3])
        gat_end(m_full)

        def ffn_tile(tile, carry):
            at = tile_cols(tile)
            pre = dot_nn(m_full[...], w_i[layer, :, at]) + bin_all[layer : layer + 1, at]
            cumul = 0.5 * (1.0 + lax.erf(pre * 0.7071067811865476))
            dens = jnp.exp(-0.5 * pre * pre) * 0.3989422804014327
            active[:, at] = (pre * cumul).astype(b16)
            slope[layer, :, at] = (cumul + pre * dens).astype(b16)
            return carry

        have(layer, 2)
        pass_on(layer, *SLOTS[4])
        lax.fori_loop(0, hidden_cols // TILE, ffn_tile, 0)
        turn(m_full, m_turn, layer)
        have(layer, 3)
        sum_start(lambda tile: dot_nn(active[...], w_b[layer, :, tile_cols(tile)]))
        turn(active, g_turn, layer)
        pass_on(layer, *SLOTS[5])
        sum_end()
        for which in range(2):
            at = pl.ds(which * half, half)
            late = sum_rows(which) + vec_row(layer, 6) + m_full[own_rows(which), :].astype(f32)
            y_own[layer, at, :] = late
            center, rate = norm_parts(late)
            result = (center * rate * vec_row(layer, 1) + vec_row(layer, 7)).astype(b16)
            h_full[own_rows(which), :] = result
            if layer + 1 < LAYERS:
                gat_start(h_full, which)
        if layer + 1 < LAYERS:
            pass_on(layer, *SLOTS[6])
            gat_end(h_full)

    out_logits = pltpu.make_async_copy(scores, logits_out, out_sem.at[0])
    out_logits.start()
    all_own = pl.ds(mult(ten * share, share), share)
    out_hidden = pltpu.make_async_copy(h_full.at[all_own], hidden_out, out_sem.at[2])
    out_hidden.start()
    load_c = pltpu.make_async_copy(cotangent, sum_chip, out_sem.at[3])
    load_c.start()
    w_finish()

    packs = (pk_q, pk_o, pk_i, pk_b)
    got_x = (rx_q, rx_o, rx_i, rx_b)
    got_z = (rz_q, rz_o, rz_i, rz_b)
    sums = (sum_qkv, sum_out, sum_in, sum_back)

    def turn_of(turn_at):
        upper = place // 2
        inner = upper * (cols_n - 1) + (1 - 2 * upper) * place
        pairs_of = turn_at * (turn_at - 1)
        swing = 2 * turn_at - pairs_of // 2 - pairs_of * (turn_at - 2) // 3
        at = (1 - inner) * (3 - turn_at) + inner * swing
        return upper * (cols_n - 1) + (1 - 2 * upper) * at

    at_end = (place == 0) | (place == cols_n - 1)

    def g_x(kind, at):
        first = kind not in Z_FIRST
        return rdma(
            packs[kind].at[at, 1 - side],
            got_x[kind].at[at if first else 0],
            gxs_sem.at[kind, at],
            gxr_sem.at[kind, at],
            across,
            ten,
        )

    def g_z(kind, at):
        far = (at - place) * (at - place) // 9
        to = (1 - far) * at + far * (place + 1 - 2 * (place // 2))
        slot = (1 - far) * (lax.rem(at - place + cols_n, cols_n) - 1) + far * 3
        return rdma(
            packs[kind].at[at, side],
            got_z[kind].at[slot],
            gzs_sem.at[kind, at],
            gzr_sem.at[kind, slot],
            to * 2 + side,
            ten,
        )

    def g_z_came(kind, slot):
        copy = rdma(
            packs[kind].at[0, side],
            got_z[kind].at[slot],
            gzs_sem.at[kind, 0],
            gzr_sem.at[kind, slot],
            dp,
            ten,
        )
        comes = (place > 0, place >= 0, place < cols_n - 1, jnp.logical_not(at_end))[slot]

        @pl.when(comes)
        def _():
            copy.wait_recv()

    def g_far(kind, step):
        to = lax.rem(place + step, cols_n)
        return rdma(
            packs[kind].at[to],
            got_z[kind].at[step - 1],
            gzs_sem.at[kind, step],
            gzr_sem.at[kind, step - 1],
            to * 2 + side,
            ten,
        )

    def g_free(kind, layer):
        add_upto(layer, (3 - kind) * cols_n + cols_n - 1)
        for turn_at in range(cols_n - 1):
            at = turn_of(turn_at)
            if kind in Z_FIRST:
                g_far(kind, turn_at + 1).wait_send()
            else:
                g_z(kind, at).wait_send()
                g_x(kind, at).wait_send()
        g_x(kind, place).wait_send()

    def give_credit(kind):
        pl.semaphore_signal(
            credit.at[0, kind], inc=1, device_id=(across, ten), device_id_type=MESH
        )
        if kind in Z_FIRST:
            for step in range(1, cols_n):
                pl.semaphore_signal(
                    credit.at[1, kind], inc=1, device_id=(along(step), ten), device_id_type=MESH
                )
            return

        for hop in (2, -2, 1, -1):

            @pl.when(place < cols_n - hop if hop > 0 else place >= -hop)
            def _():
                pl.semaphore_signal(
                    credit.at[1, kind], inc=1, device_id=(dp + 2 * hop, ten), device_id_type=MESH
                )

    def take_credit_x(kind):
        pl.semaphore_wait(credit.at[0, kind], 1)

    def take_credit_z(kind):
        if kind in Z_FIRST:
            pl.semaphore_wait(credit.at[1, kind], cols_n - 1)
            return

        @pl.when(at_end)
        def _():
            pl.semaphore_wait(credit.at[1, kind], 2)

        @pl.when(jnp.logical_not(at_end))
        def _():
            pl.semaphore_wait(credit.at[1, kind], 3)

    def chunks_of(kind):
        if kind == 0:
            return [(which,) for which in range(3)]
        if kind == 3:
            return [(pl.ds(piece * 256, 256),) for piece in range(hidden_cols // 256)]
        return [()]

    g_order = [
        (kind, layer, turn_at)
        for layer in reversed(range(LAYERS))
        for kind in (3, 2, 1, 0)
        for turn_at in range(cols_n)
    ]
    added = [0]

    def add_event(kind, layer, turn_at):
        if layer + 1 < LAYERS and turn_at == 0 and kind not in Z_FIRST:
            take_credit_z(kind)
        at = turn_of(turn_at)
        last = turn_at + 1 == cols_n
        if kind in Z_FIRST:
            if last:
                if layer + 1 < LAYERS:
                    take_credit_x(kind)
                for step in range(1, cols_n):
                    g_far(kind, step).wait_recv()
                for piece in chunks_of(kind):
                    ours = (at, 1 - side) + piece
                    total = packs[kind][ours].astype(f32)
                    for step in range(1, cols_n):
                        total = total + got_z[kind][(step - 1, 1 - side) + piece].astype(f32)
                    packs[kind][ours] = total.astype(b16)
                g_x(kind, at).start()
            return
        if last:
            return
        g_x(kind, at).wait_recv()
        passing = turn_at == cols_n - 2
        if passing:
            g_z_came(kind, 3)
        for piece in chunks_of(kind):
            ours = (at, side) + piece
            total = packs[kind][ours].astype(f32) + got_x[kind][(at,) + piece].astype(f32)
            if passing:
                total = total + got_z[kind][(3,) + piece].astype(f32)
            packs[kind][ours] = total.astype(b16)
        g_z(kind, at).start()

    def add_upto(layer_at, index):
        index = (LAYERS - 1 - layer_at) * 4 * cols_n + index
        while added[0] <= min(index, len(g_order) - 1):
            add_event(*g_order[added[0]])
            added[0] += 1

    def lamb_update(weight, first, second, gradient, decay):
        moment_one = BETA_ONE * first + (1.0 - BETA_ONE) * gradient
        moment_two = BETA_TWO * second + (1.0 - BETA_TWO) * gradient * gradient
        return (
            moment_one / CORRECT_ONE / (jnp.sqrt(moment_two / CORRECT_TWO) + ADAM_EPS)
            + decay * weight
        )

    def note_norm(row, values):
        norms[row : row + 1, 0 : values.shape[-1]] += jnp.sum(
            values * values, axis=0, keepdims=True
        )

    def g_end(kind, layer):
        add_upto(layer, (3 - kind) * cols_n + cols_n - 1)
        g_x(kind, place).wait_recv()
        if kind not in Z_FIRST:
            for slot in range(3):
                g_z_came(kind, slot)
        for which in range(3):
            if which or layer + 1 < LAYERS:
                lamb_load(kind, layer, which).wait()
        for piece in chunks_of(kind):
            total = packs[kind][(place, side) + piece].astype(f32)
            if kind in Z_FIRST:
                total = total + got_x[kind][(0,) + piece].astype(f32)
            else:
                total = total + got_x[kind][(place,) + piece].astype(f32)
            if kind in Z_FIRST:
                for step in range(1, cols_n):
                    total = total + got_z[kind][(step - 1, side) + piece].astype(f32)
            else:
                for slot in range(3):
                    total = total + got_z[kind][(slot,) + piece].astype(f32)
            here = piece if piece else (slice(None),)
            weight = held[0][kind][here]
            step_by = lamb_update(
                weight, held[1][kind][here], held[2][kind][here], total, DECAY_RATE
            )
            packs[kind][(place, side) + piece] = total.astype(b16)
            note_norm((layer * 4 + kind) * 2, weight)
            note_norm((layer * 4 + kind) * 2 + 1, step_by)
        fin_copy(kind, layer).start()
        if layer:
            give_credit(kind)
            for which in range(3):
                lamb_load(kind, layer - 1, which).start()

    def fin_copy(kind, layer):
        return pltpu.make_async_copy(
            packs[kind].at[place, side], sums[kind].at[layer], fin_sem.at[kind]
        )

    def g_x_go(kind, layer, turn_at, at):
        if kind in Z_FIRST:
            return
        if layer:
            g_x(kind, at).start()
            return

        @pl.when(turn_at < cols_n - 1)
        def _():
            g_x(kind, at).start()

    def pair_rows(at):
        return pl.ds(mult(at * 2 * cut, 2 * cut), 2 * cut)

    def grad_back(layer):
        if layer + 1 < LAYERS:
            fin_copy(3, layer + 1).wait()
            (take_credit_z if 3 in Z_FIRST else take_credit_x)(3)

        def one(turn_at, carry):
            at = turn_of(turn_at)
            for piece in range(hidden_cols // 512):
                rows = slice(piece * 512, (piece + 1) * 512)
                value = dot_nn(g_turn[layer, rows, :], m_full[:, pair_rows(at)]).astype(b16)
                pk_b[at, 0, rows, :] = value[:, :cut]
                pk_b[at, 1, rows, :] = value[:, cut:]
            g_x_go(3, layer, turn_at, at)
            return carry

        lax.fori_loop(0, cols_n, one, 0)
        if 3 in Z_FIRST:
            for step in range(1, cols_n):
                g_far(3, step).start()

    def grad_in(layer):
        if layer + 1 < LAYERS:
            fin_copy(2, layer + 1).wait()
            (take_credit_z if 2 in Z_FIRST else take_credit_x)(2)

        def one(turn_at, carry):
            at = turn_of(turn_at)
            for piece in range(hidden_cols // 512):
                cols = slice(piece * 512, (piece + 1) * 512)
                value = dot_nn(m_turn[layer, pair_rows(at), :], active[:, cols]).astype(b16)
                pk_i[at, 0, :, cols] = value[:cut]
                pk_i[at, 1, :, cols] = value[cut:]
            g_x_go(2, layer, turn_at, at)
            return carry

        lax.fori_loop(0, cols_n, one, 0)
        if 2 in Z_FIRST:
            for step in range(1, cols_n):
                g_far(2, step).start()

    def grad_out(layer):
        if layer + 1 < LAYERS:
            fin_copy(1, layer + 1).wait()
            (take_credit_z if 1 in Z_FIRST else take_credit_x)(1)

        def one(turn_at, carry):
            at = turn_of(turn_at)
            value = dot_nn(o_turn[layer], h_full[:, pair_rows(at)]).astype(b16)
            pk_o[at, 0] = value[:, :cut]
            pk_o[at, 1] = value[:, cut:]
            g_x_go(1, layer, turn_at, at)
            return carry

        lax.fori_loop(0, cols_n, one, 0)
        if 1 in Z_FIRST:
            for step in range(1, cols_n):
                g_far(1, step).start()

    def grad_qkv(layer):
        if layer + 1 < LAYERS:
            fin_copy(0, layer + 1).wait()
            (take_credit_z if 0 in Z_FIRST else take_credit_x)(0)

        def one(turn_at, carry):
            at = turn_of(turn_at)
            for which in range(3):
                value = dot_nn(h_turn[layer, pair_rows(at), :], d_qkv[which]).astype(b16)
                pk_q[at, 0, which] = value[:cut]
                pk_q[at, 1, which] = value[cut:]
            g_x_go(0, layer, turn_at, at)
            return carry

        lax.fori_loop(0, cols_n, one, 0)
        if 0 in Z_FIRST:
            for step in range(1, cols_n):
                g_far(0, step).start()

    def norm_back(kept, upstream, gain):
        center, rate = norm_parts(kept)
        unit = center * rate
        scaled = upstream * gain
        down = rate * (
            scaled
            - jnp.mean(scaled, axis=-1, keepdims=True)
            - unit * jnp.mean(scaled * unit, axis=-1, keepdims=True)
        )
        return down, unit

    def note(row, values):
        small_acc[row : row + 1, :] += jnp.sum(values, axis=0, keepdims=True)

    norms[...] = jnp.zeros_like(norms)
    for kind in range(ROWS_MAT):
        for which in (1, 2):
            lamb_load(kind, LAYERS - 1, which).start()
    load_c.wait()
    for layer in reversed(range(LAYERS)):
        last = layer + 1 == LAYERS
        base = layer * 8
        for which in range(2):
            at = pl.ds(which * half, half)
            upstream = sum_chip[at, :].astype(f32) if last else grad_hidden[at, :]
            down, unit = norm_back(y_own[layer, at, :], upstream, vec_row(layer, 1))
            m_full[own_rows(which), :] = down.astype(b16)
            gat_start(m_full, which)
            note(base + 1, upstream * unit)
            note(base + 7, upstream)
            note(base + 6, down)
            d_keep[at, :] = down
        marks = BACK_SLOTS[0 if last else 1]
        add_upto(layer, marks[0])
        if not last:
            g_free(3, layer + 1)
            g_end(3, layer + 1)
        gat_end(m_full)
        grad_back(layer)
        add_upto(layer, marks[1])

        def slope_tile(tile, carry):
            at = tile_cols(tile)
            d_active = dot_nt(m_full[...], w_b[layer, at, :])
            d_pre = (d_active * slope[layer, :, at].astype(f32)).astype(b16)
            active[:, at] = d_pre
            small_acc[LAYERS * 8 + layer : LAYERS * 8 + layer + 1, at] = jnp.sum(
                d_pre.astype(f32), axis=0, keepdims=True
            )
            return carry

        lax.fori_loop(0, hidden_cols // TILE, slope_tile, 0)
        sum_start(lambda tile: dot_nt(active[...], w_i[layer, tile_cols(tile), :]))
        add_upto(layer, marks[2])
        if not last:
            g_free(2, layer + 1)
            g_end(2, layer + 1)
        grad_in(layer)
        add_upto(layer, marks[3])
        sum_end()
        if last:
            out_hidden.wait()
        for which in range(2):
            at = pl.ds(which * half, half)
            upstream = sum_rows(which) + d_keep[at, :]
            down, unit = norm_back(x_own[layer, at, :], upstream, vec_row(layer, 0))
            h_full[own_rows(which), :] = down.astype(b16)
            gat_start(h_full, which)
            note(base + 0, upstream * unit)
            note(base + 5, upstream)
            note(base + 4, down)
            d_keep[at, :] = down
        add_upto(layer, marks[4])
        gat_end(h_full)
        if not last:
            g_free(1, layer + 1)
            g_end(1, layer + 1)
        attn[...] = dot_nt(h_full[...], w_o[layer]).astype(b16)
        grad_out(layer)
        if last:
            out_logits.wait()
        add_upto(layer, marks[5])
        attend_back(layer, last, (0,))
        add_upto(layer, marks[6])
        attend_back(layer, last, (1,))
        add_upto(layer, marks[7])
        small_acc[base + 2 : base + 3, own_cols] = jnp.sum(
            d_qkv[0].astype(f32), axis=0, keepdims=True
        )
        small_acc[base + 3 : base + 4, own_cols] = jnp.sum(
            d_qkv[2].astype(f32), axis=0, keepdims=True
        )

        def input_tile(tile):
            rows = tile_cols(tile)
            total = dot_nt(d_qkv[0], w_q[layer, 0, rows, :])
            total = total + dot_nt(d_qkv[1], w_q[layer, 1, rows, :])
            return total + dot_nt(d_qkv[2], w_q[layer, 2, rows, :])

        sum_start(input_tile)
        if not last:
            g_free(0, layer + 1)
            g_end(0, layer + 1)
        grad_qkv(layer)
        if layer == 0:
            for kind in (3, 2, 1, 0):
                if kind not in Z_FIRST:
                    g_x(kind, place).start()
        add_upto(layer, marks[8])
        sum_end()
        for which in range(2):
            at = pl.ds(which * half, half)
            result = sum_rows(which) + d_keep[at, :]
            grad_hidden[at, :] = result

    out_scores = pltpu.make_async_copy(scores, grad_scores, out_sem.at[1])
    out_scores.start()

    small_got[ten] = small_acc[...]

    def small_one(step):
        return rdma(
            small_acc,
            small_got.at[ten],
            sml_s.at[step - 1],
            sml_r.at[step - 1],
            dp,
            lax.rem(ten + step, 4),
        )

    for step in range(1, 4):
        small_one(step).start()
    add_upto(0, BACK_SLOTS[2][0])
    for step in range(1, 4):
        small_one(step).wait_recv()
    mat_rows = LAYERS * 8
    for dev in range(data_parts):
        cols = slice(dev * LANES, (dev + 1) * LANES)
        total = small_got[0, 0:mat_rows, cols]
        for other in range(1, 4):
            total = total + small_got[other, 0:mat_rows, cols]
        small_send[dev, 0:mat_rows, :] = total
        from_cols = pl.ds(mult(((dev % 2) * 4 + ten) * LANES, LANES), LANES)
        small_send[dev, mat_rows : mat_rows + 8, :] = small_got[
            dev // 2, mat_rows : mat_rows + 8, from_cols
        ]

    def small_two(step):
        to = lax.rem(dp + step, data_parts)
        return rdma(
            small_send.at[to],
            small_sum.at[step - 1],
            sml_s.at[2 + step],
            sml_r.at[2 + step],
            to,
            ten,
        )

    def small_go(step, carry):
        small_two(step).start()
        return carry

    lax.fori_loop(1, data_parts, small_go, 0)
    add_upto(0, 4 * cols_n - 1)
    g_end(3, 0)
    g_end(2, 0)
    g_end(1, 0)
    small_out[...] = small_send[dp]

    def small_wait(step, carry):
        small_two(step).wait_recv()
        small_two(step).wait_send()
        small_out[...] += small_sum[step - 1]
        return carry

    lax.fori_loop(1, data_parts, small_wait, 0)
    for step in range(1, 4):
        small_one(step).wait_send()
    g_end(0, 0)

    row_at = lax.broadcasted_iota(jnp.int32, (24, LANES), 0)
    lane_at = lax.broadcasted_iota(jnp.int32, (24, LANES), 1)
    in_share = (row_at >= mat_rows) | (lane_at // (width // data_parts // 4) == ten)
    small_grad = jnp.where(in_share & (row_at < mat_rows + LAYERS), small_out[...], 0.0)
    small_step = lamb_update(small_in[0, 0:24], small_in[1, 0:24], small_in[2, 0:24], small_grad, 0.0)
    norm_send[0:mat_rows, :] = jnp.broadcast_to(
        jnp.sum(norms[...], axis=-1, keepdims=True), (mat_rows, LANES)
    )
    for layer in range(LAYERS):
        for group, rows in enumerate(
            (slice(layer * 8, layer * 8 + 8), slice(mat_rows + layer, mat_rows + layer + 1))
        ):
            for which, values in enumerate((small_in[0, rows], small_step[rows])):
                total = jnp.sum(
                    jnp.sum(values * values, axis=0, keepdims=True), axis=1, keepdims=True
                )
                row = mat_rows + (layer * 2 + group) * 2 + which
                norm_send[row : row + 1, :] = jnp.broadcast_to(total, (1, LANES))

    def norm_one(step):
        return rdma(
            norm_send,
            norm_ten.at[ten],
            ns_sem.at[step - 1],
            nr_sem.at[step - 1],
            dp,
            lax.rem(ten + step, 4),
        )

    def norm_two(step):
        return rdma(
            norm_mid,
            norm_dp.at[dp],
            ns_sem.at[2 + step],
            nr_sem.at[2 + step],
            lax.rem(dp + step, data_parts),
            ten,
        )

    norm_ten[ten] = norm_send[...]
    for step in range(1, 4):
        norm_one(step).start()
    for step in range(1, 4):
        norm_one(step).wait_recv()
    total = norm_ten[0]
    for other in range(1, 4):
        total = total + norm_ten[other]
    norm_mid[...] = total
    norm_dp[dp] = total
    for step in range(1, data_parts):
        norm_two(step).start()
    for kind in range(ROWS_MAT):
        g_free(kind, 0)
        fin_copy(kind, 0).wait()
    out_scores.wait()
    for step in range(1, 4):
        norm_one(step).wait_send()
    for step in range(1, data_parts):
        norm_two(step).wait_recv()
    total = norm_dp[0]
    for other in range(1, data_parts):
        total = total + norm_dp[other]
    norm_out[...] = total
    for step in range(1, data_parts):
        norm_two(step).wait_send()


def fits(parts, head_cols, hidden_cols, heads_here, tokens, width, blocks):
    data_parts, tensor_parts = parts
    return (
        tensor_parts == 4
        and data_parts == 8
        and width // data_parts == LANES
        and head_cols // heads_here == 64
        and head_cols % TILE == 0
        and hidden_cols == data_parts * LANES
        and hidden_cols % 512 == 0
        and blocks == 1
        and tokens % 512 == 0
    )


def shards(*arrays, parts):
    (
        hidden_in,
        logits_in,
        cotangent,
        bucket_ids,
        seq_counts,
        key_mask,
        w_qkv,
        w_out,
        w_in,
        w_back,
        vectors,
        bias_in,
    ) = arrays[:12]
    data_parts = parts[0]
    tokens, width = hidden_in.shape
    head_cols = w_qkv.shape[3]
    hidden_cols = w_in.shape[2]
    heads = logits_in.shape[1]
    if not fits(parts, head_cols, hidden_cols, heads, tokens, width, logits_in.shape[0]):
        return plain_shards(*arrays)
    f32 = jnp.float32
    b16 = jnp.bfloat16
    ten = lax.axis_index("tensor")
    share = tokens // 4
    cut = width // data_parts
    cols_n = data_parts // 2
    owned = vectors.shape[2]
    hbm = pl.BlockSpec(memory_space=pl.ANY)
    vmem = pl.BlockSpec(memory_space=pltpu.VMEM)
    smem = pl.BlockSpec(memory_space=pltpu.SMEM)
    dma = pltpu.SemaphoreType.DMA
    shape = jax.ShapeDtypeStruct
    n = LAYERS
    grad_shapes = (
        (3, cut, head_cols),
        (head_cols, cut),
        (cut, hidden_cols),
        (hidden_cols, cut),
    )
    results = pl.pallas_call(
        functools.partial(step_kernel, data_parts),
        out_shape=(
            shape((share, width), b16),
            shape((heads, tokens, tokens), b16),
            shape((share, width), f32),
            shape((heads, tokens, tokens), b16),
        )
        + tuple(shape((n,) + size, b16) for size in grad_shapes)
        + (shape((24, LANES), f32),) * 2,
        in_specs=[hbm] * 3 + [smem] * 2 + [vmem] * 7 + [hbm] * 12,
        out_specs=(hbm, hbm, vmem, hbm, hbm, hbm, hbm, hbm, vmem, vmem),
        scratch_shapes=[
            pltpu.VMEM((8, tokens), f32),
            pltpu.VMEM((3, 32, LANES), f32),
            pltpu.VMEM((n, 3, width, head_cols), b16),
            pltpu.VMEM((n, head_cols, width), b16),
            pltpu.VMEM((n, width, hidden_cols), b16),
            pltpu.VMEM((n, hidden_cols, width), b16),
            pltpu.VMEM((heads, tokens, tokens), b16),
            pltpu.VMEM((n, heads, tokens, tokens), b16),
            pltpu.VMEM((tokens, width), b16),
            pltpu.VMEM((tokens, width), b16),
            pltpu.VMEM((tokens, hidden_cols), b16),
            pltpu.VMEM((tokens, head_cols), b16),
            pltpu.VMEM((n, width, tokens), b16),
            pltpu.VMEM((n, width, tokens), b16),
            pltpu.VMEM((n, hidden_cols, tokens), b16),
            pltpu.VMEM((n, head_cols, tokens), b16),
            pltpu.VMEM((n, tokens, hidden_cols), b16),
            pltpu.VMEM((n, 3, tokens, head_cols), b16),
            pltpu.VMEM((n, share, width), f32),
            pltpu.VMEM((n, share, width), f32),
            pltpu.VMEM((3, tokens, head_cols), b16),
            pltpu.VMEM((share, width), f32),
            pltpu.VMEM((LANES, tokens), f32),
            pltpu.VMEM((LANES, tokens), f32),
            pltpu.VMEM((tokens, width), b16),
            pltpu.VMEM((2, share, width), b16),
            pltpu.VMEM((share, width), b16),
            pltpu.VMEM((share, width), b16),
            pltpu.VMEM((4, data_parts, 32, LANES), b16),
            pltpu.VMEM((n * 8, width), f32),
            pltpu.VMEM((8, hidden_cols), f32),
            pltpu.VMEM((n * 8 + 8, width), f32),
            pltpu.VMEM((4, n * 8 + 8, width), f32),
            pltpu.VMEM((data_parts, n * 8 + 8, LANES), f32),
            pltpu.VMEM((data_parts - 1, n * 8 + 8, LANES), f32),
        ]
        + [pltpu.VMEM((cols_n, 2) + size, b16) for size in grad_shapes]
        + [
            pltpu.VMEM((1 if kind in Z_FIRST else cols_n,) + size, b16)
            for kind, size in enumerate(grad_shapes)
        ]
        + [
            pltpu.VMEM(((cols_n - 1, 2) if kind in Z_FIRST else (cols_n,)) + size, b16)
            for kind, size in enumerate(grad_shapes)
        ]
        + [pltpu.VMEM(size, f32) for _ in range(3) for size in grad_shapes]
        + [
            pltpu.VMEM((n * 8, width), f32),
            pltpu.VMEM((24, LANES), f32),
            pltpu.VMEM((4, 24, LANES), f32),
            pltpu.VMEM((24, LANES), f32),
            pltpu.VMEM((data_parts, 24, LANES), f32),
        ]
        + [
            dma((2,)),
            dma((n, 4)),
            dma((n, 4, cols_n, 2, 2)),
            dma((n, 4, cols_n, 2)),
            dma((n, 4, cols_n)),
            dma((n, 4, cols_n)),
            dma((width // TILE, 2)),
            dma((width // TILE, 2)),
            dma((width // TILE,)),
            dma((width // TILE,)),
            dma((2, 3)),
            dma((2, 3)),
            dma((data_parts + 2,)),
            dma((data_parts + 2,)),
            dma((data_parts + 2,)),
            dma((data_parts + 2,)),
            dma((4, cols_n)),
            dma((4, cols_n)),
            dma((4, cols_n)),
            dma((4, cols_n)),
            dma((4,)),
            dma((4,)),
            dma((3, 4)),
            dma((data_parts + 2,)),
            dma((data_parts + 2,)),
            pltpu.SemaphoreType.REGULAR((3, 4)),
        ],
        compiler_params=pltpu.CompilerParams(
            collective_id=0, has_side_effects=True, vmem_limit_bytes=63 * 1024 * 1024
        ),
    )(
        hidden_in,
        logits_in,
        cotangent,
        bucket_ids,
        seq_counts,
        key_mask.reshape(1, tokens),
        vectors,
        bias_in,
        arrays[16],
        arrays[17],
        arrays[22],
        arrays[23],
        *arrays[6:10],
        *arrays[12:16],
        *arrays[18:22],
    )
    hidden_out, logits_out, grad_hidden, grad_scores = results[:4]
    small = results[8]
    vec_sum = lax.dynamic_slice_in_dim(small[: LAYERS * 8], ten * owned, owned, 1)
    bin_sum = small[LAYERS * 8 : LAYERS * 9]
    grads_all = tuple(one.astype(f32) for one in results[4:8]) + (vec_sum.reshape(LAYERS, 8, owned), bin_sum)
    masters = arrays[6:12]
    firsts = arrays[12:18]
    seconds = arrays[18:24]
    decays = (DECAY_RATE, DECAY_RATE, DECAY_RATE, DECAY_RATE, 0.0, 0.0)
    moved = []
    for master, gradient, first_prev, second_prev, decay_rate in zip(
        masters, grads_all, firsts, seconds, decays
    ):
        moment_one = BETA_ONE * first_prev + (1.0 - BETA_ONE) * gradient
        moment_two = BETA_TWO * second_prev + (1.0 - BETA_TWO) * gradient * gradient
        update = (
            moment_one / CORRECT_ONE / (jnp.sqrt(moment_two / CORRECT_TWO) + ADAM_EPS)
            + decay_rate * master
        )
        moved.append((moment_one, update))
    norms = jnp.sqrt(results[9][:, 0])
    trust_rows = norms[0::2] / norms[1::2]
    trust_all = jnp.concatenate(
        [trust_rows[: LAYERS * 4].reshape(LAYERS, 4), trust_rows[LAYERS * 4 :].reshape(LAYERS, 2)],
        axis=1,
    ).T
    new_params = tuple(
        (
            master
            - LEARN_RATE
            * trust_all[group_at].reshape((LAYERS,) + (1,) * (master.ndim - 1))
            * moved_one[1]
            for group_at, (master, moved_one) in enumerate(zip(masters, moved))
        )
    )
    return (
        (hidden_out, logits_out[None], grad_hidden, grad_scores[None].astype(f32))
        + grads_all
        + new_params
        + tuple(moved_one[0] for moved_one in moved)
        + (trust_all.T,)
    )


def solution(mesh):
    return jax.shard_map(
        functools.partial(shards, parts=(mesh.shape["dp"], mesh.shape["tensor"])),
        mesh=mesh,
        in_specs=(
            P("dp", None),
            P("dp", "tensor", None, None),
            P(("dp", "tensor"), None),
            P("dp"),
            P("dp"),
            P("dp"),
            P(None, None, "dp", "tensor"),
            P(None, "tensor", "dp"),
            P(None, "dp", "tensor"),
            P(None, "tensor", "dp"),
            P(None, None, ("dp", "tensor")),
            P(None, ("dp", "tensor")),
            P(None, None, "dp", "tensor"),
            P(None, "tensor", "dp"),
            P(None, "dp", "tensor"),
            P(None, "tensor", "dp"),
            P(None, None, ("dp", "tensor")),
            P(None, ("dp", "tensor")),
            P(None, None, "dp", "tensor"),
            P(None, "tensor", "dp"),
            P(None, "dp", "tensor"),
            P(None, "tensor", "dp"),
            P(None, None, ("dp", "tensor")),
            P(None, ("dp", "tensor")),
        ),
        out_specs=(
            P(("dp", "tensor"), None),
            P("dp", "tensor", None, None),
            P(("dp", "tensor"), None),
            P("dp", "tensor", None, None),
            P(None, None, "dp", "tensor"),
            P(None, "tensor", "dp"),
            P(None, "dp", "tensor"),
            P(None, "tensor", "dp"),
            P(None, None, ("dp", "tensor")),
            P(None, ("dp", "tensor")),
            P(None, None, "dp", "tensor"),
            P(None, "tensor", "dp"),
            P(None, "dp", "tensor"),
            P(None, "tensor", "dp"),
            P(None, None, ("dp", "tensor")),
            P(None, ("dp", "tensor")),
            P(None, None, "dp", "tensor"),
            P(None, "tensor", "dp"),
            P(None, "dp", "tensor"),
            P(None, "tensor", "dp"),
            P(None, None, ("dp", "tensor")),
            P(None, ("dp", "tensor")),
            P(),
        ),
        check_vma=False,
    )
```
